128 devices in a mesh: seq: 8 (over z, core), mod: 16 (over y, x).
Axes of the slice: x: 4, y: 4, z: 4, core: 2. Of those that a mesh axis runs over, the one named last changes fastest.
Arguments:
- tokens: bfloat16 [4096, 4096], P('seq', 'mod'), may hold values from -22 to 22
- modality: int32 [4096, 1], P('seq'), may hold values from 0 to 2; in each aligned block of 512 rows (0 to 511, 512 to 1023, ...) at most 256 rows name the same one
- doc_lengths: int32 [4], replicated, may hold values from 1 to 2048, 4096 in all
- w_query: bfloat16 [3, 4096, 4096], P(None, None, 'mod'), may hold values from -0.09375 to 0.09375
- w_key: bfloat16 [3, 4096, 4096], P(None, None, 'mod'), may hold values from -0.109375 to 0.109375
- w_value: bfloat16 [3, 4096, 4096], P(None, None, 'mod'), may hold values from -0.09375 to 0.09375
- d_out: bfloat16 [4096, 4096], P('seq', 'mod'), may hold values from -6 to 6
Outputs:
- attn_out: bfloat16 [4096, 4096], P('seq', 'mod')
- grad_tokens: bfloat16 [4096, 4096], P('seq', 'mod')
- grad_query: float32 [3, 4096, 4096], P(None, 'seq', 'mod')
- grad_key: float32 [3, 4096, 4096], P(None, 'seq', 'mod')
- grad_value: float32 [3, 4096, 4096], P(None, 'seq', 'mod')
The draws below stay inside these ranges and needn't reach their ends.
Inputs may be any that keep to these rules, and one draw needn't show every extreme that they name: In each aligned block of 512 positions (the positions of one device) no modality appears more than 256 times, and in some block one modality appears exactly 256 times. `doc_lengths`: the lengths sum to 4096; the longest document is exactly half of 4096.
All inputs are finite; a program needn't handle non-finite values.
Results may differ from the reference program's by a relative error of at most 0.035.
Values may be sent and summed in bfloat16 or wider, within the bound.
A program may use at most 192 MiB of HBM per device.

```python
import math
import jax
import jax.numpy as jnp
import numpy as np
from jax import lax

D = 4096
HEADS = 32
HEAD_DIM = 128
MODALITIES = 3
DOCS = 4
TOK_DEV = 512
CAP = 256
TOKENS = 4096
N_SEQ = 8


def shared_weight(key):
    weight_shape = (MODALITIES, D, HEADS * HEAD_DIM)
    return jax.random.truncated_normal(key, -6.0, 6.0, weight_shape, jnp.float32) * D ** (-0.5)


def draw_w_query(key, part):
    common_part = shared_weight(key)
    return common_part.astype(jnp.bfloat16)


def draw_w_key(key, part):
    common_part = shared_weight(key)
    key = jax.random.fold_in(key, 2)
    private_part = jax.random.truncated_normal(key, -6.0, 6.0, common_part.shape, jnp.float32) * D ** (-0.5)
    blended = private_part
    return blended.astype(jnp.bfloat16)


def draw_tokens(key, part):
    key = jax.random.fold_in(key, 5)
    key_base = jax.random.fold_in(key, 0)
    blended = jax.random.truncated_normal(key_base, -6.0, 6.0, (TOKENS, D), jnp.float32)
    return blended.astype(jnp.bfloat16)


def levels(own_key, dims, pieces, least, top_value):
    level, own = 1.0, jax.random.fold_in(own_key, 6)
    for position, blocks in pieces:
        draws = jnp.exp(jax.random.uniform(jax.random.fold_in(own, position), (blocks,), jnp.float32, least / len(pieces), top_value / len(pieces)))
        level = level * jnp.repeat(draws, dims[position] // blocks).reshape([-1 if axis == position else 1 for axis in range(len(dims))])
    return level


def length_profile(amount, total, reach, lean):
    portions = [(1 << 20) // math.isqrt(grade ** lean) + 1 for grade in range(2, amount + 1)]
    surplus, counts = total - reach - (amount - 1), [1] * (amount - 1)
    while surplus > 0:
        candidates = [i for i in range(amount - 1) if counts[i] < reach]
        whole, budget = sum([portions[i] for i in candidates]), surplus
        for i in candidates:
            more = min(reach - counts[i], max(1, budget * portions[i] // whole), surplus)
            counts[i] = counts[i] + more
            surplus = surplus - more
    return np.array([reach] + counts)


def uneven(stream_key, count, total, reach, skew):
    if count == 2:
        one = jax.random.randint(stream_key, (), max(1, total - reach), min(reach, total - 1) + 1)
        return jnp.stack([one, total - one])
    tallies = jnp.asarray(length_profile(count, total, reach, skew), jnp.int32)
    couples = (count - 1) // 2
    source_of, taker = tallies[1:1 + 2 * couples:2], tallies[2:2 + 2 * couples:2]
    margin = jnp.minimum(source_of - 1, reach - taker)
    shifted = jax.random.randint(jax.random.fold_in(stream_key, 1), (couples,), 0, 1 << 20) % (margin + 1)
    tallies = tallies.at[1:1 + 2 * couples:2].set(source_of - shifted).at[2:2 + 2 * couples:2].set(taker + shifted)
    return tallies[jax.random.permutation(jax.random.fold_in(stream_key, 2), count)]


def shared_out(key, own, number, rows, count, top, reach, lean):
    sequence = jax.random.permutation(key, count)
    heavy_load, common = portions_of(count, rows * top, reach, lean, True), portions_of(count, rows * top, reach, lean, False)
    places = jnp.arange(count)

    def named(lengths, turn):
        used = int((lengths > 0).sum())
        fixed = max(1, used // 4)
        moved = fixed + (places - fixed + turn * (used - fixed)) % max(1, count - fixed)
        return jnp.zeros((count,), jnp.int32).at[sequence[jnp.where(places < fixed, places, moved)]].set(jnp.asarray(lengths, jnp.int32))

    lengths = jnp.where(number % 4 == 0, named(heavy_load, number // 4), named(common, number - number // 4 - 1))
    mixed = jax.random.permutation(jax.random.fold_in(own, 3), count)
    donor, sink = mixed[0:count // 2 * 2:2], mixed[1:count // 2 * 2:2]
    room = jnp.minimum(lengths[donor] - 1, reach - lengths[sink]) // 2
    room = jnp.where((donor == sequence[0]) | (sink == sequence[0]) | (lengths[sink] == 0), 0, jnp.maximum(room, 0))
    moved = jax.random.randint(jax.random.fold_in(own, 4), (count // 2,), 0, 1 << 20) % (room + 1)
    lengths = lengths.at[donor].add(-moved).at[sink].add(moved)
    items = jnp.searchsorted(jnp.cumsum(lengths), jnp.arange(rows * top), side="right").astype(jnp.int32)
    table = items.reshape(top, rows).T
    table = table[jax.random.permutation(jax.random.fold_in(own, 1), rows)]
    turn = jax.random.randint(jax.random.fold_in(own, 2), (rows, 1), 0, top)
    return jnp.take_along_axis(table, (jnp.arange(top)[None, :] + turn) % top, axis=1)


def portions_of(amount, total, bound, skew, full):
    loads = [(1 << 20) // math.isqrt(standing ** skew) + 1 for standing in range(1, amount + 1)]
    largest = bound if full else min(bound, max(-(-total // amount), total * loads[0] // sum(loads)))
    least = 1 if total - largest >= amount - 1 else 0
    given, rest = [largest] + [least] * (amount - 1), total - largest - least * (amount - 1)
    while rest > 0:
        movable = [i for i in range(1, amount) if given[i] < largest] or [i for i in range(1, amount) if given[i] < bound]
        pool, remaining = sum([loads[i] for i in movable]), rest
        for i in movable:
            more = min(bound - given[i], max(1, remaining * loads[i] // pool), rest)
            given[i] = given[i] + more
            rest = rest - more
    return np.array(given)


def noise(key, extent, scale, limit, pieces=(), kind=jnp.bfloat16):
    array = jax.random.normal(key, extent, jnp.float32) * scale
    if len(pieces) > 0:
        array = levels(key, extent, pieces, -0.22, 0.18) * array
    return jnp.clip(array, min=-limit, max=limit).astype(kind)


def setup_inputs(seed: int = 0) -> dict:
    key_list = jax.random.split(jax.random.key(seed), 8)
    tokens = draw_tokens(jax.random.fold_in(key_list[7], 71), 0)
    modality_keys = jax.random.split(jax.random.fold_in(key_list[1], 1), TOKENS // TOK_DEV)
    modality_turns = jax.random.permutation(jax.random.fold_in(key_list[1], 3), TOKENS // TOK_DEV)
    modality = jax.vmap(lambda own, number: shared_out(jax.random.fold_in(key_list[1], 2), own, number, TOK_DEV, MODALITIES, 1, CAP, 2))(modality_keys, modality_turns).reshape((TOKENS, 1))
    doc_lengths = uneven(key_list[2], DOCS, TOKENS, TOKENS // 2, 2).astype(jnp.int32)
    w_query = draw_w_query(jax.random.fold_in(key_list[7], 71), 0)
    w_key = draw_w_key(jax.random.fold_in(key_list[7], 71), 0)
    w_value = noise(key_list[5], (MODALITIES, D, HEADS * HEAD_DIM), D ** -0.5, 0.09375, ((2, 16),))
    d_out = noise(key_list[6], (TOKENS, HEADS * HEAD_DIM), 1.0, 6.0, ((0, 8), (1, 16)))
    return dict(tokens=tokens, modality=modality, doc_lengths=doc_lengths, w_query=w_query, w_key=w_key, w_value=w_value, d_out=d_out)


def slot_table(kind_ids):
    kind_range = jnp.arange(MODALITIES, dtype=jnp.int32)
    one_hot = (kind_ids[:, None] == kind_range[None, :]).astype(jnp.int32)
    before = jnp.cumsum(one_hot, 0) - one_hot
    rank_ids = lax.optimization_barrier(jnp.sum(before * one_hot, 1))
    slot_ids = kind_ids * CAP + rank_ids
    places = jnp.arange(kind_ids.shape[0], dtype=jnp.int32)
    source_ids = jnp.zeros((MODALITIES * CAP,), jnp.int32).at[slot_ids].set(places)
    filled = jnp.zeros((MODALITIES * CAP,), jnp.int32).at[slot_ids].set(1)
    return (slot_ids, source_ids, filled)

def to_buffer(row_block, source_ids, filled):
    picked = row_block[source_ids] * filled[:, None].astype(row_block.dtype)
    return picked.reshape(MODALITIES, CAP, row_block.shape[1])

def from_buffer(buffer, slot_ids):
    return buffer.reshape(MODALITIES * CAP, buffer.shape[2])[slot_ids]

def by_heads(matrix):
    return matrix.reshape(TOKENS, HEADS, HEAD_DIM).transpose(1, 0, 2)

def from_heads(stacked):
    return stacked.transpose(1, 0, 2).reshape(TOKENS, HEADS * HEAD_DIM)

def block_rounded_sum(left, right):
    left_blocks = left.reshape(N_SEQ, TOK_DEV, left.shape[1]).astype(jnp.float32)
    right_blocks = right.reshape(N_SEQ, TOK_DEV, right.shape[1]).astype(jnp.float32)
    block_parts = jnp.einsum('sqk,sqc->skc', left_blocks, right_blocks)
    rounded = lax.optimization_barrier(block_parts.astype(jnp.bfloat16))
    return lax.optimization_barrier(jnp.sum(rounded.astype(jnp.float32), 0))

def reference(tokens, modality, doc_lengths, w_query, w_key, w_value, d_out):
    kind_ids = modality[:, 0].reshape(N_SEQ, TOK_DEV)
    slot_ids, source_ids, filled = jax.vmap(slot_table)(kind_ids)
    x_buffers = jax.vmap(to_buffer)(tokens.reshape(N_SEQ, TOK_DEV, D), source_ids, filled)
    x_wide = x_buffers.astype(jnp.float32)

    def project(weight):
        projected = jnp.einsum('secd,edh->sech', x_wide, weight.astype(jnp.float32)).astype(jnp.bfloat16)
        return jax.vmap(from_buffer)(projected, slot_ids).reshape(TOKENS, HEADS * HEAD_DIM)
    queries = project(w_query)
    key_rows = project(w_key)
    value_rows = project(w_value)
    positions = jnp.arange(TOKENS, dtype=jnp.int32)
    doc_ends = jnp.cumsum(doc_lengths)
    documents = lax.optimization_barrier(jnp.sum((positions[:, None] >= doc_ends[None, :]).astype(jnp.int32), 1))
    visible = (positions[None, :] <= positions[:, None]) & (documents[None, :] == documents[:, None])
    score_scale = 1.0 / math.sqrt(HEAD_DIM)

    def one_head(packed):
        query_h, key_h, value_h, grad_h = packed
        scores = jnp.dot(query_h, key_h.T, preferred_element_type=jnp.float32) * score_scale
        scores = jnp.where(visible, scores, -jnp.inf)
        row_max = lax.optimization_barrier(jnp.max(scores, 1, keepdims=True))
        weights = jnp.where(visible, jnp.exp(scores - row_max), 0.0)
        totals = lax.optimization_barrier(jnp.sum(weights, 1, keepdims=True))
        attended = (jnp.dot(weights.astype(jnp.bfloat16), value_h, preferred_element_type=jnp.float32) / totals).astype(jnp.bfloat16)
        spread = jnp.dot(grad_h, value_h.T, preferred_element_type=jnp.float32)
        row_dot = lax.optimization_barrier(jnp.sum(grad_h.astype(jnp.float32) * attended.astype(jnp.float32), 1, keepdims=True))
        chances = weights / totals
        dscore = (chances * (spread - row_dot) * score_scale).astype(jnp.bfloat16)
        grad_query_h = jnp.dot(dscore, key_h, preferred_element_type=jnp.float32).astype(jnp.bfloat16)
        grad_key_h = block_rounded_sum(dscore, query_h).astype(jnp.bfloat16)
        grad_value_h = block_rounded_sum(chances.astype(jnp.bfloat16), grad_h).astype(jnp.bfloat16)
        return (attended, grad_query_h, grad_key_h, grad_value_h)
    attended, grad_q, grad_k, grad_v = lax.map(one_head, (by_heads(queries), by_heads(key_rows), by_heads(value_rows), by_heads(d_out)))
    attn_out = from_heads(attended)

    def buffered(act_rows):
        return jax.vmap(to_buffer)(act_rows.reshape(N_SEQ, TOK_DEV, HEADS * HEAD_DIM), source_ids, filled)
    q_buffers = buffered(from_heads(grad_q))
    k_buffers = buffered(from_heads(grad_k))
    v_buffers = buffered(from_heads(grad_v))

    def back_project(act_buffers, weight):
        return jnp.einsum('sech,edh->secd', act_buffers.astype(jnp.float32), weight.astype(jnp.float32))
    back_sum = back_project(q_buffers, w_query) + back_project(k_buffers, w_key) + back_project(v_buffers, w_value)
    grad_tokens = jax.vmap(from_buffer)(back_sum, slot_ids).reshape(TOKENS, D).astype(jnp.bfloat16)

    def weight_grad(act_buffers):

        def add_block(running, block_pair):
            x_block, act_block = block_pair
            block_part = jnp.einsum('ecd,ech->edh', x_block.astype(jnp.float32), act_block.astype(jnp.float32))
            rounded = lax.optimization_barrier(block_part.astype(jnp.bfloat16))
            return (running + rounded.astype(jnp.float32), None)
        start_value = jnp.zeros((MODALITIES, D, HEADS * HEAD_DIM), jnp.float32)
        running, unused = lax.scan(add_block, start_value, (x_buffers, act_buffers))
        return running
    return (attn_out, grad_tokens, weight_grad(q_buffers), weight_grad(k_buffers), weight_grad(v_buffers))
```

```python
import functools
import math

import jax
import jax.numpy as jnp
from jax import lax
from jax.experimental import pallas as pl
from jax.experimental.pallas import tpu as pltpu
from jax.sharding import PartitionSpec as P

HEAD_DIM = 128
WINDOW_PAD = 16
MAX_BACK = 5
VMEM_BYTES = 56 * 1024 * 1024


def dot(left, right, left_dim=1, right_dim=0):
    return lax.dot_general(
        left,
        right,
        (((left_dim,), (right_dim,)), ((), ())),
        preferred_element_type=jnp.float32,
    )


def params():
    return pltpu.CompilerParams(vmem_limit_bytes=VMEM_BYTES)


SMEM = pl.BlockSpec(memory_space=pltpu.SMEM)
WHOLE = pl.BlockSpec(memory_space=pltpu.VMEM)


def window_start(offsets_ref, group, rows, window):
    start = (offsets_ref[group] // WINDOW_PAD) * WINDOW_PAD
    return pl.multiple_of(jnp.minimum(start, rows - window), WINDOW_PAD)


def project_kernel(offsets, x_ref, wq_ref, wk_ref, wv_ref, rank_ref, kind_ref, out_ref, acc):
    groups, window, cols = acc.shape
    rows, depth = x_ref.shape[1:]
    step = pl.program_id(0)
    width = wq_ref.shape[2]

    @pl.when(step == 0)
    def _():
        acc[...] = jnp.zeros_like(acc)

    for group in range(groups):
        start = window_start(offsets, group, rows, window)
        for which, weight in enumerate((wq_ref, wk_ref, wv_ref)):
            part = None
            for piece in range(x_ref.shape[0]):
                picked = x_ref[piece, pl.ds(start, window), :]
                term = dot(picked, weight[group, piece * depth : (piece + 1) * depth])
                part = term if part is None else part + term
            acc[group, :, which * width : (which + 1) * width] += part

    @pl.when(step == pl.num_programs(0) - 1)
    def _():
        total = jnp.zeros((rows, cols), jnp.float32)
        for group in range(groups):
            start = window_start(offsets, group, rows, window)
            place = start + lax.broadcasted_iota(jnp.int32, (rows, window), 1)
            chosen = (rank_ref[...] == place) & (kind_ref[...] == group)
            total += dot(chosen.astype(jnp.bfloat16), acc[group].astype(jnp.bfloat16))
        out_ref[...] = total.astype(out_ref.dtype)


def project(offsets, x, weights, rank, kind):
    blocks, rows, depth = x.shape
    groups, _, width = weights[0].shape
    window = rows // 2 + WINDOW_PAD
    steps = 8
    each = blocks // steps
    weight_spec = pl.BlockSpec((groups, each * depth, width), lambda i: (0, i, 0))
    return pl.pallas_call(
        project_kernel,
        grid=(steps,),
        out_shape=jax.ShapeDtypeStruct((rows, 3 * width), jnp.bfloat16),
        in_specs=[
            SMEM,
            pl.BlockSpec((each, rows, depth), lambda i: (i, 0, 0)),
            weight_spec,
            weight_spec,
            weight_spec,
            WHOLE,
            WHOLE,
        ],
        out_specs=pl.BlockSpec((rows, 3 * width), lambda i: (0, 0)),
        scratch_shapes=[pltpu.VMEM((groups, window, 3 * width), jnp.float32)],
        compiler_params=params(),
    )(offsets, x, *weights, rank, kind)


def attention_kernel(
    bounds, q_ref, kv_ref, do_ref, qdoc_ref, kdoc_ref, out_ref, dq_ref, dkv_ref, scores
):
    rows, width = q_ref.shape
    heads = width // HEAD_DIM
    scale = 1.0 / math.sqrt(HEAD_DIM)
    first, mine = bounds[0], bounds[1]
    dkv_ref[...] = jnp.zeros_like(dkv_ref)
    own = lax.broadcasted_iota(jnp.int32, (rows, 1), 0) + mine * rows
    cols = [slice(h * HEAD_DIM, (h + 1) * HEAD_DIM) for h in range(heads)]
    vcols = [slice(width + h * HEAD_DIM, width + (h + 1) * HEAD_DIM) for h in range(heads)]

    def at(block):
        return pl.ds(pl.multiple_of(block * rows, rows), rows)

    def score_step(block, row_max):
        key_pos = lax.broadcasted_iota(jnp.int32, (1, rows), 1) + block * rows
        visible = (key_pos <= own) & (kdoc_ref[:, at(block)] == qdoc_ref[...])
        new = []
        for h in range(heads):
            part = dot(q_ref[:, cols[h]], kv_ref[block, :, cols[h]], 1, 1) * scale
            part = jnp.where(visible, part, -jnp.inf)
            scores[h, block - first] = part
            new.append(jnp.maximum(row_max[h], jnp.max(part, 1, keepdims=True)))
        return tuple(new)

    start = tuple(jnp.full((rows, 1), -jnp.inf, jnp.float32) for _ in range(heads))
    row_max = lax.fori_loop(first, mine + 1, score_step, start)

    def value_step(block, carry):
        new = []
        for h in range(heads):
            total, summed = carry[h]
            weights = jnp.exp(scores[h, block - first] - row_max[h])
            scores[h, block - first] = weights
            total = total + jnp.sum(weights, 1, keepdims=True)
            summed = summed + dot(weights.astype(jnp.bfloat16), kv_ref[block, :, vcols[h]])
            new.append((total, summed))
        return tuple(new)

    start = tuple(
        (jnp.zeros((rows, 1), jnp.float32), jnp.zeros((rows, HEAD_DIM), jnp.float32))
        for _ in range(heads)
    )
    sums = lax.fori_loop(first, mine + 1, value_step, start)
    inverse, row_dot = [], []
    for h in range(heads):
        total, summed = sums[h]
        attended = (summed / total).astype(jnp.bfloat16)
        out_ref[:, cols[h]] = attended
        inverse.append(1.0 / total)
        row_dot.append(
            jnp.sum(
                do_ref[:, cols[h]].astype(jnp.float32) * attended.astype(jnp.float32),
                1,
                keepdims=True,
            )
        )

    def grad_step(block, carry):
        new = []
        for h in range(heads):
            key_h = kv_ref[block, :, cols[h]]
            spread = dot(do_ref[:, cols[h]], kv_ref[block, :, vcols[h]], 1, 1)
            chances = scores[h, block - first] * inverse[h]
            dscore = (chances * (spread - row_dot[h]) * scale).astype(jnp.bfloat16)
            new.append(carry[h] + dot(dscore, key_h))
            dkv_ref[block, :, cols[h]] = dot(dscore, q_ref[:, cols[h]], 0, 0).astype(jnp.bfloat16)
            dkv_ref[block, :, vcols[h]] = dot(
                chances.astype(jnp.bfloat16), do_ref[:, cols[h]], 0, 0
            ).astype(jnp.bfloat16)
        return tuple(new)

    start = tuple(jnp.zeros((rows, HEAD_DIM), jnp.float32) for _ in range(heads))
    grads = lax.fori_loop(first, mine + 1, grad_step, start)
    for h in range(heads):
        dq_ref[:, cols[h]] = grads[h].astype(jnp.bfloat16)


def attention(bounds, q, kv, do, qdoc, kdoc):
    rows, width = q.shape
    shape = jax.ShapeDtypeStruct((rows, width), jnp.bfloat16)
    return pl.pallas_call(
        attention_kernel,
        out_shape=(shape, shape, jax.ShapeDtypeStruct(kv.shape, jnp.bfloat16)),
        in_specs=[SMEM] + [WHOLE] * 5,
        out_specs=(WHOLE, WHOLE, WHOLE),
        scratch_shapes=[pltpu.VMEM((width // HEAD_DIM, MAX_BACK, rows, rows), jnp.float32)],
        compiler_params=params(),
    )(bounds, q, kv, do, qdoc, kdoc)


def back_kernel(offsets, act_ref, wq_ref, wk_ref, wv_ref, kind_ref, out_ref, acc):
    rows = act_ref.shape[0]
    width = wq_ref.shape[2]
    window = rows // 2 + WINDOW_PAD
    acc[...] = jnp.zeros_like(acc)
    for group in range(wq_ref.shape[0]):
        start = window_start(offsets, group, rows, window)
        at = pl.ds(start, window)
        mine = kind_ref[at, :] == group
        part = None
        for which, weight in enumerate((wq_ref, wk_ref, wv_ref)):
            act = act_ref[at, which * width : (which + 1) * width]
            act = jnp.where(mine, act, jnp.zeros_like(act))
            term = dot(act, weight[group], 1, 1)
            part = term if part is None else part + term
        acc[at, :] += part
    depth = out_ref.shape[2]
    for piece in range(out_ref.shape[0]):
        out_ref[piece] = acc[:, piece * depth : (piece + 1) * depth].astype(out_ref.dtype)


def back_project(offsets, act, weights, sorted_kind):
    rows = act.shape[0]
    groups, depth, width = weights[0].shape
    steps = 8
    chunk = depth // steps
    weight_spec = pl.BlockSpec((groups, chunk, width), lambda i: (0, i, 0))
    return pl.pallas_call(
        back_kernel,
        grid=(steps,),
        out_shape=jax.ShapeDtypeStruct((SIDE * SIDE, rows, width), jnp.bfloat16),
        in_specs=[SMEM, WHOLE, weight_spec, weight_spec, weight_spec, WHOLE],
        out_specs=pl.BlockSpec((chunk // width, rows, width), lambda i: (i, 0, 0)),
        scratch_shapes=[pltpu.VMEM((rows, chunk), jnp.float32)],
        compiler_params=params(),
    )(offsets, act, *weights, sorted_kind)


def weight_kernel(offsets, x_ref, act_ref, gq_ref, gk_ref, gv_ref):
    step = pl.program_id(0)
    pieces, _, wide, depth, cols = x_ref.shape
    rows = pieces * depth
    groups, _, width = gq_ref.shape
    grads = (gq_ref, gk_ref, gv_ref)

    @pl.when(step == 0)
    def _():
        for grad in grads:
            grad[...] = jnp.zeros_like(grad)

    block, half = step // 2, step % 2
    base = half * rows
    for group in range(groups):
        low = offsets[block, group] - base
        high = offsets[block, group + 1] - base

        @pl.when((high > 0) & (low < rows) & (high > low))
        def _():
            row = lax.broadcasted_iota(jnp.int32, (rows, 1), 0)
            mine = (row >= low) & (row < high)
            for which, grad in enumerate(grads):
                act = act_ref[0, :, which * width : (which + 1) * width]
                act = jnp.where(mine, act, jnp.zeros_like(act))
                for part in range(wide):
                    x = x_ref[:, 0, part].reshape(rows, cols)
                    grad[group, part * cols : (part + 1) * cols] += dot(x, act, 0, 0)


def weight_grads(offsets, x, act, groups):
    pieces, count, wide, depth, cols = x.shape
    chunk = pieces * depth // 2
    width = act.shape[2] // 3
    out = jax.ShapeDtypeStruct((groups, wide * cols, width), jnp.float32)
    out_spec = pl.BlockSpec((groups, wide * cols, width), lambda i: (0, 0, 0))
    return pl.pallas_call(
        weight_kernel,
        grid=(2 * count,),
        out_shape=(out, out, out),
        in_specs=[
            SMEM,
            pl.BlockSpec(
                (pieces // 2, 1, wide, depth, cols), lambda i: (i % 2, i // 2, 0, 0, 0)
            ),
            pl.BlockSpec((1, chunk, 3 * width), lambda i: (i // 2, i % 2, 0)),
        ],
        out_specs=(out_spec, out_spec, out_spec),
        compiler_params=params(),
    )(offsets, x, act)


SIDE = 4
OFFSETS = (2, -1, 1, 0)
ANY = pl.BlockSpec(memory_space=pl.ANY)


def enter(devices):
    barrier = pltpu.get_barrier_semaphore()
    for device in devices:
        pl.semaphore_signal(
            barrier, inc=1, device_id=device, device_id_type=pl.DeviceIdType.MESH
        )
    pl.semaphore_wait(barrier, len(devices))


class Copies:
    def __init__(self, send_sem, recv_sem):
        self.send_sem, self.recv_sem = send_sem, recv_sem
        self.names = {}
        self.started = []

    def make(self, name, src, dst, device):
        number = self.names.setdefault(name, len(self.names))
        return pltpu.make_async_remote_copy(
            src_ref=src,
            dst_ref=dst,
            send_sem=self.send_sem.at[number],
            recv_sem=self.recv_sem.at[number],
            device_id=device,
            device_id_type=pl.DeviceIdType.MESH,
        )

    def send(self, name, src, dst, device):
        copy = self.make(name, src, dst, device)
        copy.start()
        self.started.append(copy)

    def receive(self, name, dst, device):
        self.make(name, dst, dst, device).wait_recv()

    def finish(self):
        for copy in self.started:
            copy.wait_send()


def plane_device(dx, dy):
    rank = lax.axis_index("mod")
    x, y = lax.rem(rank, SIDE), rank // SIDE
    return lax.rem(y + dy + SIDE, SIDE) * SIDE + lax.rem(x + dx + SIDE, SIDE)


def line_device(dz, other=False):
    rank = lax.axis_index("seq")
    z, core = rank // 2, lax.rem(rank, 2)
    return lax.rem(z + dz + SIDE, SIDE) * 2 + (1 - core if other else core)


def plane_neighbours():
    return [{"mod": plane_device(*step)} for step in ((1, 0), (-1, 0), (0, 1), (0, -1))]


def line_neighbours():
    return [{"seq": line_device(1)}, {"seq": line_device(-1)}, {"seq": line_device(0, True)}]


def plane_gather(copies, src, out):
    half = src.shape[0] // 2

    def part(turn, which):
        if which is None:
            return pl.ds(turn * half, half)
        return pl.ds(turn * half + which * (half // 2), half // 2)

    def device(turn, da, db):
        return plane_device(da, db) if turn == 0 else plane_device(db, da)

    def region(turn, da, db, which):
        return out.at[device(turn, da, db), part(turn, which)]

    def target(turn, axis, way):
        return {"mod": device(turn, way, 0) if axis == "a" else device(turn, 0, way)}

    def send(turn, axis, way, kind, offset):
        which = None if kind == "full" else (0 if way > 0 else 1)
        own = kind == "full" and offset == 0
        da = (0 if kind == "full" else -way) if axis == "a" else offset
        db = 0 if axis == "a" or kind == "full" else -way
        there = region(turn, da, db, which)
        here = src.at[part(turn, which)] if own else there
        copies.send(("pg", turn, axis, way, kind, offset), here, there, target(turn, axis, way))

    def receive(turn, axis, way, kind, offset):
        which = None if kind == "full" else (0 if way > 0 else 1)
        far = -way if kind == "full" else 2
        da, db = (far, 0) if axis == "a" else (offset, far)
        copies.receive(
            ("pg", turn, axis, way, kind, offset),
            region(turn, da, db, which),
            target(turn, axis, way),
        )

    ways, turns = (1, -1), (0, 1)

    def stage_0():
        for turn in turns:
            for way in ways:
                send(turn, "a", way, "full", 0)
        for turn in turns:
            for way in ways:
                send(turn, "b", way, "full", 0)

    def stage_1():
        for way in ways:
            for turn in turns:
                receive(turn, "a", way, "full", 0)
                send(turn, "a", way, "half", 0)
                for second in ways:
                    send(turn, "b", second, "full", -way)

    def stage_2():
        for turn in turns:
            for way in ways:
                receive(turn, "a", way, "half", 0)
            for second in ways:
                send(turn, "b", second, "full", 2)

    def forward(offset):
        def stage():
            for turn in turns:
                for way in ways:
                    receive(turn, "b", way, "full", offset)
                    send(turn, "b", way, "half", offset)

        return stage

    def last():
        for offset in (0, -1, 1, 2):
            for turn in turns:
                for way in ways:
                    receive(turn, "b", way, "half", offset)

    return [stage_0, stage_1, forward(0), stage_2, forward(-1), forward(1), forward(2), last]


def line_gather(copies, src, out):
    half = src.shape[0] // 2

    def region(dz, other, which):
        rows = pl.ds(0, 2 * half) if which is None else pl.ds(which * half, half)
        return out.at[line_device(dz, other), rows]

    def along(way):
        return {"seq": line_device(way)}

    sibling = {"seq": line_device(0, True)}

    def pass_on(dz):
        copies.send(("sib", dz), region(dz, False, None), region(dz, False, None), sibling)

    def stage_0():
        for way in (1, -1):
            copies.send(("z", way, "full"), src, region(0, False, None), along(way))
        copies.send(("sib", 0), src, region(0, False, None), sibling)

    def stage_1():
        for way in (1, -1):
            which = 0 if way > 0 else 1
            copies.receive(("z", way, "full"), region(-way, False, None), along(way))
            there = region(-way, False, which)
            copies.send(("z", way, "half"), there, there, along(way))
        for way in (1, -1):
            pass_on(-way)

    def stage_2():
        for way in (1, -1):
            which = 0 if way > 0 else 1
            copies.receive(("z", way, "half"), region(2, False, which), along(way))
        pass_on(2)

    def last():
        for dz in (0, -1, 1, 2):
            copies.receive(("sib", dz), region(dz, True, None), sibling)

    return [stage_0, stage_1, stage_2, last]


def add(*terms):
    total = terms[0].astype(jnp.float32)
    for term in terms[1:]:
        total = total + term.astype(jnp.float32)
    return total.astype(jnp.bfloat16)


class RingSum:
    def __init__(self, copies, name, source, device, halves, fulls, sums):
        self.copies, self.name, self.source, self.device = copies, name, source, device
        self.halves, self.fulls, self.sums = halves, fulls, sums
        self.half = halves.shape[1]

    def rows(self, which):
        return pl.ds(which * self.half, self.half)

    def send(self, kind, way, src, dst):
        self.copies.send((self.name, kind, way), src, dst, self.device(way))

    def receive(self, kind, way, dst):
        self.copies.receive((self.name, kind, way), dst, self.device(way))

    def far(self):
        for number, way in enumerate((1, -1)):
            self.send("half", way, self.source(2).at[self.rows(number)], self.halves.at[number])

    def early(self, way):
        number = 0 if way > 0 else 1
        there = self.fulls.at[number, self.rows(1 - number)]
        self.send("early", way, self.source(way).at[self.rows(1 - number)], there)

    def late(self):
        for number, way in enumerate((1, -1)):
            self.receive("half", way, self.halves.at[number])
            term = self.source(way)[self.rows(number)]
            self.sums[number] = add(term, self.halves[number])
            self.send("late", way, self.sums.at[number], self.fulls.at[number, self.rows(number)])

    def result(self):
        for number, way in enumerate((1, -1)):
            self.receive("early", way, self.fulls.at[number, self.rows(1 - number)])
            self.receive("late", way, self.fulls.at[number, self.rows(number)])
        return add(self.source(0)[...], self.fulls[0], self.fulls[1])


def in_turn(*groups):
    for place in range(max(len(group) for group in groups)):
        for group in groups:
            if place < len(group):
                group[place]()


def token_gather_kernel(src, out, send_sem, recv_sem, own_sem):
    copies = Copies(send_sem, recv_sem)
    own = pltpu.make_async_copy(src, out.at[plane_device(0, 0)], own_sem)
    own.start()
    enter(plane_neighbours())
    in_turn(plane_gather(copies, src, out))
    copies.finish()
    own.wait()


def remote_params(number):
    return pltpu.CompilerParams(
        collective_id=number, has_side_effects=True, vmem_limit_bytes=VMEM_BYTES
    )


def semaphores(count):
    return [pltpu.SemaphoreType.DMA((count,)), pltpu.SemaphoreType.DMA((count,))]


def token_gather(block):
    return pl.pallas_call(
        token_gather_kernel,
        out_shape=jax.ShapeDtypeStruct((SIDE * SIDE, *block.shape), block.dtype),
        in_specs=[ANY],
        out_specs=ANY,
        scratch_shapes=[*semaphores(40), pltpu.SemaphoreType.DMA],
        compiler_params=remote_params(0),
    )(block)


def key_gather_kernel(kv, rows, kv_all, pieces, columns, send_sem, recv_sem, own_sem):
    copies = Copies(send_sem, recv_sem)
    count = pieces.shape[0]
    me, place = lax.axis_index("seq"), lax.axis_index("mod")
    depth = pieces.shape[2]

    def piece(rank):
        return rows.at[pl.ds(2 * rank, 2), pl.ds(pl.multiple_of(place * depth, depth), depth)]

    own_kv = pltpu.make_async_copy(kv, kv_all.at[me], own_sem.at[0])
    own_kv.start()
    own_piece = pltpu.make_async_copy(piece(me), pieces.at[me], own_sem.at[1])
    own_piece.start()
    others = [lax.rem(me + step, count) for step in range(1, count)]
    enter([{"seq": other} for other in others] + plane_neighbours())
    for step, other in enumerate(others):
        copies.send(("piece", step), piece(other), pieces.at[me], {"seq": other})
    line = line_gather(copies, kv, kv_all)
    line[0]()
    for step in range(count - 1):
        sender = lax.rem(me + count - 1 - step, count)
        copies.receive(("piece", step), pieces.at[sender], {"seq": others[step]})
    own_piece.wait()
    own_columns = pltpu.make_async_copy(pieces, columns.at[place], own_sem.at[2])
    own_columns.start()
    plane = plane_gather(copies, pieces, columns)
    in_turn(plane, line[1:])
    copies.finish()
    own_kv.wait()
    own_columns.wait()


def key_gather(kv, rows, count):
    blocks, tall, width = rows.shape
    depth = tall // blocks
    pieces = jax.ShapeDtypeStruct((count, 2, depth, width), rows.dtype)
    return pl.pallas_call(
        key_gather_kernel,
        out_shape=(
            jax.ShapeDtypeStruct((count, *kv.shape), kv.dtype),
            pieces,
            jax.ShapeDtypeStruct((blocks, *pieces.shape), rows.dtype),
        ),
        in_specs=[ANY, ANY],
        out_specs=(ANY, ANY, ANY),
        scratch_shapes=[*semaphores(56), pltpu.SemaphoreType.DMA((3,))],
        compiler_params=remote_params(1),
    )(kv, rows)


def key_sum_kernel(
    partial, out, theirs, ours, halves, fulls, sums, send_sem, recv_sem
):
    copies = Copies(send_sem, recv_sem)
    enter(line_neighbours())
    sibling = {"seq": line_device(0, True)}
    places = {offset: number for number, offset in enumerate(OFFSETS)}
    for offset in OFFSETS:
        copies.send(
            ("pair", offset),
            partial.at[line_device(offset, True)],
            theirs.at[places[offset]],
            sibling,
        )
    ring = RingSum(
        copies,
        "ring",
        lambda offset: ours.at[places[offset]],
        lambda way: {"seq": line_device(way)},
        halves,
        fulls,
        sums,
    )
    for offset in OFFSETS:
        copies.receive(("pair", offset), theirs.at[places[offset]], sibling)
        ours[places[offset]] = add(partial[line_device(offset)], theirs[places[offset]])
        if offset == 2:
            ring.far()
        elif offset != 0:
            ring.early(offset)
    ring.late()
    out[...] = ring.result()
    copies.finish()


def key_sum(partial):
    _, tall, width = partial.shape

    def buffer(count, rows):
        return pltpu.VMEM((count, rows, width), partial.dtype)

    return pl.pallas_call(
        key_sum_kernel,
        out_shape=jax.ShapeDtypeStruct((tall, width), partial.dtype),
        in_specs=[WHOLE],
        out_specs=WHOLE,
        scratch_shapes=[
            buffer(SIDE, tall),
            buffer(SIDE, tall),
            buffer(2, tall // 2),
            buffer(2, tall),
            buffer(2, tall // 2),
            *semaphores(16),
        ],
        compiler_params=remote_params(2),
    )(partial)


def act_gather_kernel(
    act, partial, act_all, out, halves, fulls, sums, results, send_sem, recv_sem, own_sem
):
    copies = Copies(send_sem, recv_sem)
    own = pltpu.make_async_copy(act, act_all.at[lax.axis_index("seq")], own_sem)
    own.start()
    enter(plane_neighbours() + line_neighbours())
    line = line_gather(copies, act, act_all)
    half = out.shape[0] // 2

    def device(turn, da, db):
        return plane_device(da, db) if turn == 0 else plane_device(db, da)

    def second(turn, place):
        offset, number = OFFSETS[place], turn * len(OFFSETS) + place
        return RingSum(
            copies,
            ("b", number),
            lambda db: partial.at[device(turn, offset, db), pl.ds(turn * half, half)],
            lambda way: {"mod": device(turn, 0, way)},
            halves.at[number],
            fulls.at[number],
            sums.at[number],
        )

    def first(turn):
        number = 2 * len(OFFSETS) + turn
        return RingSum(
            copies,
            ("a", turn),
            lambda da: results.at[turn, OFFSETS.index(da)],
            lambda way: {"mod": device(turn, way, 0)},
            halves.at[number],
            fulls.at[number],
            sums.at[number],
        )

    rings = {(turn, place): second(turn, place) for place in range(4) for turn in range(2)}
    tops = [first(turn) for turn in range(2)]
    line[0]()
    for ring in rings.values():
        ring.far()
    for ring in rings.values():
        ring.early(1)
        ring.early(-1)
    for ring in rings.values():
        ring.late()
    line[1]()
    for (turn, place), ring in rings.items():
        results[turn, place] = ring.result()
        offset = OFFSETS[place]
        if offset == 2:
            tops[turn].far()
        elif offset != 0:
            tops[turn].early(offset)
        if (turn, place) == (1, 1):
            line[2]()
    for top in tops:
        top.late()
    for turn, top in enumerate(tops):
        out[turn * half : (turn + 1) * half] = top.result()
    line[3]()
    copies.finish()
    own.wait()


def act_gather(act, partial, count):
    _, tall, width = partial.shape
    half = tall // 2

    def buffer(*shape):
        return pltpu.VMEM((*shape, width), partial.dtype)

    return pl.pallas_call(
        act_gather_kernel,
        out_shape=(
            jax.ShapeDtypeStruct((count, *act.shape), act.dtype),
            jax.ShapeDtypeStruct((tall, width), partial.dtype),
        ),
        in_specs=[ANY, WHOLE],
        out_specs=(ANY, WHOLE),
        scratch_shapes=[
            buffer(10, 2, half // 2),
            buffer(10, 2, half),
            buffer(10, 2, half // 2),
            buffer(2, 4, half),
            *semaphores(72),
            pltpu.SemaphoreType.DMA,
        ],
        compiler_params=remote_params(3),
    )(act, partial)


def per_device(tokens, modality, doc_lengths, w_query, w_key, w_value, d_out):
    groups = w_query.shape[0]
    tok_rows = tokens.shape[0]
    col_count = w_query.shape[2]
    seq_count = lax.axis_size("seq")
    seq_rank = lax.axis_index("seq")
    weights = (w_query, w_key, w_value)

    kind = modality[:, 0]
    one_hot = (kind[:, None] == jnp.arange(groups, dtype=jnp.int32)[None, :]).astype(jnp.int32)
    counts = jnp.sum(one_hot, 0)
    ends = jnp.cumsum(counts)
    offsets = jnp.concatenate([jnp.zeros((1,), jnp.int32), ends])
    before = jnp.cumsum(one_hot, 0) - one_hot
    rank = jnp.sum((before + offsets[None, :groups]) * one_hot, 1)
    places = jnp.arange(tok_rows, dtype=jnp.int32)
    sort_matrix = (rank[None, :] == places[:, None]).astype(jnp.bfloat16)
    sorted_kind = jnp.sum((places[:, None] >= ends[None, :]).astype(jnp.int32), 1)[:, None]
    all_offsets = lax.all_gather(offsets, "seq", axis=0)

    sorted_tokens = dot(sort_matrix, tokens).astype(jnp.bfloat16)
    whole_rows = token_gather(sorted_tokens)
    projected = project(offsets, whole_rows, weights, rank[:, None], modality)
    queries = projected[:, :col_count]
    gathered, _, token_columns = key_gather(projected[:, col_count:], whole_rows, seq_count)

    key_pos = jnp.arange(tok_rows * seq_count, dtype=jnp.int32)
    doc_ends = jnp.cumsum(doc_lengths)
    document = jnp.sum((key_pos[:, None] >= doc_ends[None, :]).astype(jnp.int32), 1)
    own_document = lax.dynamic_slice(document, (seq_rank * tok_rows,), (tok_rows,))
    first_key = jnp.sum((document < own_document[0]).astype(jnp.int32))
    bounds = jnp.stack([first_key // tok_rows, seq_rank]).astype(jnp.int32)
    attn_out, act_query, partial = attention(
        bounds, queries, gathered, d_out, own_document[:, None], document[None, :]
    )
    act_key_value = key_sum(partial)
    act = jnp.concatenate([act_query, act_key_value], 1)
    act = dot(sort_matrix, act).astype(jnp.bfloat16)
    token_part = back_project(offsets, act, weights, sorted_kind)
    act_all, grad_sorted = act_gather(act, token_part, seq_count)
    grad_tokens = dot(sort_matrix, grad_sorted, 0, 0).astype(jnp.bfloat16)
    grads = weight_grads(all_offsets, token_columns, act_all, groups)
    return (attn_out, grad_tokens, *grads)


def solution(mesh):
    placed = (
        P("seq", "mod"),
        P("seq", None),
        P(),
        P(None, None, "mod"),
        P(None, None, "mod"),
        P(None, None, "mod"),
        P("seq", "mod"),
    )
    return jax.shard_map(
        per_device,
        mesh=mesh,
        in_specs=placed,
        out_specs=(
            P("seq", "mod"),
            P("seq", "mod"),
            P(None, "seq", "mod"),
            P(None, "seq", "mod"),
            P(None, "seq", "mod"),
        ),
        check_vma=False,
    )
```

```python
import functools
import math

import jax
import jax.numpy as jnp
from jax import lax
from jax.experimental import pallas as pl
from jax.experimental.pallas import tpu as pltpu
from jax.sharding import PartitionSpec as P

HEAD_DIM = 128
WINDOW_PAD = 16
MAX_BACK = 5
VMEM_BYTES = 56 * 1024 * 1024


def dot(left, right, left_dim=1, right_dim=0):
    return lax.dot_general(
        left,
        right,
        (((left_dim,), (right_dim,)), ((), ())),
        preferred_element_type=jnp.float32,
    )


def params():
    return pltpu.CompilerParams(vmem_limit_bytes=VMEM_BYTES)


ANY = pl.BlockSpec(memory_space=pl.ANY)
SMEM = pl.BlockSpec(memory_space=pltpu.SMEM)
WHOLE = pl.BlockSpec(memory_space=pltpu.VMEM)


def attention_kernel(
    lengths, q_ref, k_ref, v_ref, do_ref, out_ref, dq_ref, dk_ref, dv_ref, scores
):
    rows, width = q_ref.shape
    heads = width // HEAD_DIM
    scale = 1.0 / math.sqrt(HEAD_DIM)
    mine = lax.axis_index("seq")
    ends = [lengths[0]]
    for number in range(1, lengths.shape[0]):
        ends.append(ends[-1] + lengths[number])
    first = jnp.int32(0)
    for end in ends:
        first = jnp.where(end <= mine * rows, end, first)
    first = first // rows

    def document(positions):
        return sum((positions >= end).astype(jnp.int32) for end in ends)

    def clear(block, _):
        dk_ref[block] = jnp.zeros_like(dk_ref[block])
        dv_ref[block] = jnp.zeros_like(dv_ref[block])
        return 0

    lax.fori_loop(0, first, clear, 0)
    lax.fori_loop(mine + 1, k_ref.shape[0], clear, 0)
    own = lax.broadcasted_iota(jnp.int32, (rows, 1), 0) + mine * rows
    own_document = document(own)
    cols = [slice(h * HEAD_DIM, (h + 1) * HEAD_DIM) for h in range(heads)]

    def score_step(block, row_max):
        key_pos = lax.broadcasted_iota(jnp.int32, (1, rows), 1) + block * rows
        visible = (key_pos <= own) & (document(key_pos) == own_document)
        new = []
        for h in range(heads):
            part = dot(q_ref[:, cols[h]], k_ref[block, :, cols[h]], 1, 1) * scale
            part = jnp.where(visible, part, -jnp.inf)
            scores[h, block - first] = part
            new.append(jnp.maximum(row_max[h], jnp.max(part, 1, keepdims=True)))
        return tuple(new)

    start = tuple(jnp.full((rows, 1), -jnp.inf, jnp.float32) for _ in range(heads))
    row_max = lax.fori_loop(first, mine + 1, score_step, start)

    def value_step(block, carry):
        new = []
        for h in range(heads):
            total, summed = carry[h]
            weights = jnp.exp(scores[h, block - first] - row_max[h])
            scores[h, block - first] = weights
            total = total + jnp.sum(weights, 1, keepdims=True)
            summed = summed + dot(weights.astype(jnp.bfloat16), v_ref[block, :, cols[h]])
            new.append((total, summed))
        return tuple(new)

    start = tuple(
        (jnp.zeros((rows, 1), jnp.float32), jnp.zeros((rows, HEAD_DIM), jnp.float32))
        for _ in range(heads)
    )
    sums = lax.fori_loop(first, mine + 1, value_step, start)
    inverse, row_dot = [], []
    for h in range(heads):
        total, summed = sums[h]
        attended = (summed / total).astype(jnp.bfloat16)
        out_ref[:, cols[h]] = attended
        inverse.append(1.0 / total)
        row_dot.append(
            jnp.sum(
                do_ref[:, cols[h]].astype(jnp.float32) * attended.astype(jnp.float32),
                1,
                keepdims=True,
            )
        )

    def grad_step(block, carry):
        new = []
        for h in range(heads):
            key_h = k_ref[block, :, cols[h]]
            spread = dot(do_ref[:, cols[h]], v_ref[block, :, cols[h]], 1, 1)
            chances = scores[h, block - first] * inverse[h]
            dscore = (chances * (spread - row_dot[h]) * scale).astype(jnp.bfloat16)
            new.append(carry[h] + dot(dscore, key_h))
            dk_ref[block, :, cols[h]] = dot(dscore, q_ref[:, cols[h]], 0, 0).astype(jnp.bfloat16)
            dv_ref[block, :, cols[h]] = dot(
                chances.astype(jnp.bfloat16), do_ref[:, cols[h]], 0, 0
            ).astype(jnp.bfloat16)
        return tuple(new)

    start = tuple(jnp.zeros((rows, HEAD_DIM), jnp.float32) for _ in range(heads))
    grads = lax.fori_loop(first, mine + 1, grad_step, start)
    for h in range(heads):
        dq_ref[:, cols[h]] = grads[h].astype(jnp.bfloat16)


def attention(lengths, q, k, v, do):
    rows, width = q.shape
    shape = jax.ShapeDtypeStruct((rows, width), jnp.bfloat16)
    wide = jax.ShapeDtypeStruct(k.shape, jnp.bfloat16)
    return pl.pallas_call(
        attention_kernel,
        out_shape=(shape, shape, wide, wide),
        in_specs=[SMEM] + [WHOLE] * 4,
        out_specs=(WHOLE,) * 4,
        scratch_shapes=[pltpu.VMEM((width // HEAD_DIM, MAX_BACK, rows, rows), jnp.float32)],
        compiler_params=params(),
    )(lengths, q, k, v, do)


def weight_kernel(
    table, x_ref, act_ref, gq_ref, gk_ref, gv_ref, x_in, act_in, x_rows, x_turned, grads, sem
):
    count, rows, wide = x_rows.shape
    groups, _, depth = x_turned.shape
    window = depth // count
    loads = [pltpu.make_async_copy(x_ref, x_in, sem.at[0])]
    for which in range(3):
        loads.append(
            pltpu.make_async_copy(act_ref.at[which], act_in.at[which], sem.at[1 + which])
        )
    for load in loads:
        load.start()

    def bounds(block, group):
        low, high = table[block, 0, group], table[block, 0, group + 1]
        start = jnp.minimum((low // WINDOW_PAD) * WINDOW_PAD, rows - window)
        return low, high, pl.multiple_of(start, WINDOW_PAD)

    def chosen(block, group, start, size):
        low, high, _ = bounds(block, group)
        at = pl.ds(start, size)
        place = lax.broadcasted_iota(jnp.int32, (size, 1), 0) + start
        picked = x_rows[block, at, :]
        return jnp.where((place >= low) & (place < high), picked, jnp.zeros_like(picked))

    loads[0].wait()
    for block in range(count):
        for part in range(x_in.shape[2]):
            cols = x_in.shape[4]
            x_rows[block, :, part * cols : (part + 1) * cols] = x_in[:, block, part].reshape(
                rows, cols
            )
        for group in range(groups):
            picked = chosen(block, group, bounds(block, group)[2], window)
            x_turned[group, :, block * window : (block + 1) * window] = picked.T
    stores = []
    for which, out in enumerate((gq_ref, gk_ref, gv_ref)):
        loads[1 + which].wait()
        for group in range(groups):
            total = None
            for block in range(count):
                at = pl.ds(bounds(block, group)[2], window)
                term = dot(
                    x_turned[group, :, block * window : (block + 1) * window],
                    act_in[which, block, at, :],
                )
                total = term if total is None else total + term
            grads[which, group] = total

            def rest(block, _):
                low, high, start = bounds(block, group)

                @pl.when(high > start + window)
                def _():
                    at = pl.multiple_of(start + window, WINDOW_PAD)
                    picked = chosen(block, group, at, WINDOW_PAD)
                    act = act_in[which, block, pl.ds(at, WINDOW_PAD), :]
                    grads[which, group] += dot(picked, act, 0, 0)

                return 0

            lax.fori_loop(0, count, rest, 0)
        stores.append(pltpu.make_async_copy(grads.at[which], out, sem.at[4 + which]))
        stores[-1].start()
    for store in stores:
        store.wait()


def weight_grads(table, x, act, groups):
    pieces, count, parts, deep, cols = x.shape
    rows, wide = pieces * deep, parts * cols
    width = act.shape[3]
    out = jax.ShapeDtypeStruct((groups, wide, width), jnp.float32)
    return pl.pallas_call(
        weight_kernel,
        out_shape=(out, out, out),
        in_specs=[SMEM, ANY, ANY],
        out_specs=(ANY, ANY, ANY),
        scratch_shapes=[
            pltpu.VMEM(x.shape, x.dtype),
            pltpu.VMEM(act.shape, act.dtype),
            pltpu.VMEM((count, rows, wide), x.dtype),
            pltpu.VMEM((groups, wide, count * (rows // 2)), x.dtype),
            pltpu.VMEM((3, groups, wide, width), jnp.float32),
            pltpu.SemaphoreType.DMA((7,)),
        ],
        compiler_params=params(),
    )(table, x, act)


SIDE = 4
OFFSETS = (2, -1, 1, 0)


def greet(devices):
    barrier = pltpu.get_barrier_semaphore()
    for device in devices:
        pl.semaphore_signal(
            barrier, inc=1, device_id=device, device_id_type=pl.DeviceIdType.MESH
        )


def enter(devices):
    greet(devices)
    pl.semaphore_wait(pltpu.get_barrier_semaphore(), len(devices))


class Copies:
    def __init__(self, send_sem, recv_sem):
        self.send_sem, self.recv_sem = send_sem, recv_sem
        self.names = {}
        self.started = []

    def make(self, name, src, dst, device):
        number = self.names.setdefault(name, len(self.names))
        return pltpu.make_async_remote_copy(
            src_ref=src,
            dst_ref=dst,
            send_sem=self.send_sem.at[number],
            recv_sem=self.recv_sem.at[number],
            device_id=device,
            device_id_type=pl.DeviceIdType.MESH,
        )

    def send(self, name, src, dst, device):
        copy = self.make(name, src, dst, device)
        copy.start()
        self.started.append(copy)

    def receive(self, name, dst, device):
        self.make(name, dst, dst, device).wait_recv()

    def finish(self):
        for copy in self.started:
            copy.wait_send()


def plane_device(dx, dy):
    rank = lax.axis_index("mod")
    x, y = lax.rem(rank, SIDE), rank // SIDE
    return lax.rem(y + dy + SIDE, SIDE) * SIDE + lax.rem(x + dx + SIDE, SIDE)


def line_device(dz, other=False):
    rank = lax.axis_index("seq")
    z, core = rank // 2, lax.rem(rank, 2)
    return lax.rem(z + dz + SIDE, SIDE) * 2 + (1 - core if other else core)


def plane_neighbours():
    return [{"mod": plane_device(*step)} for step in ((1, 0), (-1, 0), (0, 1), (0, -1))]


def line_neighbours():
    return [{"seq": line_device(1)}, {"seq": line_device(-1)}, {"seq": line_device(0, True)}]


def plane_gather(copies, name, src, out):
    half = src.shape[0] // 2

    def part(turn, which):
        if which is None:
            return pl.ds(turn * half, half)
        return pl.ds(turn * half + which * (half // 2), half // 2)

    def device(turn, da, db):
        return plane_device(da, db) if turn == 0 else plane_device(db, da)

    def region(turn, da, db, which):
        return out.at[device(turn, da, db), part(turn, which)]

    def target(turn, axis, way):
        return {"mod": device(turn, way, 0) if axis == "a" else device(turn, 0, way)}

    def send(turn, axis, way, kind, offset):
        which = None if kind == "full" else (0 if way > 0 else 1)
        own = kind == "full" and offset == 0
        da = (0 if kind == "full" else -way) if axis == "a" else offset
        db = 0 if axis == "a" or kind == "full" else -way
        there = region(turn, da, db, which)
        here = src.at[part(turn, which)] if own else there
        copies.send((name, turn, axis, way, kind, offset), here, there, target(turn, axis, way))

    def receive(turn, axis, way, kind, offset):
        which = None if kind == "full" else (0 if way > 0 else 1)
        far = -way if kind == "full" else 2
        da, db = (far, 0) if axis == "a" else (offset, far)
        copies.receive(
            (name, turn, axis, way, kind, offset),
            region(turn, da, db, which),
            target(turn, axis, way),
        )

    ways, turns = (1, -1), (0, 1)

    def begin():
        for turn in turns:
            for way in ways:
                send(turn, "a", way, "full", 0)
        for turn in turns:
            for way in ways:
                send(turn, "b", way, "full", 0)

    def near():
        for way in ways:
            for turn in turns:
                receive(turn, "a", way, "full", 0)
                send(turn, "a", way, "half", 0)
                for second in ways:
                    send(turn, "b", second, "full", -way)

    def far():
        for turn in turns:
            for way in ways:
                receive(turn, "a", way, "half", 0)
            for second in ways:
                send(turn, "b", second, "full", 2)

    def fold(offset):
        for turn in turns:
            for way in ways:
                receive(turn, "b", way, "full", offset)
                send(turn, "b", way, "half", offset)

    def last(offset):
        for turn in turns:
            for way in ways:
                receive(turn, "b", way, "half", offset)

    return begin, near, far, fold, last


def line_gather(copies, name, src, out):
    half = src.shape[0] // 2

    def region(dz, other, which):
        rows = pl.ds(0, 2 * half) if which is None else pl.ds(which * half, half)
        return out.at[line_device(dz, other), rows]

    def along(way):
        return {"seq": line_device(way)}

    sibling = {"seq": line_device(0, True)}

    def pass_on(dz):
        copies.send((name, "sib", dz), region(dz, False, None), region(dz, False, None), sibling)

    def stage_0():
        for way in (1, -1):
            copies.send((name, way, "full"), src, region(0, False, None), along(way))
        copies.send((name, "sib", 0), src, region(0, False, None), sibling)

    def stage_1():
        for way in (1, -1):
            which = 0 if way > 0 else 1
            copies.receive((name, way, "full"), region(-way, False, None), along(way))
            there = region(-way, False, which)
            copies.send((name, way, "half"), there, there, along(way))
        for way in (1, -1):
            pass_on(-way)

    def stage_2():
        for way in (1, -1):
            which = 0 if way > 0 else 1
            copies.receive((name, way, "half"), region(2, False, which), along(way))
        pass_on(2)

    def last():
        for dz in (0, -1, 1, 2):
            copies.receive((name, "sib", dz), region(dz, True, None), sibling)

    return [stage_0, stage_1, stage_2, last]


def add(*terms):
    total = terms[0].astype(jnp.float32)
    for term in terms[1:]:
        total = total + term.astype(jnp.float32)
    return total.astype(jnp.bfloat16)


class RingSum:
    def __init__(self, copies, name, source, device, halves, fulls, sums):
        self.copies, self.name, self.source, self.device = copies, name, source, device
        self.halves, self.fulls, self.sums = halves, fulls, sums
        self.half = halves.shape[1]

    def rows(self, which):
        return pl.ds(which * self.half, self.half)

    def send(self, kind, way, src, dst):
        self.copies.send((self.name, kind, way), src, dst, self.device(way))

    def receive(self, kind, way, dst):
        self.copies.receive((self.name, kind, way), dst, self.device(way))

    def far(self):
        for number, way in enumerate((1, -1)):
            self.send("half", way, self.source(2).at[self.rows(number)], self.halves.at[number])

    def early(self, way):
        number = 0 if way > 0 else 1
        there = self.fulls.at[number, self.rows(1 - number)]
        self.send("early", way, self.source(way).at[self.rows(1 - number)], there)

    def late(self):
        for number, way in enumerate((1, -1)):
            self.receive("half", way, self.halves.at[number])
            term = self.source(way)[self.rows(number)]
            self.sums[number] = add(term, self.halves[number])
            self.send("late", way, self.sums.at[number], self.fulls.at[number, self.rows(number)])

    def result(self):
        for number, way in enumerate((1, -1)):
            self.receive("early", way, self.fulls.at[number, self.rows(1 - number)])
            self.receive("late", way, self.fulls.at[number, self.rows(number)])
        return add(self.source(0)[...], self.fulls[0], self.fulls[1])


def remote_params(number):
    return pltpu.CompilerParams(
        collective_id=number, has_side_effects=True, vmem_limit_bytes=VMEM_BYTES
    )


def semaphores(count):
    return [pltpu.SemaphoreType.DMA((count,)), pltpu.SemaphoreType.DMA((count,))]


def front_kernel(
    tokens,
    modality,
    wq_ref,
    wk_ref,
    wv_ref,
    q_out,
    sort_out,
    table_out,
    k_all,
    v_all,
    columns,
    rows_all,
    weights,
    pieces,
    acc,
    kv_own,
    table,
    send_sem,
    recv_sem,
    own_sem,
):
    copies = Copies(send_sem, recv_sem)
    rows, depth = tokens.shape
    groups, width, half = weights.shape[1], q_out.shape[1], rows // 2
    count = pieces.shape[0]
    me, place = lax.axis_index("seq"), lax.axis_index("mod")
    others = [lax.rem(me + step, count) for step in range(1, count)]
    greeted = [{"seq": other} for other in others] + plane_neighbours()
    greet(greeted)
    loads = [
        pltpu.make_async_copy(weight, weights.at[which], own_sem.at[which])
        for which, weight in enumerate((wq_ref, wk_ref, wv_ref))
    ]
    for load in loads:
        load.start()

    kind = modality[...]
    counts = [jnp.sum((kind == group).astype(jnp.int32)) for group in range(groups)]
    firsts = [jnp.int32(0)]
    for group in range(groups):
        firsts.append(firsts[-1] + counts[group])
    lane = lax.broadcasted_iota(jnp.int32, table.shape, 1)
    table[...] = sum(jnp.where(lane > group, counts[group], 0) for group in range(groups))

    lanes = lax.broadcasted_iota(jnp.int32, (rows, 128), 1)
    one_hot = (lanes == kind).astype(jnp.bfloat16)
    down = lax.broadcasted_iota(jnp.int32, (rows, rows), 0)
    across = lax.broadcasted_iota(jnp.int32, (rows, rows), 1)
    first_lane = lax.broadcasted_iota(jnp.int32, (1, 128), 1)
    base = jnp.zeros((1, 128), jnp.float32)
    for group in range(groups):
        base = jnp.where(first_lane == group, firsts[group].astype(jnp.float32), base)
    before = dot((across < down).astype(jnp.bfloat16), one_hot) + base
    rank = jnp.sum(before * one_hot.astype(jnp.float32), 1, keepdims=True).astype(jnp.int32)
    unsort = (rank == across).astype(jnp.bfloat16)
    sort = unsort.T
    sort_out[...] = sort
    rows_all[place] = dot(sort, tokens[...]).astype(jnp.bfloat16)

    line = lax.broadcasted_iota(jnp.int32, (rows, 1), 0)
    sorted_kind = sum((line >= firsts[group]).astype(jnp.int32) for group in range(1, groups))

    def multiply(blocks, new):
        for which in (1, 2, 0):
            low = middle = high = None
            for step in blocks:
                block = plane_device(*step)
                deep = pl.ds(pl.multiple_of(block * depth, depth), depth)
                x = rows_all[block]
                terms = []
                for group, at in enumerate((slice(0, half), slice(0, rows), slice(half, rows))):
                    own = jnp.where(sorted_kind[at] == group, x[at], jnp.zeros_like(x[at]))
                    terms.append(dot(own, weights[which, group, deep, :]))
                low = terms[0] if low is None else low + terms[0]
                middle = terms[1] if middle is None else middle + terms[1]
                high = terms[2] if high is None else high + terms[2]
            span = slice(which * width, (which + 1) * width)
            for number, part in enumerate((low, high)):
                at = slice(number * half, (number + 1) * half)
                if new:
                    acc[at, span] = part + middle[at]
                else:
                    acc[at, span] += part + middle[at]

    def projected(which):
        span = slice(which * width, (which + 1) * width)
        return dot(unsort, acc[:, span].astype(jnp.bfloat16)).astype(jnp.bfloat16)

    pl.semaphore_wait(pltpu.get_barrier_semaphore(), len(greeted))
    for step, other in enumerate(others):
        copies.send(("table", step), table, table_out.at[me], {"seq": other})
    own_table = pltpu.make_async_copy(table, table_out.at[me], own_sem.at[3])
    own_table.start()
    begin, near, far, fold, last = plane_gather(
        copies, "rows", rows_all.at[place], rows_all
    )
    begin()
    near()
    fold(0)
    for load in loads:
        load.wait()
    multiply([(0, 0), (1, 0), (-1, 0), (0, 1), (0, -1)], True)
    far()
    last(0)
    fold(-1)
    multiply([(2, 0), (0, 2)], False)
    fold(1)
    fold(2)
    multiply([(1, 1), (1, -1), (-1, 1), (-1, -1)], False)
    last(-1)
    last(1)
    multiply([(1, 2), (-1, 2), (2, 1), (2, -1)], False)
    last(2)

    deep = pieces.shape[2]

    def piece(target):
        return rows_all.at[
            pl.ds(2 * target, 2), pl.ds(pl.multiple_of(place * deep, deep), deep)
        ]

    own_piece = pltpu.make_async_copy(piece(me), pieces.at[me], own_sem.at[4])
    own_piece.start()
    for step, other in enumerate(others):
        copies.send(("piece", step), piece(other), pieces.at[me], {"seq": other})
    multiply([(2, 2)], False)
    kv_own[0] = projected(1)
    kv_own[1] = projected(2)
    own_keys = pltpu.make_async_copy(kv_own.at[0], k_all.at[me], own_sem.at[5])
    own_values = pltpu.make_async_copy(kv_own.at[1], v_all.at[me], own_sem.at[6])
    own_keys.start()
    own_values.start()
    keys = line_gather(copies, "keys", kv_own.at[0], k_all)
    values = line_gather(copies, "values", kv_own.at[1], v_all)
    keys[0]()
    values[0]()
    for step in range(count - 1):
        sender = lax.rem(me + count - 1 - step, count)
        copies.receive(("piece", step), pieces.at[sender], {"seq": others[step]})
    own_piece.wait()
    own_columns = pltpu.make_async_copy(pieces, columns.at[place], own_sem.at[7])
    own_columns.start()
    begin, near, far, fold, last = plane_gather(copies, "columns", pieces, columns)
    begin()
    q_out[...] = projected(0)
    near()
    fold(0)
    keys[1]()
    far()
    last(0)
    fold(-1)
    values[1]()
    fold(1)
    keys[2]()
    fold(2)
    values[2]()
    for offset in (-1, 1, 2):
        last(offset)
    keys[3]()
    values[3]()
    for step in range(count - 1):
        sender = lax.rem(me + count - 1 - step, count)
        copies.receive(("table", step), table_out.at[sender], {"seq": others[step]})
    copies.finish()
    for own in (own_table, own_keys, own_values, own_columns):
        own.wait()


def front(tokens, modality, weights, count):
    rows, depth = tokens.shape
    groups, tall, width = weights[0].shape
    blocks = SIDE * SIDE
    kind = tokens.dtype
    piece = (count, 2, rows // blocks, depth)
    half = jax.ShapeDtypeStruct((count, rows, width), kind)
    return pl.pallas_call(
        front_kernel,
        out_shape=(
            jax.ShapeDtypeStruct((rows, width), kind),
            jax.ShapeDtypeStruct((rows, rows), kind),
            jax.ShapeDtypeStruct((count, 8, 128), jnp.int32),
            half,
            half,
            jax.ShapeDtypeStruct((blocks, *piece), kind),
        ),
        in_specs=[WHOLE, WHOLE, ANY, ANY, ANY],
        out_specs=(WHOLE, WHOLE, WHOLE, ANY, ANY, ANY),
        scratch_shapes=[
            pltpu.VMEM((blocks, rows, depth), kind),
            pltpu.VMEM((3, groups, tall, width), kind),
            pltpu.VMEM(piece, kind),
            pltpu.VMEM((rows, 3 * width), jnp.float32),
            pltpu.VMEM((2, rows, width), kind),
            pltpu.VMEM((8, 128), jnp.int32),
            *semaphores(116),
            pltpu.SemaphoreType.DMA((8,)),
        ],
        compiler_params=remote_params(0),
    )(tokens, modality, *weights)


def key_sum_kernel(
    dk, dv, out, theirs, ours, halves, fulls, sums, send_sem, recv_sem
):
    copies = Copies(send_sem, recv_sem)
    enter(line_neighbours())
    sibling = {"seq": line_device(0, True)}
    places = {offset: number for number, offset in enumerate(OFFSETS)}
    width = dk.shape[2]
    parts = ((dk, pl.ds(0, width)), (dv, pl.ds(width, width)))
    for offset in OFFSETS:
        for which, (partial, span) in enumerate(parts):
            copies.send(
                ("pair", offset, which),
                partial.at[line_device(offset, True)],
                theirs.at[places[offset], :, span],
                sibling,
            )
    ring = RingSum(
        copies,
        "ring",
        lambda offset: ours.at[places[offset]],
        lambda way: {"seq": line_device(way)},
        halves,
        fulls,
        sums,
    )
    for offset in OFFSETS:
        for which, (partial, span) in enumerate(parts):
            there = theirs.at[places[offset], :, span]
            copies.receive(("pair", offset, which), there, sibling)
            ours[places[offset], :, span] = add(partial[line_device(offset)], there[...])
        if offset == 2:
            ring.far()
        elif offset != 0:
            ring.early(offset)
    ring.late()
    out[...] = ring.result()
    copies.finish()


def key_sum(dk, dv):
    _, tall, width = dk.shape
    width = 2 * width

    def buffer(count, rows):
        return pltpu.VMEM((count, rows, width), dk.dtype)

    return pl.pallas_call(
        key_sum_kernel,
        out_shape=jax.ShapeDtypeStruct((tall, width), dk.dtype),
        in_specs=[WHOLE, WHOLE],
        out_specs=WHOLE,
        scratch_shapes=[
            buffer(SIDE, tall),
            buffer(SIDE, tall),
            buffer(2, tall // 2),
            buffer(2, tall),
            buffer(2, tall // 2),
            *semaphores(16),
        ],
        compiler_params=remote_params(2),
    )(dk, dv)


def tail_kernel(
    table,
    act_query,
    act_key_value,
    sort,
    wq_ref,
    wk_ref,
    wv_ref,
    act_all,
    out,
    weights,
    act_own,
    middle,
    outer,
    partial,
    halves,
    fulls,
    sums,
    results,
    send_sem,
    recv_sem,
    own_sem,
    load_sem,
):
    copies = Copies(send_sem, recv_sem)
    greeted = plane_neighbours() + line_neighbours()
    greet(greeted)
    _, groups, _, depth = weights.shape
    rows = sort.shape[0]
    me = lax.axis_index("seq")
    half = rows // 2
    order = [(2, 2), (1, 2), (-1, 2), (2, 1), (2, -1), (0, 2), (2, 0)]
    order += [(1, 1), (1, -1), (-1, 1), (-1, -1)]
    order += [(0, 1), (0, -1), (1, 0), (-1, 0), (0, 0)]
    loads = {}
    for number, step in enumerate(order):
        at = pl.ds(pl.multiple_of(plane_device(*step) * depth, depth), depth)
        loads[step] = [
            pltpu.make_async_copy(
                weight.at[:, at], weights.at[which, :, at], load_sem.at[3 * number + which]
            )
            for which, weight in enumerate((wq_ref, wk_ref, wv_ref))
        ]
        for load in loads[step]:
            load.start()

    width = act_query.shape[1]
    acts = (act_query[...], act_key_value[:, :width], act_key_value[:, width:])
    for which, act in enumerate(acts):
        act_own[which] = dot(sort[...], act).astype(jnp.bfloat16)
    own_act = [
        pltpu.make_async_copy(act_own.at[which], act_all.at[which, me], own_sem.at[which])
        for which in range(3)
    ]
    for own in own_act:
        own.start()
    pl.semaphore_wait(pltpu.get_barrier_semaphore(), len(greeted))
    lines = [
        line_gather(copies, ("act", which), act_own.at[which], act_all.at[which])
        for which in range(3)
    ]
    for line in lines:
        line[0]()

    place = lax.broadcasted_iota(jnp.int32, (rows, 1), 0)
    sorted_kind = sum(
        (place >= table[me, 0, group]).astype(jnp.int32) for group in range(1, groups)
    )
    for which in range(3):
        act = act_own[which]
        span = slice(which * width, (which + 1) * width)
        middle[:, span] = jnp.where(sorted_kind == 1, act, jnp.zeros_like(act))
        for number in range(2):
            at = slice(number * half, (number + 1) * half)
            outer[number, :, span] = jnp.where(
                sorted_kind[at] == 2 * number, act[at], jnp.zeros_like(act[at])
            )

    def multiply(step):
        for load in loads[step]:
            load.wait()
        block = plane_device(*step)
        deep = pl.ds(pl.multiple_of(block * depth, depth), depth)

        def product(acts, group):
            total = None
            for which in range(3):
                act = acts[:, which * width : (which + 1) * width]
                term = dot(act, weights[which, group, deep, :], 1, 1)
                total = term if total is None else total + term
            return total

        both = product(middle, 1)
        for number in range(2):
            at = slice(number * half, (number + 1) * half)
            part = product(outer.at[number], 2 * number) + both[at]
            partial[block, at] = part.astype(jnp.bfloat16)

    def device(turn, da, db):
        return plane_device(da, db) if turn == 0 else plane_device(db, da)

    def second(turn, place):
        offset, number = OFFSETS[place], turn * len(OFFSETS) + place
        return RingSum(
            copies,
            ("b", number),
            lambda db: partial.at[device(turn, offset, db), pl.ds(turn * half, half)],
            lambda way: {"mod": device(turn, 0, way)},
            halves.at[number],
            fulls.at[number],
            sums.at[number],
        )

    def first(turn):
        number = 2 * len(OFFSETS) + turn
        return RingSum(
            copies,
            ("a", turn),
            lambda da: results.at[turn, OFFSETS.index(da)],
            lambda way: {"mod": device(turn, way, 0)},
            halves.at[number],
            fulls.at[number],
            sums.at[number],
        )

    rings = {
        (turn, OFFSETS[place]): second(turn, place) for place in range(4) for turn in range(2)
    }
    tops = [first(turn) for turn in range(2)]
    for number, step in enumerate(order):
        multiply(step)
        for turn in range(2):
            da, db = step if turn == 0 else (step[1], step[0])
            if db == 2:
                rings[turn, da].far()
            elif db != 0:
                rings[turn, da].early(db)
        if number == 6:
            lines[0][1]()
        if number == 10:
            for turn in range(2):
                rings[turn, 2].late()
            lines[1][1]()
        if number == 12:
            for turn in range(2):
                rings[turn, -1].late()
        if number == 14:
            for turn in range(2):
                rings[turn, 1].late()
    for turn in range(2):
        rings[turn, 0].late()
    lines[2][1]()

    for offset in OFFSETS:
        for turn in range(2):
            results[turn, OFFSETS.index(offset)] = rings[turn, offset].result()
            if offset == 2:
                tops[turn].far()
            elif offset != 0:
                tops[turn].early(offset)
        if offset == 2:
            lines[0][2]()
    for top in tops:
        top.late()
    lines[1][2]()
    total = None
    for turn, top in enumerate(tops):
        term = dot(sort[turn * half : (turn + 1) * half], top.result(), 0, 0)
        total = term if total is None else total + term
    out[...] = total.astype(out.dtype)
    lines[2][2]()
    for line in lines:
        line[3]()
    copies.finish()
    for own in own_act:
        own.wait()


def tail(table, act_query, act_key_value, sort, weights, count):
    rows, width = act_query.shape
    groups, tall, _ = weights[0].shape
    kind = act_query.dtype
    half, blocks = rows // 2, SIDE * SIDE
    depth = tall // blocks

    def buffer(*shape):
        return pltpu.VMEM((*shape, depth), kind)

    return pl.pallas_call(
        tail_kernel,
        out_shape=(
            jax.ShapeDtypeStruct((3, count, rows, width), kind),
            jax.ShapeDtypeStruct((rows, depth), kind),
        ),
        in_specs=[SMEM, WHOLE, WHOLE, WHOLE, ANY, ANY, ANY],
        out_specs=(ANY, WHOLE),
        scratch_shapes=[
            pltpu.VMEM((3, groups, tall, width), kind),
            pltpu.VMEM((3, rows, width), kind),
            pltpu.VMEM((rows, 3 * width), kind),
            pltpu.VMEM((2, half, 3 * width), kind),
            buffer(blocks, rows),
            buffer(10, 2, half // 2),
            buffer(10, 2, half),
            buffer(10, 2, half // 2),
            buffer(2, 4, half),
            *semaphores(96),
            pltpu.SemaphoreType.DMA((3,)),
            pltpu.SemaphoreType.DMA((3 * blocks,)),
        ],
        compiler_params=remote_params(3),
    )(table, act_query, act_key_value, sort, *weights)


def per_device(tokens, modality, doc_lengths, w_query, w_key, w_value, d_out):
    groups = w_query.shape[0]
    seq_count = lax.axis_size("seq")
    weights = (w_query, w_key, w_value)
    queries, sort_matrix, table, keys, values, token_columns = front(
        tokens, modality, weights, seq_count
    )
    attn_out, act_query, key_part, value_part = attention(
        doc_lengths, queries, keys, values, d_out
    )
    act_key_value = key_sum(key_part, value_part)
    act_all, grad_tokens = tail(
        table, act_query, act_key_value, sort_matrix, weights, seq_count
    )
    grads = weight_grads(table, token_columns, act_all, groups)
    return (attn_out, grad_tokens, *grads)


def solution(mesh):
    placed = (
        P("seq", "mod"),
        P("seq", None),
        P(),
        P(None, None, "mod"),
        P(None, None, "mod"),
        P(None, None, "mod"),
        P("seq", "mod"),
    )
    return jax.shard_map(
        per_device,
        mesh=mesh,
        in_specs=placed,
        out_specs=(
            P("seq", "mod"),
            P("seq", "mod"),
            P(None, "seq", "mod"),
            P(None, "seq", "mod"),
            P(None, "seq", "mod"),
        ),
        check_vma=False,
    )
```

```python
import functools
import math

import jax
import jax.numpy as jnp
from jax import lax
from jax.experimental import pallas as pl
from jax.experimental.pallas import tpu as pltpu
from jax.sharding import PartitionSpec as P

HEAD_DIM = 128
WINDOW_PAD = 16
MAX_BACK = 5
VMEM_BYTES = 56 * 1024 * 1024


def dot(left, right, left_dim=1, right_dim=0):
    return lax.dot_general(
        left,
        right,
        (((left_dim,), (right_dim,)), ((), ())),
        preferred_element_type=jnp.float32,
    )


def params():
    return pltpu.CompilerParams(vmem_limit_bytes=VMEM_BYTES)


ANY = pl.BlockSpec(memory_space=pl.ANY)
SMEM = pl.BlockSpec(memory_space=pltpu.SMEM)
WHOLE = pl.BlockSpec(memory_space=pltpu.VMEM)


def weight_kernel(
    table, x_ref, act_ref, gq_ref, gk_ref, gv_ref, x_in, act_in, x_rows, x_turned, grads, sem
):
    count, rows, wide = x_rows.shape
    groups, _, depth = x_turned.shape
    window = depth // count
    loads = [pltpu.make_async_copy(x_ref, x_in, sem.at[0])]
    for which in range(3):
        loads.append(
            pltpu.make_async_copy(act_ref.at[which], act_in.at[which], sem.at[1 + which])
        )
    for load in loads:
        load.start()

    def bounds(block, group):
        low, high = table[block, 0, group], table[block, 0, group + 1]
        start = jnp.minimum((low // WINDOW_PAD) * WINDOW_PAD, rows - window)
        return low, high, pl.multiple_of(start, WINDOW_PAD)

    def chosen(block, group, start, size):
        low, high, _ = bounds(block, group)
        at = pl.ds(start, size)
        place = lax.broadcasted_iota(jnp.int32, (size, 1), 0) + start
        picked = x_rows[block, at, :]
        return jnp.where((place >= low) & (place < high), picked, jnp.zeros_like(picked))

    loads[0].wait()
    for block in range(count):
        for part in range(x_in.shape[2]):
            cols = x_in.shape[4]
            x_rows[block, :, part * cols : (part + 1) * cols] = x_in[:, block, part].reshape(
                rows, cols
            )
        for group in range(groups):
            picked = chosen(block, group, bounds(block, group)[2], window)
            x_turned[group, :, block * window : (block + 1) * window] = picked.T
    stores = []
    for which, out in enumerate((gq_ref, gk_ref, gv_ref)):
        loads[1 + which].wait()
        for group in range(groups):
            total = None
            for block in range(count):
                at = pl.ds(bounds(block, group)[2], window)
                term = dot(
                    x_turned[group, :, block * window : (block + 1) * window],
                    act_in[which, block, at, :],
                )
                total = term if total is None else total + term
            grads[which, group] = total

            def rest(block, _):
                low, high, start = bounds(block, group)

                @pl.when(high > start + window)
                def _():
                    at = pl.multiple_of(start + window, WINDOW_PAD)
                    picked = chosen(block, group, at, WINDOW_PAD)
                    act = act_in[which, block, pl.ds(at, WINDOW_PAD), :]
                    grads[which, group] += dot(picked, act, 0, 0)

                return 0

            lax.fori_loop(0, count, rest, 0)
        stores.append(pltpu.make_async_copy(grads.at[which], out, sem.at[4 + which]))
        stores[-1].start()
    for store in stores:
        store.wait()


def weight_grads(table, x, act, groups):
    pieces, count, parts, deep, cols = x.shape
    rows, wide = pieces * deep, parts * cols
    width = act.shape[3]
    out = jax.ShapeDtypeStruct((groups, wide, width), jnp.float32)
    return pl.pallas_call(
        weight_kernel,
        out_shape=(out, out, out),
        in_specs=[SMEM, ANY, ANY],
        out_specs=(ANY, ANY, ANY),
        scratch_shapes=[
            pltpu.VMEM(x.shape, x.dtype),
            pltpu.VMEM(act.shape, act.dtype),
            pltpu.VMEM((count, rows, wide), x.dtype),
            pltpu.VMEM((groups, wide, count * (rows // 2)), x.dtype),
            pltpu.VMEM((3, groups, wide, width), jnp.float32),
            pltpu.SemaphoreType.DMA((7,)),
        ],
        compiler_params=params(),
    )(table, x, act)


SIDE = 4
OFFSETS = (2, -1, 1, 0)


def greet(devices):
    barrier = pltpu.get_barrier_semaphore()
    for device in devices:
        pl.semaphore_signal(
            barrier, inc=1, device_id=device, device_id_type=pl.DeviceIdType.MESH
        )


def enter(devices):
    greet(devices)
    pl.semaphore_wait(pltpu.get_barrier_semaphore(), len(devices))


class Copies:
    def __init__(self, send_sem, recv_sem):
        self.send_sem, self.recv_sem = send_sem, recv_sem
        self.names = {}
        self.started = []

    def make(self, name, src, dst, device):
        number = self.names.setdefault(name, len(self.names))
        return pltpu.make_async_remote_copy(
            src_ref=src,
            dst_ref=dst,
            send_sem=self.send_sem.at[number],
            recv_sem=self.recv_sem.at[number],
            device_id=device,
            device_id_type=pl.DeviceIdType.MESH,
        )

    def send(self, name, src, dst, device):
        copy = self.make(name, src, dst, device)
        copy.start()
        self.started.append(copy)

    def receive(self, name, dst, device):
        self.make(name, dst, dst, device).wait_recv()

    def finish(self):
        for copy in self.started:
            copy.wait_send()


def plane_device(dx, dy):
    rank = lax.axis_index("mod")
    x, y = lax.rem(rank, SIDE), rank // SIDE
    return lax.rem(y + dy + SIDE, SIDE) * SIDE + lax.rem(x + dx + SIDE, SIDE)


def line_device(dz, other=False):
    rank = lax.axis_index("seq")
    z, core = rank // 2, lax.rem(rank, 2)
    return lax.rem(z + dz + SIDE, SIDE) * 2 + (1 - core if other else core)


def plane_neighbours():
    return [{"mod": plane_device(*step)} for step in ((1, 0), (-1, 0), (0, 1), (0, -1))]


def line_neighbours():
    return [{"seq": line_device(1)}, {"seq": line_device(-1)}, {"seq": line_device(0, True)}]


def plane_gather(copies, name, src, out):
    half = src.shape[0] // 2

    def part(turn, which):
        if which is None:
            return pl.ds(turn * half, half)
        return pl.ds(turn * half + which * (half // 2), half // 2)

    def device(turn, da, db):
        return plane_device(da, db) if turn == 0 else plane_device(db, da)

    def region(turn, da, db, which):
        return out.at[device(turn, da, db), part(turn, which)]

    def target(turn, axis, way):
        return {"mod": device(turn, way, 0) if axis == "a" else device(turn, 0, way)}

    def send(turn, axis, way, kind, offset):
        which = None if kind == "full" else (0 if way > 0 else 1)
        own = kind == "full" and offset == 0
        da = (0 if kind == "full" else -way) if axis == "a" else offset
        db = 0 if axis == "a" or kind == "full" else -way
        there = region(turn, da, db, which)
        here = src.at[part(turn, which)] if own else there
        copies.send((name, turn, axis, way, kind, offset), here, there, target(turn, axis, way))

    def receive(turn, axis, way, kind, offset):
        which = None if kind == "full" else (0 if way > 0 else 1)
        far = -way if kind == "full" else 2
        da, db = (far, 0) if axis == "a" else (offset, far)
        copies.receive(
            (name, turn, axis, way, kind, offset),
            region(turn, da, db, which),
            target(turn, axis, way),
        )

    ways, turns = (1, -1), (0, 1)

    def begin():
        for turn in turns:
            for way in ways:
                send(turn, "a", way, "full", 0)
        for turn in turns:
            for way in ways:
                send(turn, "b", way, "full", 0)

    def near():
        for way in ways:
            for turn in turns:
                receive(turn, "a", way, "full", 0)
                send(turn, "a", way, "half", 0)
                for second in ways:
                    send(turn, "b", second, "full", -way)

    def far():
        for turn in turns:
            for way in ways:
                receive(turn, "a", way, "half", 0)
            for second in ways:
                send(turn, "b", second, "full", 2)

    def fold(offset):
        for turn in turns:
            for way in ways:
                receive(turn, "b", way, "full", offset)
                send(turn, "b", way, "half", offset)

    def last(offset):
        for turn in turns:
            for way in ways:
                receive(turn, "b", way, "half", offset)

    return begin, near, far, fold, last


def line_gather(copies, name, src, out):
    half = src.shape[0] // 2

    def region(dz, other, which):
        rows = pl.ds(0, 2 * half) if which is None else pl.ds(which * half, half)
        return out.at[line_device(dz, other), rows]

    def along(way):
        return {"seq": line_device(way)}

    sibling = {"seq": line_device(0, True)}

    def pass_on(dz):
        copies.send((name, "sib", dz), region(dz, False, None), region(dz, False, None), sibling)

    def stage_0():
        for way in (1, -1):
            copies.send((name, way, "full"), src, region(0, False, None), along(way))
        copies.send((name, "sib", 0), src, region(0, False, None), sibling)

    def stage_1():
        for way in (1, -1):
            which = 0 if way > 0 else 1
            copies.receive((name, way, "full"), region(-way, False, None), along(way))
            there = region(-way, False, which)
            copies.send((name, way, "half"), there, there, along(way))
        for way in (1, -1):
            pass_on(-way)

    def stage_2():
        for way in (1, -1):
            which = 0 if way > 0 else 1
            copies.receive((name, way, "half"), region(2, False, which), along(way))
        pass_on(2)

    def last():
        for dz in (0, -1, 1, 2):
            copies.receive((name, "sib", dz), region(dz, True, None), sibling)

    return [stage_0, stage_1, stage_2, last]


def add(*terms):
    total = terms[0].astype(jnp.float32)
    for term in terms[1:]:
        total = total + term.astype(jnp.float32)
    return total.astype(jnp.bfloat16)


class RingSum:
    def __init__(self, copies, name, source, device, halves, fulls, sums, absent=()):
        self.absent = absent
        self.copies, self.name, self.source, self.device = copies, name, source, device
        self.halves, self.fulls, self.sums = halves, fulls, sums
        self.half = halves.shape[1]

    def rows(self, which):
        return pl.ds(which * self.half, self.half)

    def send(self, kind, way, src, dst):
        self.copies.send((self.name, kind, way), src, dst, self.device(way))

    def receive(self, kind, way, dst):
        self.copies.receive((self.name, kind, way), dst, self.device(way))

    def far(self):
        for number, way in enumerate((1, -1)):
            self.send("half", way, self.source(2).at[self.rows(number)], self.halves.at[number])

    def early(self, way):
        number = 0 if way > 0 else 1
        there = self.fulls.at[number, self.rows(1 - number)]
        self.send("early", way, self.source(way).at[self.rows(1 - number)], there)

    def late(self):
        for number, way in enumerate((1, -1)):
            self.receive("half", way, self.halves.at[number])
            there = self.fulls.at[number, self.rows(number)]
            if way in self.absent:
                self.send("late", way, self.halves.at[number], there)
                continue
            term = self.source(way)[self.rows(number)]
            self.sums[number] = add(term, self.halves[number])
            self.send("late", way, self.sums.at[number], there)

    def result(self):
        parts = [[self.source(0)[self.rows(number)]] for number in range(2)]
        for number, way in enumerate((1, -1)):
            if way not in self.absent:
                there = self.rows(1 - number)
                self.receive("early", way, self.fulls.at[number, there])
                parts[1 - number].append(self.fulls[number, there])
            there = self.rows(number)
            self.receive("late", way, self.fulls.at[number, there])
            parts[number].append(self.fulls[number, there])
        return jnp.concatenate([add(*terms) for terms in parts], 0)


def remote_params(number):
    return pltpu.CompilerParams(
        collective_id=number, has_side_effects=True, vmem_limit_bytes=VMEM_BYTES
    )


def semaphores(count):
    return [pltpu.SemaphoreType.DMA((count,)), pltpu.SemaphoreType.DMA((count,))]


def front_kernel(
    tokens,
    modality,
    wq_ref,
    wk_ref,
    wv_ref,
    q_out,
    sort_out,
    table_out,
    k_all,
    v_all,
    pieces,
    rows_all,
    weights,
    acc,
    kv_own,
    table,
    send_sem,
    recv_sem,
    own_sem,
):
    copies = Copies(send_sem, recv_sem)
    rows, depth = tokens.shape
    groups, width, half = weights.shape[1], q_out.shape[1], rows // 2
    count = pieces.shape[0]
    me, place = lax.axis_index("seq"), lax.axis_index("mod")
    others = [lax.rem(me + step, count) for step in range(1, count)]
    greeted = [{"seq": other} for other in others] + plane_neighbours()
    greet(greeted)
    loads = [
        pltpu.make_async_copy(weight, weights.at[which], own_sem.at[which])
        for which, weight in enumerate((wq_ref, wk_ref, wv_ref))
    ]
    for load in loads:
        load.start()

    kind = modality[...]
    counts = [jnp.sum((kind == group).astype(jnp.int32)) for group in range(groups)]
    firsts = [jnp.int32(0)]
    for group in range(groups):
        firsts.append(firsts[-1] + counts[group])
    lane = lax.broadcasted_iota(jnp.int32, table.shape, 1)
    table[...] = sum(jnp.where(lane > group, counts[group], 0) for group in range(groups))

    lanes = lax.broadcasted_iota(jnp.int32, (rows, 128), 1)
    one_hot = (lanes == kind).astype(jnp.bfloat16)
    down = lax.broadcasted_iota(jnp.int32, (rows, rows), 0)
    across = lax.broadcasted_iota(jnp.int32, (rows, rows), 1)
    first_lane = lax.broadcasted_iota(jnp.int32, (1, 128), 1)
    base = jnp.zeros((1, 128), jnp.float32)
    for group in range(groups):
        base = jnp.where(first_lane == group, firsts[group].astype(jnp.float32), base)
    before = dot((across < down).astype(jnp.bfloat16), one_hot) + base
    rank = jnp.sum(before * one_hot.astype(jnp.float32), 1, keepdims=True).astype(jnp.int32)
    unsort = (rank == across).astype(jnp.bfloat16)
    sort = unsort.T
    sort_out[...] = sort
    rows_all[place] = dot(sort, tokens[...]).astype(jnp.bfloat16)

    line = lax.broadcasted_iota(jnp.int32, (rows, 1), 0)
    sorted_kind = sum((line >= firsts[group]).astype(jnp.int32) for group in range(1, groups))

    def multiply(blocks, new, wanted=(1, 2, 0)):
        for which in wanted:
            low = middle = high = None
            for step in blocks:
                block = plane_device(*step)
                deep = pl.ds(pl.multiple_of(block * depth, depth), depth)
                x = rows_all[block]
                terms = []
                for group, at in enumerate((slice(0, half), slice(0, rows), slice(half, rows))):
                    own = jnp.where(sorted_kind[at] == group, x[at], jnp.zeros_like(x[at]))
                    terms.append(dot(own, weights[which, group, deep, :]))
                low = terms[0] if low is None else low + terms[0]
                middle = terms[1] if middle is None else middle + terms[1]
                high = terms[2] if high is None else high + terms[2]
            span = slice(which * width, (which + 1) * width)
            for number, part in enumerate((low, high)):
                at = slice(number * half, (number + 1) * half)
                if new:
                    acc[at, span] = part + middle[at]
                else:
                    acc[at, span] += part + middle[at]

    def projected(which):
        span = slice(which * width, (which + 1) * width)
        return dot(unsort, acc[:, span].astype(jnp.bfloat16)).astype(jnp.bfloat16)

    pl.semaphore_wait(pltpu.get_barrier_semaphore(), len(greeted))
    for step, other in enumerate(others):
        copies.send(("table", step), table, table_out.at[me], {"seq": other})
    own_table = pltpu.make_async_copy(table, table_out.at[me], own_sem.at[3])
    own_table.start()
    begin, near, far, fold, last = plane_gather(
        copies, "rows", rows_all.at[place], rows_all
    )
    begin()
    near()
    fold(0)
    for load in loads:
        load.wait()
    multiply([(0, 0), (1, 0), (-1, 0), (0, 1), (0, -1)], True)
    far()
    last(0)
    fold(-1)
    multiply([(2, 0), (0, 2)], False)
    fold(1)
    fold(2)
    multiply([(1, 1), (1, -1), (-1, 1), (-1, -1)], False)
    last(-1)
    last(1)
    rest = [(1, 2), (-1, 2), (2, 1), (2, -1)]
    multiply(rest, False, (1, 2))
    last(2)

    deep = pieces.shape[2]

    def piece(target):
        return rows_all.at[
            pl.ds(2 * target, 2), pl.ds(pl.multiple_of(place * deep, deep), deep)
        ]

    own_piece = pltpu.make_async_copy(piece(me), pieces.at[me], own_sem.at[4])
    own_piece.start()
    for step, other in enumerate(others):
        copies.send(("piece", step), piece(other), pieces.at[me], {"seq": other})
    multiply([(2, 2)], False, (1, 2))
    kv_own[0] = projected(1)
    kv_own[1] = projected(2)
    own_keys = pltpu.make_async_copy(kv_own.at[0], k_all.at[me], own_sem.at[5])
    own_values = pltpu.make_async_copy(kv_own.at[1], v_all.at[me], own_sem.at[6])
    own_keys.start()
    own_values.start()
    keys = line_gather(copies, "keys", kv_own.at[0], k_all)
    values = line_gather(copies, "values", kv_own.at[1], v_all)
    keys[0]()
    values[0]()
    multiply([*rest, (2, 2)], False, (0,))
    q_out[...] = projected(0)
    for stage in (1, 2, 3):
        keys[stage]()
        values[stage]()
    for step in range(count - 1):
        sender = lax.rem(me + count - 1 - step, count)
        copies.receive(("table", step), table_out.at[sender], {"seq": others[step]})
        copies.receive(("piece", step), pieces.at[sender], {"seq": others[step]})
    copies.finish()
    for own in (own_table, own_keys, own_values, own_piece):
        own.wait()


def front(tokens, modality, weights, count):
    rows, depth = tokens.shape
    groups, tall, width = weights[0].shape
    blocks = SIDE * SIDE
    kind = tokens.dtype
    piece = (count, 2, rows // blocks, depth)
    half = jax.ShapeDtypeStruct((count, rows, width), kind)
    return pl.pallas_call(
        front_kernel,
        out_shape=(
            jax.ShapeDtypeStruct((rows, width), kind),
            jax.ShapeDtypeStruct((rows, rows), kind),
            jax.ShapeDtypeStruct((count, 8, 128), jnp.int32),
            half,
            half,
            jax.ShapeDtypeStruct(piece, kind),
        ),
        in_specs=[WHOLE, WHOLE, ANY, ANY, ANY],
        out_specs=(WHOLE, WHOLE, WHOLE, ANY, ANY, ANY),
        scratch_shapes=[
            pltpu.VMEM((blocks, rows, depth), kind),
            pltpu.VMEM((3, groups, tall, width), kind),
            pltpu.VMEM((rows, 3 * width), jnp.float32),
            pltpu.VMEM((2, rows, width), kind),
            pltpu.VMEM((8, 128), jnp.int32),
            *semaphores(76),
            pltpu.SemaphoreType.DMA((7,)),
        ],
        compiler_params=remote_params(0),
    )(tokens, modality, *weights)


def attention_kernel(
    lengths,
    q_ref,
    k_ref,
    v_ref,
    do_ref,
    pieces,
    out_ref,
    dq_ref,
    dkv_ref,
    columns,
    scores,
    dq_sum,
    away,
    theirs,
    mine,
    ours,
    halves,
    fulls,
    sums,
    send_sem,
    recv_sem,
    own_sem,
):
    copies = Copies(send_sem, recv_sem)
    greeted = plane_neighbours() + line_neighbours()
    greet(greeted)
    rows, width = q_ref.shape
    heads = width // HEAD_DIM
    scale = 1.0 / math.sqrt(HEAD_DIM)
    me, place = lax.axis_index("seq"), lax.axis_index("mod")
    first = jnp.maximum(me - (MAX_BACK - 1), 0)
    own_columns = pltpu.make_async_copy(pieces, columns.at[place], own_sem)
    own_columns.start()
    ends = [lengths[0]]
    for number in range(1, lengths.shape[0]):
        ends.append(ends[-1] + lengths[number])

    def document(positions):
        return sum((positions >= end).astype(jnp.int32) for end in ends)

    own = lax.broadcasted_iota(jnp.int32, (rows, 1), 0) + me * rows
    own_document = document(own)
    cols = [slice(h * HEAD_DIM, (h + 1) * HEAD_DIM) for h in range(heads)]
    vcols = [slice(width + h * HEAD_DIM, width + (h + 1) * HEAD_DIM) for h in range(heads)]
    pl.semaphore_wait(pltpu.get_barrier_semaphore(), len(greeted))
    begin, near, far, fold, last = plane_gather(copies, "columns", pieces, columns)
    begin()

    def score_step(block, row_max):
        key_pos = lax.broadcasted_iota(jnp.int32, (1, rows), 1) + block * rows
        visible = (key_pos <= own) & (document(key_pos) == own_document)
        new = []
        for h in range(heads):
            part = dot(q_ref[:, cols[h]], k_ref[block, :, cols[h]], 1, 1) * scale
            part = jnp.where(visible, part, -jnp.inf)
            scores[h, block - first] = part
            new.append(jnp.maximum(row_max[h], jnp.max(part, 1, keepdims=True)))
        return tuple(new)

    start = tuple(jnp.full((rows, 1), -jnp.inf, jnp.float32) for _ in range(heads))
    row_max = lax.fori_loop(first, me + 1, score_step, start)
    near()
    fold(0)

    def value_step(block, carry):
        new = []
        for h in range(heads):
            total, summed = carry[h]
            weights = jnp.exp(scores[h, block - first] - row_max[h])
            scores[h, block - first] = weights
            total = total + jnp.sum(weights, 1, keepdims=True)
            summed = summed + dot(weights.astype(jnp.bfloat16), v_ref[block, :, cols[h]])
            new.append((total, summed))
        return tuple(new)

    start = tuple(
        (jnp.zeros((rows, 1), jnp.float32), jnp.zeros((rows, HEAD_DIM), jnp.float32))
        for _ in range(heads)
    )
    totals = lax.fori_loop(first, me + 1, value_step, start)
    inverse, row_dot = [], []
    for h in range(heads):
        total, summed = totals[h]
        attended = (summed / total).astype(jnp.bfloat16)
        out_ref[:, cols[h]] = attended
        inverse.append(1.0 / total)
        row_dot.append(
            jnp.sum(
                do_ref[:, cols[h]].astype(jnp.float32) * attended.astype(jnp.float32),
                1,
                keepdims=True,
            )
        )
    dq_sum[...] = jnp.zeros_like(dq_sum)
    far()
    last(0)

    def grads(block, result):
        seen = (block >= first) & (block <= me)

        @pl.when(seen)
        def _():
            for h in range(heads):
                spread = dot(do_ref[:, cols[h]], v_ref[block, :, cols[h]], 1, 1)
                chances = scores[h, block - first] * inverse[h]
                dscore = (chances * (spread - row_dot[h]) * scale).astype(jnp.bfloat16)
                dq_sum[:, cols[h]] += dot(dscore, k_ref[block, :, cols[h]])
                result[:, cols[h]] = dot(dscore, q_ref[:, cols[h]], 0, 0).astype(jnp.bfloat16)
                result[:, vcols[h]] = dot(
                    chances.astype(jnp.bfloat16), do_ref[:, cols[h]], 0, 0
                ).astype(jnp.bfloat16)

        @pl.when(jnp.logical_not(seen))
        def _():
            result[...] = jnp.zeros(result.shape, jnp.bfloat16)

    sibling = {"seq": line_device(0, True)}
    order = (2, -1, 0)

    def compute(number):
        grads(line_device(order[number], True), away.at[number])
        copies.send(("pair", number), away.at[number], theirs.at[number], sibling)
        grads(line_device(order[number]), mine.at[number])

    def join(number):
        copies.receive(("pair", number), theirs.at[number], sibling)
        ours[number] = add(mine[number], theirs[number])

    ring = RingSum(
        copies,
        "ring",
        lambda offset: ours.at[order.index(offset)],
        lambda way: {"seq": line_device(way)},
        halves,
        fulls,
        sums,
        (1,),
    )
    compute(0)
    join(0)
    ring.far()
    fold(-1)
    compute(1)
    join(1)
    ring.early(-1)
    fold(1)
    compute(2)
    for h in range(heads):
        dq_ref[:, cols[h]] = dq_sum[:, cols[h]].astype(jnp.bfloat16)
    ring.late()
    fold(2)
    join(2)
    dkv_ref[...] = ring.result()
    for offset in (-1, 1, 2):
        last(offset)
    copies.finish()
    own_columns.wait()


def attention(lengths, q, k, v, do, pieces):
    rows, width = q.shape
    kind = q.dtype
    shape = jax.ShapeDtypeStruct((rows, width), kind)

    def buffer(count, tall):
        return pltpu.VMEM((count, tall, 2 * width), kind)

    return pl.pallas_call(
        attention_kernel,
        out_shape=(
            shape,
            shape,
            jax.ShapeDtypeStruct((rows, 2 * width), kind),
            jax.ShapeDtypeStruct((SIDE * SIDE, *pieces.shape), kind),
        ),
        in_specs=[SMEM] + [WHOLE] * 4 + [ANY],
        out_specs=(WHOLE, WHOLE, WHOLE, ANY),
        scratch_shapes=[
            pltpu.VMEM((width // HEAD_DIM, MAX_BACK, rows, rows), jnp.float32),
            pltpu.VMEM((rows, width), jnp.float32),
            buffer(3, rows),
            buffer(3, rows),
            buffer(3, rows),
            buffer(3, rows),
            buffer(2, rows // 2),
            buffer(2, rows),
            buffer(2, rows // 2),
            *semaphores(52),
            pltpu.SemaphoreType.DMA,
        ],
        compiler_params=remote_params(1),
    )(lengths, q, k, v, do, pieces)


def tail_kernel(
    table,
    act_query,
    act_key_value,
    sort,
    wq_ref,
    wk_ref,
    wv_ref,
    act_all,
    out,
    weights,
    act_own,
    middle,
    outer,
    partial,
    halves,
    fulls,
    sums,
    results,
    send_sem,
    recv_sem,
    own_sem,
    load_sem,
):
    copies = Copies(send_sem, recv_sem)
    greeted = plane_neighbours() + line_neighbours()
    greet(greeted)
    _, groups, _, depth = weights.shape
    rows = sort.shape[0]
    me = lax.axis_index("seq")
    half = rows // 2
    order = [(2, 2), (1, 2), (-1, 2), (2, 1), (2, -1), (0, 2), (2, 0)]
    order += [(1, 1), (1, -1), (-1, 1), (-1, -1)]
    order += [(0, 1), (0, -1), (1, 0), (-1, 0), (0, 0)]
    loads = {}
    for number, step in enumerate(order):
        at = pl.ds(pl.multiple_of(plane_device(*step) * depth, depth), depth)
        loads[step] = [
            pltpu.make_async_copy(
                weight.at[:, at], weights.at[which, :, at], load_sem.at[3 * number + which]
            )
            for which, weight in enumerate((wq_ref, wk_ref, wv_ref))
        ]
        for load in loads[step]:
            load.start()

    width = act_query.shape[1]
    acts = (act_query[...], act_key_value[:, :width], act_key_value[:, width:])
    for which, act in enumerate(acts):
        act_own[which] = dot(sort[...], act).astype(jnp.bfloat16)
    own_act = [
        pltpu.make_async_copy(act_own.at[which], act_all.at[which, me], own_sem.at[which])
        for which in range(3)
    ]
    for own in own_act:
        own.start()
    pl.semaphore_wait(pltpu.get_barrier_semaphore(), len(greeted))
    lines = [
        line_gather(copies, ("act", which), act_own.at[which], act_all.at[which])
        for which in range(3)
    ]
    for line in lines:
        line[0]()

    place = lax.broadcasted_iota(jnp.int32, (rows, 1), 0)
    sorted_kind = sum(
        (place >= table[me, 0, group]).astype(jnp.int32) for group in range(1, groups)
    )
    for which in range(3):
        act = act_own[which]
        span = slice(which * width, (which + 1) * width)
        middle[:, span] = jnp.where(sorted_kind == 1, act, jnp.zeros_like(act))
        for number in range(2):
            at = slice(number * half, (number + 1) * half)
            outer[number, :, span] = jnp.where(
                sorted_kind[at] == 2 * number, act[at], jnp.zeros_like(act[at])
            )

    def multiply(step):
        for load in loads[step]:
            load.wait()
        block = plane_device(*step)
        deep = pl.ds(pl.multiple_of(block * depth, depth), depth)

        def product(acts, group):
            total = None
            for which in range(3):
                act = acts[:, which * width : (which + 1) * width]
                term = dot(act, weights[which, group, deep, :], 1, 1)
                total = term if total is None else total + term
            return total

        both = product(middle, 1)
        for number in range(2):
            at = slice(number * half, (number + 1) * half)
            part = product(outer.at[number], 2 * number) + both[at]
            partial[block, at] = part.astype(jnp.bfloat16)

    def device(turn, da, db):
        return plane_device(da, db) if turn == 0 else plane_device(db, da)

    def second(turn, place):
        offset, number = OFFSETS[place], turn * len(OFFSETS) + place
        return RingSum(
            copies,
            ("b", number),
            lambda db: partial.at[device(turn, offset, db), pl.ds(turn * half, half)],
            lambda way: {"mod": device(turn, 0, way)},
            halves.at[number],
            fulls.at[number],
            sums.at[number],
        )

    def first(turn):
        number = 2 * len(OFFSETS) + turn
        return RingSum(
            copies,
            ("a", turn),
            lambda da: results.at[turn, OFFSETS.index(da)],
            lambda way: {"mod": device(turn, way, 0)},
            halves.at[number],
            fulls.at[number],
            sums.at[number],
        )

    rings = {
        (turn, OFFSETS[place]): second(turn, place) for place in range(4) for turn in range(2)
    }
    tops = [first(turn) for turn in range(2)]
    for number, step in enumerate(order):
        multiply(step)
        for turn in range(2):
            da, db = step if turn == 0 else (step[1], step[0])
            if db == 2:
                rings[turn, da].far()
            elif db != 0:
                rings[turn, da].early(db)
        if number == 6:
            lines[0][1]()
        if number == 10:
            for turn in range(2):
                rings[turn, 2].late()
            lines[1][1]()
        if number == 12:
            for turn in range(2):
                rings[turn, -1].late()
        if number == 14:
            for turn in range(2):
                rings[turn, 1].late()
    for turn in range(2):
        rings[turn, 0].late()
    lines[2][1]()

    for offset in OFFSETS:
        for turn in range(2):
            results[turn, OFFSETS.index(offset)] = rings[turn, offset].result()
            if offset == 2:
                tops[turn].far()
            elif offset != 0:
                tops[turn].early(offset)
        if offset == 2:
            lines[0][2]()
    for top in tops:
        top.late()
    lines[1][2]()
    total = None
    for turn, top in enumerate(tops):
        term = dot(sort[turn * half : (turn + 1) * half], top.result(), 0, 0)
        total = term if total is None else total + term
    out[...] = total.astype(out.dtype)
    lines[2][2]()
    for line in lines:
        line[3]()
    copies.finish()
    for own in own_act:
        own.wait()


def tail(table, act_query, act_key_value, sort, weights, count):
    rows, width = act_query.shape
    groups, tall, _ = weights[0].shape
    kind = act_query.dtype
    half, blocks = rows // 2, SIDE * SIDE
    depth = tall // blocks

    def buffer(*shape):
        return pltpu.VMEM((*shape, depth), kind)

    return pl.pallas_call(
        tail_kernel,
        out_shape=(
            jax.ShapeDtypeStruct((3, count, rows, width), kind),
            jax.ShapeDtypeStruct((rows, depth), kind),
        ),
        in_specs=[SMEM, WHOLE, WHOLE, WHOLE, ANY, ANY, ANY],
        out_specs=(ANY, WHOLE),
        scratch_shapes=[
            pltpu.VMEM((3, groups, tall, width), kind),
            pltpu.VMEM((3, rows, width), kind),
            pltpu.VMEM((rows, 3 * width), kind),
            pltpu.VMEM((2, half, 3 * width), kind),
            buffer(blocks, rows),
            buffer(10, 2, half // 2),
            buffer(10, 2, half),
            buffer(10, 2, half // 2),
            buffer(2, 4, half),
            *semaphores(96),
            pltpu.SemaphoreType.DMA((3,)),
            pltpu.SemaphoreType.DMA((3 * blocks,)),
        ],
        compiler_params=remote_params(3),
    )(table, act_query, act_key_value, sort, *weights)


def per_device(tokens, modality, doc_lengths, w_query, w_key, w_value, d_out):
    groups = w_query.shape[0]
    seq_count = lax.axis_size("seq")
    weights = (w_query, w_key, w_value)
    queries, sort_matrix, table, keys, values, pieces = front(
        tokens, modality, weights, seq_count
    )
    attn_out, act_query, act_key_value, token_columns = attention(
        doc_lengths, queries, keys, values, d_out, pieces
    )
    act_all, grad_tokens = tail(
        table, act_query, act_key_value, sort_matrix, weights, seq_count
    )
    grads = weight_grads(table, token_columns, act_all, groups)
    return (attn_out, grad_tokens, *grads)


def solution(mesh):
    placed = (
        P("seq", "mod"),
        P("seq", None),
        P(),
        P(None, None, "mod"),
        P(None, None, "mod"),
        P(None, None, "mod"),
        P("seq", "mod"),
    )
    return jax.shard_map(
        per_device,
        mesh=mesh,
        in_specs=placed,
        out_specs=(
            P("seq", "mod"),
            P("seq", "mod"),
            P(None, "seq", "mod"),
            P(None, "seq", "mod"),
            P(None, "seq", "mod"),
        ),
        check_vma=False,
    )
```

```python
import functools
import math

import jax
import jax.numpy as jnp
from jax import lax
from jax.experimental import pallas as pl
from jax.experimental.pallas import tpu as pltpu
from jax.sharding import PartitionSpec as P

HEAD_DIM = 128
WINDOW_PAD = 16
MAX_BACK = 5
VMEM_BYTES = 56 * 1024 * 1024


def dot(left, right, left_dim=1, right_dim=0):
    return lax.dot_general(
        left,
        right,
        (((left_dim,), (right_dim,)), ((), ())),
        preferred_element_type=jnp.float32,
    )


def params():
    return pltpu.CompilerParams(vmem_limit_bytes=VMEM_BYTES)


ANY = pl.BlockSpec(memory_space=pl.ANY)
SMEM = pl.BlockSpec(memory_space=pltpu.SMEM)
WHOLE = pl.BlockSpec(memory_space=pltpu.VMEM)


def weight_kernel(
    table, x_ref, act_ref, gq_ref, gk_ref, gv_ref, x_in, act_in, x_rows, x_turned, grads, sem
):
    count, rows, wide = x_rows.shape
    groups, _, depth = x_turned.shape
    window = depth // count
    loads = [pltpu.make_async_copy(x_ref, x_in, sem.at[0])]
    for which in range(3):
        loads.append(
            pltpu.make_async_copy(act_ref.at[which], act_in.at[which], sem.at[1 + which])
        )
    for load in loads:
        load.start()

    def bounds(block, group):
        low, high = table[block, 0, group], table[block, 0, group + 1]
        start = jnp.minimum((low // WINDOW_PAD) * WINDOW_PAD, rows - window)
        return low, high, pl.multiple_of(start, WINDOW_PAD)

    def chosen(block, group, start, size):
        low, high, _ = bounds(block, group)
        at = pl.ds(start, size)
        place = lax.broadcasted_iota(jnp.int32, (size, 1), 0) + start
        picked = x_rows[block, at, :]
        return jnp.where((place >= low) & (place < high), picked, jnp.zeros_like(picked))

    loads[0].wait()
    def turn(block, _):
        for part in range(x_in.shape[2]):
            cols = x_in.shape[4]
            x_rows[block, :, part * cols : (part + 1) * cols] = x_in[:, block, part].reshape(
                rows, cols
            )
        columns = pl.ds(pl.multiple_of(block * window, window), window)
        for group in range(groups):
            picked = chosen(block, group, bounds(block, group)[2], window)
            x_turned[group, :, columns] = picked.T
        return 0

    lax.fori_loop(0, count, turn, 0)
    stores = []
    for which, out in enumerate((gq_ref, gk_ref, gv_ref)):
        loads[1 + which].wait()
        def one(group, _):
            total = None
            for block in range(count):
                at = pl.ds(bounds(block, group)[2], window)
                term = dot(
                    x_turned[group, :, block * window : (block + 1) * window],
                    act_in[which, block, at, :],
                )
                total = term if total is None else total + term
            grads[which, group] = total

            def rest(block, _):
                low, high, start = bounds(block, group)

                @pl.when(high > start + window)
                def _():
                    at = pl.multiple_of(start + window, WINDOW_PAD)
                    picked = chosen(block, group, at, WINDOW_PAD)
                    act = act_in[which, block, pl.ds(at, WINDOW_PAD), :]
                    grads[which, group] += dot(picked, act, 0, 0)

                return 0

            lax.fori_loop(0, count, rest, 0)
            return 0

        lax.fori_loop(0, groups, one, 0)
        stores.append(pltpu.make_async_copy(grads.at[which], out, sem.at[4 + which]))
        stores[-1].start()
    for store in stores:
        store.wait()


def weight_grads(table, x, act, groups):
    pieces, count, parts, deep, cols = x.shape
    rows, wide = pieces * deep, parts * cols
    width = act.shape[3]
    out = jax.ShapeDtypeStruct((groups, wide, width), jnp.float32)
    return pl.pallas_call(
        weight_kernel,
        out_shape=(out, out, out),
        in_specs=[SMEM, ANY, ANY],
        out_specs=(ANY, ANY, ANY),
        scratch_shapes=[
            pltpu.VMEM(x.shape, x.dtype),
            pltpu.VMEM(act.shape, act.dtype),
            pltpu.VMEM((count, rows, wide), x.dtype),
            pltpu.VMEM((groups, wide, count * (rows // 2)), x.dtype),
            pltpu.VMEM((3, groups, wide, width), jnp.float32),
            pltpu.SemaphoreType.DMA((7,)),
        ],
        compiler_params=params(),
    )(table, x, act)


SIDE = 4
OFFSETS = (2, -1, 1, 0)


def greet(devices):
    barrier = pltpu.get_barrier_semaphore()
    for device in devices:
        pl.semaphore_signal(
            barrier, inc=1, device_id=device, device_id_type=pl.DeviceIdType.MESH
        )


def enter(devices):
    greet(devices)
    pl.semaphore_wait(pltpu.get_barrier_semaphore(), len(devices))


class Copies:
    def __init__(self, send_sem, recv_sem):
        self.send_sem, self.recv_sem = send_sem, recv_sem
        self.names = {}
        self.started = []

    def make(self, name, src, dst, device):
        number = self.names.setdefault(name, len(self.names))
        return pltpu.make_async_remote_copy(
            src_ref=src,
            dst_ref=dst,
            send_sem=self.send_sem.at[number],
            recv_sem=self.recv_sem.at[number],
            device_id=device,
            device_id_type=pl.DeviceIdType.MESH,
        )

    def send(self, name, src, dst, device):
        copy = self.make(name, src, dst, device)
        copy.start()
        self.started.append(copy)

    def receive(self, name, dst, device):
        self.make(name, dst, dst, device).wait_recv()

    def finish(self):
        for copy in self.started:
            copy.wait_send()


def plane_device(dx, dy):
    rank = lax.axis_index("mod")
    x, y = lax.rem(rank, SIDE), rank // SIDE
    return lax.rem(y + dy + SIDE, SIDE) * SIDE + lax.rem(x + dx + SIDE, SIDE)


def line_device(dz, other=False):
    rank = lax.axis_index("seq")
    z, core = rank // 2, lax.rem(rank, 2)
    return lax.rem(z + dz + SIDE, SIDE) * 2 + (1 - core if other else core)


def plane_neighbours():
    return [{"mod": plane_device(*step)} for step in ((1, 0), (-1, 0), (0, 1), (0, -1))]


def line_neighbours():
    return [{"seq": line_device(1)}, {"seq": line_device(-1)}, {"seq": line_device(0, True)}]


def plane_gather(copies, name, src, out):
    half = src.shape[0] // 2

    def part(turn, which):
        if which is None:
            return pl.ds(turn * half, half)
        return pl.ds(turn * half + which * (half // 2), half // 2)

    def device(turn, da, db):
        return plane_device(da, db) if turn == 0 else plane_device(db, da)

    def region(turn, da, db, which):
        return out.at[device(turn, da, db), part(turn, which)]

    def target(turn, axis, way):
        return {"mod": device(turn, way, 0) if axis == "a" else device(turn, 0, way)}

    def send(turn, axis, way, kind, offset):
        which = None if kind == "full" else (0 if way > 0 else 1)
        own = kind == "full" and offset == 0
        da = (0 if kind == "full" else -way) if axis == "a" else offset
        db = 0 if axis == "a" or kind == "full" else -way
        there = region(turn, da, db, which)
        here = src.at[part(turn, which)] if own else there
        copies.send((name, turn, axis, way, kind, offset), here, there, target(turn, axis, way))

    def receive(turn, axis, way, kind, offset):
        which = None if kind == "full" else (0 if way > 0 else 1)
        far = -way if kind == "full" else 2
        da, db = (far, 0) if axis == "a" else (offset, far)
        copies.receive(
            (name, turn, axis, way, kind, offset),
            region(turn, da, db, which),
            target(turn, axis, way),
        )

    ways, turns = (1, -1), (0, 1)

    def begin():
        for turn in turns:
            for way in ways:
                send(turn, "a", way, "full", 0)
        for turn in turns:
            for way in ways:
                send(turn, "b", way, "full", 0)

    def near():
        for way in ways:
            for turn in turns:
                receive(turn, "a", way, "full", 0)
                send(turn, "a", way, "half", 0)
                for second in ways:
                    send(turn, "b", second, "full", -way)

    def far():
        for turn in turns:
            for way in ways:
                receive(turn, "a", way, "half", 0)
            for second in ways:
                send(turn, "b", second, "full", 2)

    def fold(offset):
        for turn in turns:
            for way in ways:
                receive(turn, "b", way, "full", offset)
                send(turn, "b", way, "half", offset)

    def last(offset):
        for turn in turns:
            for way in ways:
                receive(turn, "b", way, "half", offset)

    return begin, near, far, fold, last


def line_gather(copies, name, src, out):
    half = src.shape[0] // 2

    def region(dz, other, which):
        rows = pl.ds(0, 2 * half) if which is None else pl.ds(which * half, half)
        return out.at[line_device(dz, other), rows]

    def along(way):
        return {"seq": line_device(way)}

    sibling = {"seq": line_device(0, True)}

    def pass_on(dz):
        copies.send((name, "sib", dz), region(dz, False, None), region(dz, False, None), sibling)

    def stage_0():
        for way in (1, -1):
            copies.send((name, way, "full"), src, region(0, False, None), along(way))
        copies.send((name, "sib", 0), src, region(0, False, None), sibling)

    def stage_1():
        for way in (1, -1):
            which = 0 if way > 0 else 1
            copies.receive((name, way, "full"), region(-way, False, None), along(way))
            there = region(-way, False, which)
            copies.send((name, way, "half"), there, there, along(way))
        for way in (1, -1):
            pass_on(-way)

    def stage_2():
        for way in (1, -1):
            which = 0 if way > 0 else 1
            copies.receive((name, way, "half"), region(2, False, which), along(way))
        pass_on(2)

    def last():
        for dz in (0, -1, 1, 2):
            copies.receive((name, "sib", dz), region(dz, True, None), sibling)

    return [stage_0, stage_1, stage_2, last]


def add(*terms):
    total = terms[0].astype(jnp.float32)
    for term in terms[1:]:
        total = total + term.astype(jnp.float32)
    return total.astype(jnp.bfloat16)


class RingSum:
    def __init__(self, copies, name, source, device, halves, fulls, sums, absent=()):
        self.absent = absent
        self.copies, self.name, self.source, self.device = copies, name, source, device
        self.halves, self.fulls, self.sums = halves, fulls, sums
        self.half = halves.shape[1]

    def rows(self, which):
        return pl.ds(which * self.half, self.half)

    def send(self, kind, way, src, dst):
        self.copies.send((self.name, kind, way), src, dst, self.device(way))

    def receive(self, kind, way, dst):
        self.copies.receive((self.name, kind, way), dst, self.device(way))

    def far(self):
        for number, way in enumerate((1, -1)):
            self.send("half", way, self.source(2).at[self.rows(number)], self.halves.at[number])

    def early(self, way):
        number = 0 if way > 0 else 1
        there = self.fulls.at[number, self.rows(1 - number)]
        self.send("early", way, self.source(way).at[self.rows(1 - number)], there)

    def late(self):
        for number, way in enumerate((1, -1)):
            self.receive("half", way, self.halves.at[number])
            there = self.fulls.at[number, self.rows(number)]
            if way in self.absent:
                self.send("late", way, self.halves.at[number], there)
                continue
            term = self.source(way)[self.rows(number)]
            self.sums[number] = add(term, self.halves[number])
            self.send("late", way, self.sums.at[number], there)

    def result(self):
        parts = [[self.source(0)[self.rows(number)]] for number in range(2)]
        for number, way in enumerate((1, -1)):
            if way not in self.absent:
                there = self.rows(1 - number)
                self.receive("early", way, self.fulls.at[number, there])
                parts[1 - number].append(self.fulls[number, there])
            there = self.rows(number)
            self.receive("late", way, self.fulls.at[number, there])
            parts[number].append(self.fulls[number, there])
        return jnp.concatenate([add(*terms) for terms in parts], 0)


def remote_params(number):
    return pltpu.CompilerParams(
        collective_id=number, has_side_effects=True, vmem_limit_bytes=VMEM_BYTES
    )


def semaphores(count):
    return [pltpu.SemaphoreType.DMA((count,)), pltpu.SemaphoreType.DMA((count,))]


def front_kernel(
    tokens,
    modality,
    wq_ref,
    wk_ref,
    wv_ref,
    q_out,
    sort_out,
    table_out,
    k_all,
    v_all,
    pieces,
    rows_all,
    weights,
    acc,
    kv_own,
    table,
    send_sem,
    recv_sem,
    own_sem,
):
    copies = Copies(send_sem, recv_sem)
    rows, depth = tokens.shape
    groups, width, half = weights.shape[1], q_out.shape[1], rows // 2
    count = pieces.shape[0]
    me, place = lax.axis_index("seq"), lax.axis_index("mod")
    others = [lax.rem(me + step, count) for step in range(1, count)]
    greeted = [{"seq": other} for other in others] + plane_neighbours()
    greet(greeted)
    loads = [
        pltpu.make_async_copy(weight, weights.at[which], own_sem.at[which])
        for which, weight in enumerate((wq_ref, wk_ref, wv_ref))
    ]
    for load in loads:
        load.start()

    kind = modality[...]
    counts = [jnp.sum((kind == group).astype(jnp.int32)) for group in range(groups)]
    firsts = [jnp.int32(0)]
    for group in range(groups):
        firsts.append(firsts[-1] + counts[group])
    lane = lax.broadcasted_iota(jnp.int32, table.shape, 1)
    table[...] = sum(jnp.where(lane > group, counts[group], 0) for group in range(groups))

    lanes = lax.broadcasted_iota(jnp.int32, (rows, 128), 1)
    one_hot = (lanes == kind).astype(jnp.bfloat16)
    down = lax.broadcasted_iota(jnp.int32, (rows, rows), 0)
    across = lax.broadcasted_iota(jnp.int32, (rows, rows), 1)
    first_lane = lax.broadcasted_iota(jnp.int32, (1, 128), 1)
    base = jnp.zeros((1, 128), jnp.float32)
    for group in range(groups):
        base = jnp.where(first_lane == group, firsts[group].astype(jnp.float32), base)
    before = dot((across < down).astype(jnp.bfloat16), one_hot) + base
    rank = jnp.sum(before * one_hot.astype(jnp.float32), 1, keepdims=True).astype(jnp.int32)
    unsort = (rank == across).astype(jnp.bfloat16)
    sort = unsort.T
    sort_out[...] = sort
    rows_all[place] = dot(sort, tokens[...]).astype(jnp.bfloat16)

    line = lax.broadcasted_iota(jnp.int32, (rows, 1), 0)
    sorted_kind = sum((line >= firsts[group]).astype(jnp.int32) for group in range(1, groups))

    def multiply(blocks, new, wanted=(0, 3)):
        def one(which, _):
            low = middle = high = None
            for step in blocks:
                block = plane_device(*step)
                deep = pl.ds(pl.multiple_of(block * depth, depth), depth)
                x = rows_all[block]
                terms = []
                for group, at in enumerate((slice(0, half), slice(0, rows), slice(half, rows))):
                    own = jnp.where(sorted_kind[at] == group, x[at], jnp.zeros_like(x[at]))
                    terms.append(dot(own, weights[which, group, deep, :]))
                low = terms[0] if low is None else low + terms[0]
                middle = terms[1] if middle is None else middle + terms[1]
                high = terms[2] if high is None else high + terms[2]
            for number, part in enumerate((low, high)):
                at = slice(number * half, (number + 1) * half)
                if new:
                    acc[which, at] = part + middle[at]
                else:
                    acc[which, at] += part + middle[at]
            return 0

        lax.fori_loop(*wanted, one, 0)

    def projected(which):
        return dot(unsort, acc[which].astype(jnp.bfloat16)).astype(jnp.bfloat16)

    pl.semaphore_wait(pltpu.get_barrier_semaphore(), len(greeted))
    for step, other in enumerate(others):
        copies.send(("table", step), table, table_out.at[me], {"seq": other})
    own_table = pltpu.make_async_copy(table, table_out.at[me], own_sem.at[3])
    own_table.start()
    begin, near, far, fold, last = plane_gather(
        copies, "rows", rows_all.at[place], rows_all
    )
    begin()
    near()
    fold(0)
    for load in loads:
        load.wait()
    multiply([(0, 0), (1, 0), (-1, 0), (0, 1), (0, -1)], True)
    far()
    last(0)
    fold(-1)
    multiply([(2, 0), (0, 2)], False)
    fold(1)
    fold(2)
    multiply([(1, 1), (1, -1), (-1, 1), (-1, -1)], False)
    last(-1)
    last(1)
    rest = [(1, 2), (-1, 2), (2, 1), (2, -1)]
    multiply(rest, False, (1, 3))
    last(2)

    deep = pieces.shape[2]

    def piece(target):
        return rows_all.at[
            pl.ds(2 * target, 2), pl.ds(pl.multiple_of(place * deep, deep), deep)
        ]

    own_piece = pltpu.make_async_copy(piece(me), pieces.at[me], own_sem.at[4])
    own_piece.start()
    for step, other in enumerate(others):
        copies.send(("piece", step), piece(other), pieces.at[me], {"seq": other})
    multiply([(2, 2)], False, (1, 3))
    kv_own[0] = projected(1)
    kv_own[1] = projected(2)
    own_keys = pltpu.make_async_copy(kv_own.at[0], k_all.at[me], own_sem.at[5])
    own_values = pltpu.make_async_copy(kv_own.at[1], v_all.at[me], own_sem.at[6])
    own_keys.start()
    own_values.start()
    keys = line_gather(copies, "keys", kv_own.at[0], k_all)
    values = line_gather(copies, "values", kv_own.at[1], v_all)
    keys[0]()
    values[0]()
    multiply([*rest, (2, 2)], False, (0, 1))
    q_out[...] = projected(0)
    for stage in (1, 2, 3):
        keys[stage]()
        values[stage]()
    for step in range(count - 1):
        sender = lax.rem(me + count - 1 - step, count)
        copies.receive(("table", step), table_out.at[sender], {"seq": others[step]})
        copies.receive(("piece", step), pieces.at[sender], {"seq": others[step]})
    copies.finish()
    for own in (own_table, own_keys, own_values, own_piece):
        own.wait()


def front(tokens, modality, weights, count):
    rows, depth = tokens.shape
    groups, tall, width = weights[0].shape
    blocks = SIDE * SIDE
    kind = tokens.dtype
    piece = (count, 2, rows // blocks, depth)
    half = jax.ShapeDtypeStruct((count, rows, width), kind)
    return pl.pallas_call(
        front_kernel,
        out_shape=(
            jax.ShapeDtypeStruct((rows, width), kind),
            jax.ShapeDtypeStruct((rows, rows), kind),
            jax.ShapeDtypeStruct((count, 8, 128), jnp.int32),
            half,
            half,
            jax.ShapeDtypeStruct(piece, kind),
        ),
        in_specs=[WHOLE, WHOLE, ANY, ANY, ANY],
        out_specs=(WHOLE,) * 6,
        scratch_shapes=[
            pltpu.VMEM((blocks, rows, depth), kind),
            pltpu.VMEM((3, groups, tall, width), kind),
            pltpu.VMEM((3, rows, width), jnp.float32),
            pltpu.VMEM((2, rows, width), kind),
            pltpu.VMEM((8, 128), jnp.int32),
            *semaphores(76),
            pltpu.SemaphoreType.DMA((7,)),
        ],
        compiler_params=remote_params(0),
    )(tokens, modality, *weights)


def attention_kernel(
    lengths,
    q_ref,
    k_ref,
    v_ref,
    do_ref,
    pieces,
    out_ref,
    dq_ref,
    dkv_ref,
    columns,
    scores,
    dq_sum,
    made,
    theirs,
    ours,
    halves,
    fulls,
    sums,
    send_sem,
    recv_sem,
    pair_send,
    pair_recv,
    own_sem,
):
    copies = Copies(send_sem, recv_sem)
    greeted = plane_neighbours() + line_neighbours()
    greet(greeted)
    rows, width = q_ref.shape
    heads = width // HEAD_DIM
    scale = 1.0 / math.sqrt(HEAD_DIM)
    me, place = lax.axis_index("seq"), lax.axis_index("mod")
    first = jnp.maximum(me - (MAX_BACK - 1), 0)
    own_columns = pltpu.make_async_copy(pieces, columns.at[place], own_sem)
    own_columns.start()
    ends = [lengths[0]]
    for number in range(1, lengths.shape[0]):
        ends.append(ends[-1] + lengths[number])

    def document(positions):
        return sum((positions >= end).astype(jnp.int32) for end in ends)

    own = lax.broadcasted_iota(jnp.int32, (rows, 1), 0) + me * rows
    own_document = document(own)
    cols = [slice(h * HEAD_DIM, (h + 1) * HEAD_DIM) for h in range(heads)]
    vcols = [slice(width + h * HEAD_DIM, width + (h + 1) * HEAD_DIM) for h in range(heads)]
    pl.semaphore_wait(pltpu.get_barrier_semaphore(), len(greeted))
    begin, near, far, fold, last = plane_gather(copies, "columns", pieces, columns)
    begin()

    def score_step(block, row_max):
        key_pos = lax.broadcasted_iota(jnp.int32, (1, rows), 1) + block * rows
        visible = (key_pos <= own) & (document(key_pos) == own_document)
        new = []
        for h in range(heads):
            part = dot(q_ref[:, cols[h]], k_ref[block, :, cols[h]], 1, 1) * scale
            part = jnp.where(visible, part, -jnp.inf)
            scores[h, block - first] = part
            new.append(jnp.maximum(row_max[h], jnp.max(part, 1, keepdims=True)))
        return tuple(new)

    start = tuple(jnp.full((rows, 1), -jnp.inf, jnp.float32) for _ in range(heads))
    row_max = lax.fori_loop(first, me + 1, score_step, start)
    near()
    fold(0)

    def value_step(block, carry):
        new = []
        for h in range(heads):
            total, summed = carry[h]
            weights = jnp.exp(scores[h, block - first] - row_max[h])
            scores[h, block - first] = weights
            total = total + jnp.sum(weights, 1, keepdims=True)
            summed = summed + dot(weights.astype(jnp.bfloat16), v_ref[block, :, cols[h]])
            new.append((total, summed))
        return tuple(new)

    start = tuple(
        (jnp.zeros((rows, 1), jnp.float32), jnp.zeros((rows, HEAD_DIM), jnp.float32))
        for _ in range(heads)
    )
    totals = lax.fori_loop(first, me + 1, value_step, start)
    inverse, row_dot = [], []
    for h in range(heads):
        total, summed = totals[h]
        attended = (summed / total).astype(jnp.bfloat16)
        out_ref[:, cols[h]] = attended
        inverse.append(1.0 / total)
        row_dot.append(
            jnp.sum(
                do_ref[:, cols[h]].astype(jnp.float32) * attended.astype(jnp.float32),
                1,
                keepdims=True,
            )
        )
    dq_sum[...] = jnp.zeros_like(dq_sum)
    far()
    last(0)

    def grads(block, result):
        seen = (block >= first) & (block <= me)

        @pl.when(seen)
        def _():
            for h in range(heads):
                spread = dot(do_ref[:, cols[h]], v_ref[block, :, cols[h]], 1, 1)
                chances = scores[h, block - first] * inverse[h]
                dscore = (chances * (spread - row_dot[h]) * scale).astype(jnp.bfloat16)
                dq_sum[:, cols[h]] += dot(dscore, k_ref[block, :, cols[h]])
                result[:, cols[h]] = dot(dscore, q_ref[:, cols[h]], 0, 0).astype(jnp.bfloat16)
                result[:, vcols[h]] = dot(
                    chances.astype(jnp.bfloat16), do_ref[:, cols[h]], 0, 0
                ).astype(jnp.bfloat16)

        @pl.when(jnp.logical_not(seen))
        def _():
            result[...] = jnp.zeros(result.shape, jnp.bfloat16)

    order = (2, -1, 0)

    def pair(number):
        return pltpu.make_async_remote_copy(
            src_ref=made.at[0, number],
            dst_ref=theirs.at[number],
            send_sem=pair_send.at[number],
            recv_sem=pair_recv.at[number],
            device_id={"seq": line_device(0, True)},
            device_id_type=pl.DeviceIdType.MESH,
        )

    def compute(number):
        def one(turn, _):
            chip = lax.rem(me // 2 + SIDE + order[number], SIDE)
            block = chip * 2 + lax.rem(lax.rem(me, 2) + 1 + turn, 2)
            grads(block, made.at[turn, number])

            @pl.when(turn == 0)
            def _():
                pair(number).start()

            return 0

        lax.fori_loop(0, 2, one, 0)

    def join(number):
        pair(number).wait_recv()
        ours[number] = add(made[1, number], theirs[number])

    ring = RingSum(
        copies,
        "ring",
        lambda offset: ours.at[order.index(offset)],
        lambda way: {"seq": line_device(way)},
        halves,
        fulls,
        sums,
        (1,),
    )
    compute(0)
    join(0)
    ring.far()
    fold(-1)
    compute(1)
    join(1)
    ring.early(-1)
    fold(1)
    compute(2)
    for h in range(heads):
        dq_ref[:, cols[h]] = dq_sum[:, cols[h]].astype(jnp.bfloat16)
    ring.late()
    fold(2)
    join(2)
    dkv_ref[...] = ring.result()
    for offset in (-1, 1, 2):
        last(offset)
    copies.finish()
    for number in range(3):
        pair(number).wait_send()
    own_columns.wait()


def attention(lengths, q, k, v, do, pieces):
    rows, width = q.shape
    kind = q.dtype
    shape = jax.ShapeDtypeStruct((rows, width), kind)

    def buffer(count, tall):
        return pltpu.VMEM((count, tall, 2 * width), kind)

    return pl.pallas_call(
        attention_kernel,
        out_shape=(
            shape,
            shape,
            jax.ShapeDtypeStruct((rows, 2 * width), kind),
            jax.ShapeDtypeStruct((SIDE * SIDE, *pieces.shape), kind),
        ),
        in_specs=[SMEM] + [WHOLE] * 5,
        out_specs=(WHOLE,) * 4,
        scratch_shapes=[
            pltpu.VMEM((width // HEAD_DIM, MAX_BACK, rows, rows), jnp.float32),
            pltpu.VMEM((rows, width), jnp.float32),
            pltpu.VMEM((2, 3, rows, 2 * width), kind),
            buffer(3, rows),
            buffer(3, rows),
            buffer(2, rows // 2),
            buffer(2, rows),
            buffer(2, rows // 2),
            *semaphores(52),
            *semaphores(3),
            pltpu.SemaphoreType.DMA,
        ],
        compiler_params=remote_params(1),
    )(lengths, q, k, v, do, pieces)


def tail_kernel(
    table,
    act_query,
    act_key_value,
    sort,
    wq_ref,
    wk_ref,
    wv_ref,
    act_all,
    out,
    weights,
    act_own,
    middle,
    outer,
    partial,
    halves,
    fulls,
    sums,
    results,
    send_sem,
    recv_sem,
    own_sem,
    load_sem,
):
    copies = Copies(send_sem, recv_sem)
    greeted = plane_neighbours() + line_neighbours()
    greet(greeted)
    _, groups, _, depth = weights.shape
    rows = sort.shape[0]
    me = lax.axis_index("seq")
    half = rows // 2
    order = [(2, 2), (1, 2), (-1, 2), (2, 1), (2, -1), (0, 2), (2, 0)]
    order += [(1, 1), (1, -1), (-1, 1), (-1, -1)]
    order += [(0, 1), (0, -1), (1, 0), (-1, 0), (0, 0)]
    loads = {}
    for number, step in enumerate(order):
        at = pl.ds(pl.multiple_of(plane_device(*step) * depth, depth), depth)
        loads[step] = [
            pltpu.make_async_copy(
                weight.at[:, at], weights.at[which, :, at], load_sem.at[3 * number + which]
            )
            for which, weight in enumerate((wq_ref, wk_ref, wv_ref))
        ]
        for load in loads[step]:
            load.start()

    width = act_query.shape[1]
    acts = (act_query[...], act_key_value[:, :width], act_key_value[:, width:])
    for which, act in enumerate(acts):
        act_own[which] = dot(sort[...], act).astype(jnp.bfloat16)
    own_act = [
        pltpu.make_async_copy(act_own.at[which], act_all.at[which, me], own_sem.at[which])
        for which in range(3)
    ]
    for own in own_act:
        own.start()
    pl.semaphore_wait(pltpu.get_barrier_semaphore(), len(greeted))
    lines = [
        line_gather(copies, ("act", which), act_own.at[which], act_all.at[which])
        for which in range(3)
    ]
    for line in lines:
        line[0]()

    place = lax.broadcasted_iota(jnp.int32, (rows, 1), 0)
    sorted_kind = sum(
        (place >= table[me, 0, group]).astype(jnp.int32) for group in range(1, groups)
    )
    for which in range(3):
        act = act_own[which]
        span = slice(which * width, (which + 1) * width)
        middle[:, span] = jnp.where(sorted_kind == 1, act, jnp.zeros_like(act))
        for number in range(2):
            at = slice(number * half, (number + 1) * half)
            outer[number, :, span] = jnp.where(
                sorted_kind[at] == 2 * number, act[at], jnp.zeros_like(act[at])
            )

    def multiply(step):
        for load in loads[step]:
            load.wait()
        block = plane_device(*step)
        deep = pl.ds(pl.multiple_of(block * depth, depth), depth)

        def product(acts, group):
            total = None
            for which in range(3):
                act = acts[:, which * width : (which + 1) * width]
                term = dot(act, weights[which, group, deep, :], 1, 1)
                total = term if total is None else total + term
            return total

        both = product(middle, 1)
        for number in range(2):
            at = slice(number * half, (number + 1) * half)
            part = product(outer.at[number], 2 * number) + both[at]
            partial[block, at] = part.astype(jnp.bfloat16)

    def device(turn, da, db):
        return plane_device(da, db) if turn == 0 else plane_device(db, da)

    def second(turn, place):
        offset, number = OFFSETS[place], turn * len(OFFSETS) + place
        return RingSum(
            copies,
            ("b", number),
            lambda db: partial.at[device(turn, offset, db), pl.ds(turn * half, half)],
            lambda way: {"mod": device(turn, 0, way)},
            halves.at[number],
            fulls.at[number],
            sums.at[number],
        )

    def first(turn):
        number = 2 * len(OFFSETS) + turn
        return RingSum(
            copies,
            ("a", turn),
            lambda da: results.at[turn, OFFSETS.index(da)],
            lambda way: {"mod": device(turn, way, 0)},
            halves.at[number],
            fulls.at[number],
            sums.at[number],
        )

    rings = {
        (turn, OFFSETS[place]): second(turn, place) for place in range(4) for turn in range(2)
    }
    tops = [first(turn) for turn in range(2)]
    for number, step in enumerate(order):
        multiply(step)
        for turn in range(2):
            da, db = step if turn == 0 else (step[1], step[0])
            if db == 2:
                rings[turn, da].far()
            elif db != 0:
                rings[turn, da].early(db)
        if number == 6:
            lines[0][1]()
        if number == 10:
            for turn in range(2):
                rings[turn, 2].late()
            lines[1][1]()
        if number == 12:
            for turn in range(2):
                rings[turn, -1].late()
        if number == 14:
            for turn in range(2):
                rings[turn, 1].late()
    for turn in range(2):
        rings[turn, 0].late()
    lines[2][1]()

    for offset in OFFSETS:
        for turn in range(2):
            results[turn, OFFSETS.index(offset)] = rings[turn, offset].result()
            if offset == 2:
                tops[turn].far()
            elif offset != 0:
                tops[turn].early(offset)
        if offset == 2:
            lines[0][2]()
    for top in tops:
        top.late()
    lines[1][2]()
    total = None
    for turn, top in enumerate(tops):
        term = dot(sort[turn * half : (turn + 1) * half], top.result(), 0, 0)
        total = term if total is None else total + term
    out[...] = total.astype(out.dtype)
    lines[2][2]()
    for line in lines:
        line[3]()
    copies.finish()
    for own in own_act:
        own.wait()


def tail(table, act_query, act_key_value, sort, weights, count):
    rows, width = act_query.shape
    groups, tall, _ = weights[0].shape
    kind = act_query.dtype
    half, blocks = rows // 2, SIDE * SIDE
    depth = tall // blocks

    def buffer(*shape):
        return pltpu.VMEM((*shape, depth), kind)

    return pl.pallas_call(
        tail_kernel,
        out_shape=(
            jax.ShapeDtypeStruct((3, count, rows, width), kind),
            jax.ShapeDtypeStruct((rows, depth), kind),
        ),
        in_specs=[SMEM, WHOLE, WHOLE, WHOLE, ANY, ANY, ANY],
        out_specs=(WHOLE, WHOLE),
        scratch_shapes=[
            pltpu.VMEM((3, groups, tall, width), kind),
            pltpu.VMEM((3, rows, width), kind),
            pltpu.VMEM((rows, 3 * width), kind),
            pltpu.VMEM((2, half, 3 * width), kind),
            buffer(blocks, rows),
            buffer(10, 2, half // 2),
            buffer(10, 2, half),
            buffer(10, 2, half // 2),
            buffer(2, 4, half),
            *semaphores(96),
            pltpu.SemaphoreType.DMA((3,)),
            pltpu.SemaphoreType.DMA((3 * blocks,)),
        ],
        compiler_params=remote_params(3),
    )(table, act_query, act_key_value, sort, *weights)


def per_device(tokens, modality, doc_lengths, w_query, w_key, w_value, d_out):
    groups = w_query.shape[0]
    seq_count = lax.axis_size("seq")
    weights = (w_query, w_key, w_value)
    queries, sort_matrix, table, keys, values, pieces = front(
        tokens, modality, weights, seq_count
    )
    attn_out, act_query, act_key_value, token_columns = attention(
        doc_lengths, queries, keys, values, d_out, pieces
    )
    act_all, grad_tokens = tail(
        table, act_query, act_key_value, sort_matrix, weights, seq_count
    )
    grads = weight_grads(table, token_columns, act_all, groups)
    return (attn_out, grad_tokens, *grads)


def solution(mesh):
    placed = (
        P("seq", "mod"),
        P("seq", None),
        P(),
        P(None, None, "mod"),
        P(None, None, "mod"),
        P(None, None, "mod"),
        P("seq", "mod"),
    )
    return jax.shard_map(
        per_device,
        mesh=mesh,
        in_specs=placed,
        out_specs=(
            P("seq", "mod"),
            P("seq", "mod"),
            P(None, "seq", "mod"),
            P(None, "seq", "mod"),
            P(None, "seq", "mod"),
        ),
        check_vma=False,
    )
```

```python
import functools
import math

import jax
import jax.numpy as jnp
from jax import lax
from jax.experimental import pallas as pl
from jax.experimental.pallas import tpu as pltpu
from jax.sharding import PartitionSpec as P

HEAD_DIM = 128
WINDOW_PAD = 16
MAX_BACK = 5
VMEM_BYTES = 56 * 1024 * 1024


def dot(left, right, left_dim=1, right_dim=0):
    return lax.dot_general(
        left,
        right,
        (((left_dim,), (right_dim,)), ((), ())),
        preferred_element_type=jnp.float32,
    )


def params():
    return pltpu.CompilerParams(vmem_limit_bytes=VMEM_BYTES)


ANY = pl.BlockSpec(memory_space=pl.ANY)
SMEM = pl.BlockSpec(memory_space=pltpu.SMEM)
WHOLE = pl.BlockSpec(memory_space=pltpu.VMEM)


def weight_kernel(
    table, x_ref, act_ref, gq_ref, gk_ref, gv_ref, x_in, act_in, x_rows, x_turned, grads, sem
):
    count, rows, wide = x_rows.shape
    groups, _, depth = x_turned.shape
    window = depth // count
    loads = [pltpu.make_async_copy(x_ref, x_in, sem.at[0])]
    for which in range(3):
        loads.append(
            pltpu.make_async_copy(act_ref.at[which], act_in.at[which], sem.at[1 + which])
        )
    for load in loads:
        load.start()

    def bounds(block, group):
        low, high = table[block, 0, group], table[block, 0, group + 1]
        start = jnp.minimum((low // WINDOW_PAD) * WINDOW_PAD, rows - window)
        return low, high, pl.multiple_of(start, WINDOW_PAD)

    def chosen(block, group, start, size):
        low, high, _ = bounds(block, group)
        at = pl.ds(start, size)
        place = lax.broadcasted_iota(jnp.int32, (size, 1), 0) + start
        picked = x_rows[block, at, :]
        return jnp.where((place >= low) & (place < high), picked, jnp.zeros_like(picked))

    loads[0].wait()
    def turn(block, _):
        for part in range(x_in.shape[2]):
            cols = x_in.shape[4]
            x_rows[block, :, part * cols : (part + 1) * cols] = x_in[:, block, part].reshape(
                rows, cols
            )
        columns = pl.ds(pl.multiple_of(block * window, window), window)
        for group in range(groups):
            picked = chosen(block, group, bounds(block, group)[2], window)
            x_turned[group, :, columns] = picked.T
        return 0

    lax.fori_loop(0, count, turn, 0)
    stores = []
    for which, out in enumerate((gq_ref, gk_ref, gv_ref)):
        loads[1 + which].wait()
        def one(group, _):
            total = None
            for block in range(count):
                at = pl.ds(bounds(block, group)[2], window)
                term = dot(
                    x_turned[group, :, block * window : (block + 1) * window],
                    act_in[which, block, at, :],
                )
                total = term if total is None else total + term
            grads[which, group] = total

            def rest(block, _):
                low, high, start = bounds(block, group)

                @pl.when(high > start + window)
                def _():
                    at = pl.multiple_of(start + window, WINDOW_PAD)
                    picked = chosen(block, group, at, WINDOW_PAD)
                    act = act_in[which, block, pl.ds(at, WINDOW_PAD), :]
                    grads[which, group] += dot(picked, act, 0, 0)

                return 0

            lax.fori_loop(0, count, rest, 0)
            return 0

        lax.fori_loop(0, groups, one, 0)
        stores.append(pltpu.make_async_copy(grads.at[which], out, sem.at[4 + which]))
        stores[-1].start()
    for store in stores:
        store.wait()


def weight_grads(table, x, act, groups):
    pieces, count, parts, deep, cols = x.shape
    rows, wide = pieces * deep, parts * cols
    width = act.shape[3]
    out = jax.ShapeDtypeStruct((groups, wide, width), jnp.float32)
    return pl.pallas_call(
        weight_kernel,
        out_shape=(out, out, out),
        in_specs=[SMEM, ANY, ANY],
        out_specs=(ANY, ANY, ANY),
        scratch_shapes=[
            pltpu.VMEM(x.shape, x.dtype),
            pltpu.VMEM(act.shape, act.dtype),
            pltpu.VMEM((count, rows, wide), x.dtype),
            pltpu.VMEM((groups, wide, count * (rows // 2)), x.dtype),
            pltpu.VMEM((3, groups, wide, width), jnp.float32),
            pltpu.SemaphoreType.DMA((7,)),
        ],
        compiler_params=params(),
    )(table, x, act)


SIDE = 4
OFFSETS = (2, -1, 1, 0)


def greet(devices):
    barrier = pltpu.get_barrier_semaphore()
    for device in devices:
        pl.semaphore_signal(
            barrier, inc=1, device_id=device, device_id_type=pl.DeviceIdType.MESH
        )


def enter(devices):
    greet(devices)
    pl.semaphore_wait(pltpu.get_barrier_semaphore(), len(devices))


class Copies:
    def __init__(self, send_sem, recv_sem):
        self.send_sem, self.recv_sem = send_sem, recv_sem
        self.names = {}
        self.started = []

    def make(self, name, src, dst, device):
        number = self.names.setdefault(name, len(self.names))
        return pltpu.make_async_remote_copy(
            src_ref=src,
            dst_ref=dst,
            send_sem=self.send_sem.at[number],
            recv_sem=self.recv_sem.at[number],
            device_id=device,
            device_id_type=pl.DeviceIdType.MESH,
        )

    def send(self, name, src, dst, device):
        copy = self.make(name, src, dst, device)
        copy.start()
        self.started.append(copy)

    def receive(self, name, dst, device):
        self.make(name, dst, dst, device).wait_recv()

    def finish(self):
        for copy in self.started:
            copy.wait_send()


def plane_device(dx, dy):
    rank = lax.axis_index("mod")
    x, y = lax.rem(rank, SIDE), rank // SIDE
    return lax.rem(y + dy + SIDE, SIDE) * SIDE + lax.rem(x + dx + SIDE, SIDE)


def line_device(dz, other=False):
    rank = lax.axis_index("seq")
    z, core = rank // 2, lax.rem(rank, 2)
    return lax.rem(z + dz + SIDE, SIDE) * 2 + (1 - core if other else core)


def plane_neighbours():
    return [{"mod": plane_device(*step)} for step in ((1, 0), (-1, 0), (0, 1), (0, -1))]


def line_neighbours():
    return [{"seq": line_device(1)}, {"seq": line_device(-1)}, {"seq": line_device(0, True)}]


def plane_gather(copies, name, src, out):
    half = src.shape[0] // 2

    def part(turn, which):
        if which is None:
            return pl.ds(turn * half, half)
        return pl.ds(turn * half + which * (half // 2), half // 2)

    def device(turn, da, db):
        return plane_device(da, db) if turn == 0 else plane_device(db, da)

    def region(turn, da, db, which):
        return out.at[device(turn, da, db), part(turn, which)]

    def target(turn, axis, way):
        return {"mod": device(turn, way, 0) if axis == "a" else device(turn, 0, way)}

    def send(turn, axis, way, kind, offset):
        which = None if kind == "full" else (0 if way > 0 else 1)
        own = kind == "full" and offset == 0
        da = (0 if kind == "full" else -way) if axis == "a" else offset
        db = 0 if axis == "a" or kind == "full" else -way
        there = region(turn, da, db, which)
        here = src.at[part(turn, which)] if own else there
        copies.send((name, turn, axis, way, kind, offset), here, there, target(turn, axis, way))

    def receive(turn, axis, way, kind, offset):
        which = None if kind == "full" else (0 if way > 0 else 1)
        far = -way if kind == "full" else 2
        da, db = (far, 0) if axis == "a" else (offset, far)
        copies.receive(
            (name, turn, axis, way, kind, offset),
            region(turn, da, db, which),
            target(turn, axis, way),
        )

    ways, turns = (1, -1), (0, 1)

    def begin():
        for turn in turns:
            for way in ways:
                send(turn, "a", way, "full", 0)
        for turn in turns:
            for way in ways:
                send(turn, "b", way, "full", 0)

    def near():
        for way in ways:
            for turn in turns:
                receive(turn, "a", way, "full", 0)
                send(turn, "a", way, "half", 0)
                for second in ways:
                    send(turn, "b", second, "full", -way)

    def far():
        for turn in turns:
            for way in ways:
                receive(turn, "a", way, "half", 0)
            for second in ways:
                send(turn, "b", second, "full", 2)

    def fold(offset):
        for turn in turns:
            for way in ways:
                receive(turn, "b", way, "full", offset)
                send(turn, "b", way, "half", offset)

    def last(offset):
        for turn in turns:
            for way in ways:
                receive(turn, "b", way, "half", offset)

    return begin, near, far, fold, last


def line_gather(copies, name, src, out):
    half = src.shape[0] // 2

    def region(dz, other, which):
        rows = pl.ds(0, 2 * half) if which is None else pl.ds(which * half, half)
        return out.at[line_device(dz, other), rows]

    def along(way):
        return {"seq": line_device(way)}

    sibling = {"seq": line_device(0, True)}

    def pass_on(dz):
        copies.send((name, "sib", dz), region(dz, False, None), region(dz, False, None), sibling)

    def stage_0():
        for way in (1, -1):
            copies.send((name, way, "full"), src, region(0, False, None), along(way))

    def stage_1():
        for way in (1, -1):
            which = 0 if way > 0 else 1
            copies.receive((name, way, "full"), region(-way, False, None), along(way))
            there = region(-way, False, which)
            copies.send((name, way, "half"), there, there, along(way))
        copies.send((name, "sib", 0), src, region(0, False, None), sibling)
        for way in (1, -1):
            pass_on(-way)

    def stage_2():
        for way in (1, -1):
            which = 0 if way > 0 else 1
            copies.receive((name, way, "half"), region(2, False, which), along(way))
        pass_on(2)

    def last():
        for dz in (0, -1, 1, 2):
            copies.receive((name, "sib", dz), region(dz, True, None), sibling)

    return [stage_0, stage_1, stage_2, last]


def add(*terms):
    total = terms[0].astype(jnp.float32)
    for term in terms[1:]:
        total = total + term.astype(jnp.float32)
    return total.astype(jnp.bfloat16)


class RingSum:
    def __init__(self, copies, name, source, device, halves, fulls, sums, absent=()):
        self.absent = absent
        self.copies, self.name, self.source, self.device = copies, name, source, device
        self.halves, self.fulls, self.sums = halves, fulls, sums
        self.half = halves.shape[1]

    def rows(self, which):
        return pl.ds(which * self.half, self.half)

    def send(self, kind, way, src, dst):
        self.copies.send((self.name, kind, way), src, dst, self.device(way))

    def receive(self, kind, way, dst):
        self.copies.receive((self.name, kind, way), dst, self.device(way))

    def far(self):
        for number, way in enumerate((1, -1)):
            self.send("half", way, self.source(2).at[self.rows(number)], self.halves.at[number])

    def early(self, way):
        number = 0 if way > 0 else 1
        there = self.fulls.at[number, self.rows(1 - number)]
        self.send("early", way, self.source(way).at[self.rows(1 - number)], there)

    def late(self):
        for number, way in enumerate((1, -1)):
            self.receive("half", way, self.halves.at[number])
            there = self.fulls.at[number, self.rows(number)]
            if way in self.absent:
                self.send("late", way, self.halves.at[number], there)
                continue
            term = self.source(way)[self.rows(number)]
            self.sums[number] = add(term, self.halves[number])
            self.send("late", way, self.sums.at[number], there)

    def result(self):
        parts = [[self.source(0)[self.rows(number)]] for number in range(2)]
        for number, way in enumerate((1, -1)):
            if way not in self.absent:
                there = self.rows(1 - number)
                self.receive("early", way, self.fulls.at[number, there])
                parts[1 - number].append(self.fulls[number, there])
            there = self.rows(number)
            self.receive("late", way, self.fulls.at[number, there])
            parts[number].append(self.fulls[number, there])
        return jnp.concatenate([add(*terms) for terms in parts], 0)


def remote_params(number):
    return pltpu.CompilerParams(
        collective_id=number, has_side_effects=True, vmem_limit_bytes=VMEM_BYTES
    )


def semaphores(count):
    return [pltpu.SemaphoreType.DMA((count,)), pltpu.SemaphoreType.DMA((count,))]


def front_kernel(
    tokens,
    modality,
    wq_ref,
    wk_ref,
    wv_ref,
    q_out,
    sort_out,
    table_out,
    k_all,
    v_all,
    columns,
    rows_all,
    weights,
    pieces,
    acc,
    kv_own,
    table,
    send_sem,
    recv_sem,
    own_sem,
):
    copies = Copies(send_sem, recv_sem)
    rows, depth = tokens.shape
    groups, width, half = weights.shape[1], q_out.shape[1], rows // 2
    count = pieces.shape[0]
    me, place = lax.axis_index("seq"), lax.axis_index("mod")
    others = [lax.rem(me + step, count) for step in range(1, count)]
    greeted = [{"seq": other} for other in others] + plane_neighbours()
    greet(greeted)
    loads = [
        pltpu.make_async_copy(weight, weights.at[which], own_sem.at[which])
        for which, weight in enumerate((wq_ref, wk_ref, wv_ref))
    ]
    for load in loads:
        load.start()

    kind = modality[...]
    counts = [jnp.sum((kind == group).astype(jnp.int32)) for group in range(groups)]
    firsts = [jnp.int32(0)]
    for group in range(groups):
        firsts.append(firsts[-1] + counts[group])
    lane = lax.broadcasted_iota(jnp.int32, table.shape, 1)
    table[...] = sum(jnp.where(lane > group, counts[group], 0) for group in range(groups))

    lanes = lax.broadcasted_iota(jnp.int32, (rows, 128), 1)
    one_hot = (lanes == kind).astype(jnp.bfloat16)
    down = lax.broadcasted_iota(jnp.int32, (rows, rows), 0)
    across = lax.broadcasted_iota(jnp.int32, (rows, rows), 1)
    first_lane = lax.broadcasted_iota(jnp.int32, (1, 128), 1)
    base = jnp.zeros((1, 128), jnp.float32)
    for group in range(groups):
        base = jnp.where(first_lane == group, firsts[group].astype(jnp.float32), base)
    before = dot((across < down).astype(jnp.bfloat16), one_hot) + base
    rank = jnp.sum(before * one_hot.astype(jnp.float32), 1, keepdims=True).astype(jnp.int32)
    unsort = (rank == across).astype(jnp.bfloat16)
    sort = unsort.T
    sort_out[...] = sort
    rows_all[place] = dot(sort, tokens[...]).astype(jnp.bfloat16)

    line = lax.broadcasted_iota(jnp.int32, (rows, 1), 0)
    sorted_kind = sum((line >= firsts[group]).astype(jnp.int32) for group in range(1, groups))

    def multiply(blocks, new, wanted=(0, 3)):
        def one(which, _):
            low = middle = high = None
            for step in blocks:
                block = plane_device(*step)
                deep = pl.ds(pl.multiple_of(block * depth, depth), depth)
                x = rows_all[block]
                terms = []
                for group, at in enumerate((slice(0, half), slice(0, rows), slice(half, rows))):
                    own = jnp.where(sorted_kind[at] == group, x[at], jnp.zeros_like(x[at]))
                    terms.append(dot(own, weights[which, group, deep, :]))
                low = terms[0] if low is None else low + terms[0]
                middle = terms[1] if middle is None else middle + terms[1]
                high = terms[2] if high is None else high + terms[2]
            for number, part in enumerate((low, high)):
                at = slice(number * half, (number + 1) * half)
                if new:
                    acc[which, at] = part + middle[at]
                else:
                    acc[which, at] += part + middle[at]
            return 0

        lax.fori_loop(*wanted, one, 0)

    def projected(which):
        return dot(unsort, acc[which].astype(jnp.bfloat16)).astype(jnp.bfloat16)

    pl.semaphore_wait(pltpu.get_barrier_semaphore(), len(greeted))
    for step, other in enumerate(others):
        copies.send(("table", step), table, table_out.at[me], {"seq": other})
    own_table = pltpu.make_async_copy(table, table_out.at[me], own_sem.at[3])
    own_table.start()
    begin, near, far, fold, last = plane_gather(
        copies, "rows", rows_all.at[place], rows_all
    )
    begin()
    near()
    fold(0)
    for load in loads:
        load.wait()
    multiply([(0, 0), (1, 0), (-1, 0), (0, 1), (0, -1)], True)
    far()
    last(0)
    fold(-1)
    multiply([(2, 0), (0, 2)], False)
    fold(1)
    fold(2)
    multiply([(1, 1), (1, -1), (-1, 1), (-1, -1)], False)
    last(-1)
    last(1)
    rest = [(1, 2), (-1, 2), (2, 1), (2, -1)]
    multiply(rest, False, (1, 3))
    last(2)

    deep = pieces.shape[2]

    def piece(target):
        return rows_all.at[
            pl.ds(2 * target, 2), pl.ds(pl.multiple_of(place * deep, deep), deep)
        ]

    own_piece = pltpu.make_async_copy(piece(me), pieces.at[me], own_sem.at[4])
    own_piece.start()
    for step, other in enumerate(others):
        copies.send(("piece", step), piece(other), pieces.at[me], {"seq": other})
    multiply([(2, 2)], False, (1, 3))
    kv_own[0] = projected(1)
    kv_own[1] = projected(2)
    own_keys = pltpu.make_async_copy(kv_own.at[0], k_all.at[me], own_sem.at[5])
    own_values = pltpu.make_async_copy(kv_own.at[1], v_all.at[me], own_sem.at[6])
    own_keys.start()
    own_values.start()
    keys = line_gather(copies, "keys", kv_own.at[0], k_all)
    values = line_gather(copies, "values", kv_own.at[1], v_all)
    keys[0]()
    for step in range(count - 1):
        sender = lax.rem(me + count - 1 - step, count)
        copies.receive(("piece", step), pieces.at[sender], {"seq": others[step]})
    own_piece.wait()
    own_columns = pltpu.make_async_copy(pieces, columns.at[place], own_sem.at[7])
    own_columns.start()
    begin, near, far, fold, last = plane_gather(copies, "columns", pieces, columns)
    begin()
    values[0]()
    multiply([*rest, (2, 2)], False, (0, 1))
    near()
    fold(0)
    keys[1]()
    far()
    last(0)
    q_out[...] = projected(0)
    fold(-1)
    values[1]()
    fold(1)
    keys[2]()
    fold(2)
    values[2]()
    for offset in (-1, 1, 2):
        last(offset)
    keys[3]()
    values[3]()
    for step in range(count - 1):
        sender = lax.rem(me + count - 1 - step, count)
        copies.receive(("table", step), table_out.at[sender], {"seq": others[step]})
    copies.finish()
    for own in (own_table, own_keys, own_values, own_columns):
        own.wait()


def front(tokens, modality, weights, count):
    rows, depth = tokens.shape
    groups, tall, width = weights[0].shape
    blocks = SIDE * SIDE
    kind = tokens.dtype
    piece = (count, 2, rows // blocks, depth)
    half = jax.ShapeDtypeStruct((count, rows, width), kind)
    return pl.pallas_call(
        front_kernel,
        out_shape=(
            jax.ShapeDtypeStruct((rows, width), kind),
            jax.ShapeDtypeStruct((rows, rows), kind),
            jax.ShapeDtypeStruct((count, 8, 128), jnp.int32),
            half,
            half,
            jax.ShapeDtypeStruct((blocks, *piece), kind),
        ),
        in_specs=[WHOLE, WHOLE, ANY, ANY, ANY],
        out_specs=(WHOLE, WHOLE, WHOLE, ANY, ANY, ANY),
        scratch_shapes=[
            pltpu.VMEM((blocks, rows, depth), kind),
            pltpu.VMEM((3, groups, tall, width), kind),
            pltpu.VMEM(piece, kind),
            pltpu.VMEM((3, rows, width), jnp.float32),
            pltpu.VMEM((2, rows, width), kind),
            pltpu.VMEM((8, 128), jnp.int32),
            *semaphores(116),
            pltpu.SemaphoreType.DMA((8,)),
        ],
        compiler_params=remote_params(0),
    )(tokens, modality, *weights)


def attention_kernel(
    lengths,
    q_ref,
    k_ref,
    v_ref,
    do_ref,
    out_ref,
    dq_ref,
    dkv_ref,
    scores,
    dq_sum,
    made,
    theirs,
    ours,
    halves,
    fulls,
    sums,
    send_sem,
    recv_sem,
    pair_send,
    pair_recv,
):
    copies = Copies(send_sem, recv_sem)
    greeted = line_neighbours()
    greet(greeted)
    rows, width = q_ref.shape
    heads = width // HEAD_DIM
    scale = 1.0 / math.sqrt(HEAD_DIM)
    me = lax.axis_index("seq")
    first = jnp.maximum(me - (MAX_BACK - 1), 0)
    ends = [lengths[0]]
    for number in range(1, lengths.shape[0]):
        ends.append(ends[-1] + lengths[number])

    def document(positions):
        return sum((positions >= end).astype(jnp.int32) for end in ends)

    own = lax.broadcasted_iota(jnp.int32, (rows, 1), 0) + me * rows
    own_document = document(own)
    cols = [slice(h * HEAD_DIM, (h + 1) * HEAD_DIM) for h in range(heads)]
    vcols = [slice(width + h * HEAD_DIM, width + (h + 1) * HEAD_DIM) for h in range(heads)]

    def score_step(block, row_max):
        key_pos = lax.broadcasted_iota(jnp.int32, (1, rows), 1) + block * rows
        visible = (key_pos <= own) & (document(key_pos) == own_document)
        new = []
        for h in range(heads):
            part = dot(q_ref[:, cols[h]], k_ref[block, :, cols[h]], 1, 1) * scale
            part = jnp.where(visible, part, -jnp.inf)
            scores[h, block - first] = part
            new.append(jnp.maximum(row_max[h], jnp.max(part, 1, keepdims=True)))
        return tuple(new)

    start = tuple(jnp.full((rows, 1), -jnp.inf, jnp.float32) for _ in range(heads))
    row_max = lax.fori_loop(first, me + 1, score_step, start)

    def value_step(block, carry):
        new = []
        for h in range(heads):
            total, summed = carry[h]
            weights = jnp.exp(scores[h, block - first] - row_max[h])
            scores[h, block - first] = weights
            total = total + jnp.sum(weights, 1, keepdims=True)
            summed = summed + dot(weights.astype(jnp.bfloat16), v_ref[block, :, cols[h]])
            new.append((total, summed))
        return tuple(new)

    start = tuple(
        (jnp.zeros((rows, 1), jnp.float32), jnp.zeros((rows, HEAD_DIM), jnp.float32))
        for _ in range(heads)
    )
    totals = lax.fori_loop(first, me + 1, value_step, start)
    inverse, row_dot = [], []
    for h in range(heads):
        total, summed = totals[h]
        attended = (summed / total).astype(jnp.bfloat16)
        out_ref[:, cols[h]] = attended
        inverse.append(1.0 / total)
        row_dot.append(
            jnp.sum(
                do_ref[:, cols[h]].astype(jnp.float32) * attended.astype(jnp.float32),
                1,
                keepdims=True,
            )
        )
    dq_sum[...] = jnp.zeros_like(dq_sum)
    pl.semaphore_wait(pltpu.get_barrier_semaphore(), len(greeted))

    def grads(block, result):
        seen = (block >= first) & (block <= me)

        @pl.when(seen)
        def _():
            for h in range(heads):
                spread = dot(do_ref[:, cols[h]], v_ref[block, :, cols[h]], 1, 1)
                chances = scores[h, block - first] * inverse[h]
                dscore = (chances * (spread - row_dot[h]) * scale).astype(jnp.bfloat16)
                dq_sum[:, cols[h]] += dot(dscore, k_ref[block, :, cols[h]])
                result[:, cols[h]] = dot(dscore, q_ref[:, cols[h]], 0, 0).astype(jnp.bfloat16)
                result[:, vcols[h]] = dot(
                    chances.astype(jnp.bfloat16), do_ref[:, cols[h]], 0, 0
                ).astype(jnp.bfloat16)

        @pl.when(jnp.logical_not(seen))
        def _():
            result[...] = jnp.zeros(result.shape, jnp.bfloat16)

    order = (2, -1, 0)

    def pair(number):
        return pltpu.make_async_remote_copy(
            src_ref=made.at[0, number],
            dst_ref=theirs.at[number],
            send_sem=pair_send.at[number],
            recv_sem=pair_recv.at[number],
            device_id={"seq": line_device(0, True)},
            device_id_type=pl.DeviceIdType.MESH,
        )

    def compute(number):
        def one(turn, _):
            chip = lax.rem(me // 2 + SIDE + order[number], SIDE)
            block = chip * 2 + lax.rem(lax.rem(me, 2) + 1 + turn, 2)
            grads(block, made.at[turn, number])

            @pl.when(turn == 0)
            def _():
                pair(number).start()

            return 0

        lax.fori_loop(0, 2, one, 0)

    def join(number):
        pair(number).wait_recv()
        ours[number] = add(made[1, number], theirs[number])

    ring = RingSum(
        copies,
        "ring",
        lambda offset: ours.at[order.index(offset)],
        lambda way: {"seq": line_device(way)},
        halves,
        fulls,
        sums,
        (1,),
    )
    compute(0)
    join(0)
    ring.far()
    compute(1)
    join(1)
    ring.early(-1)
    compute(2)
    for h in range(heads):
        dq_ref[:, cols[h]] = dq_sum[:, cols[h]].astype(jnp.bfloat16)
    ring.late()
    join(2)
    dkv_ref[...] = ring.result()
    copies.finish()
    for number in range(3):
        pair(number).wait_send()


def attention(lengths, q, k, v, do):
    rows, width = q.shape
    kind = q.dtype
    shape = jax.ShapeDtypeStruct((rows, width), kind)

    def buffer(count, tall):
        return pltpu.VMEM((count, tall, 2 * width), kind)

    return pl.pallas_call(
        attention_kernel,
        out_shape=(
            shape,
            shape,
            jax.ShapeDtypeStruct((rows, 2 * width), kind),
        ),
        in_specs=[SMEM] + [WHOLE] * 4,
        out_specs=(WHOLE,) * 3,
        scratch_shapes=[
            pltpu.VMEM((width // HEAD_DIM, MAX_BACK, rows, rows), jnp.float32),
            pltpu.VMEM((rows, width), jnp.float32),
            pltpu.VMEM((2, 3, rows, 2 * width), kind),
            buffer(3, rows),
            buffer(3, rows),
            buffer(2, rows // 2),
            buffer(2, rows),
            buffer(2, rows // 2),
            *semaphores(8),
            *semaphores(3),
        ],
        compiler_params=remote_params(1),
    )(lengths, q, k, v, do)


def tail_kernel(
    table,
    act_query,
    act_key_value,
    sort,
    wq_ref,
    wk_ref,
    wv_ref,
    act_all,
    out,
    weights,
    act_own,
    middle,
    outer,
    partial,
    halves,
    fulls,
    sums,
    results,
    send_sem,
    recv_sem,
    own_sem,
    load_sem,
):
    copies = Copies(send_sem, recv_sem)
    greeted = plane_neighbours() + line_neighbours()
    greet(greeted)
    _, groups, _, depth = weights.shape
    rows = sort.shape[0]
    me = lax.axis_index("seq")
    half = rows // 2
    order = [(2, 2), (1, 2), (-1, 2), (2, 1), (2, -1), (0, 2), (2, 0)]
    order += [(1, 1), (1, -1), (-1, 1), (-1, -1)]
    order += [(0, 1), (0, -1), (1, 0), (-1, 0), (0, 0)]
    loads = {}
    for number, step in enumerate(order):
        at = pl.ds(pl.multiple_of(plane_device(*step) * depth, depth), depth)
        loads[step] = [
            pltpu.make_async_copy(
                weight.at[:, at], weights.at[which, :, at], load_sem.at[3 * number + which]
            )
            for which, weight in enumerate((wq_ref, wk_ref, wv_ref))
        ]
        for load in loads[step]:
            load.start()

    width = act_query.shape[1]
    acts = (act_query[...], act_key_value[:, :width], act_key_value[:, width:])
    for which, act in enumerate(acts):
        act_own[which] = dot(sort[...], act).astype(jnp.bfloat16)
    own_act = [
        pltpu.make_async_copy(act_own.at[which], act_all.at[which, me], own_sem.at[which])
        for which in range(3)
    ]
    for own in own_act:
        own.start()
    pl.semaphore_wait(pltpu.get_barrier_semaphore(), len(greeted))
    lines = [
        line_gather(copies, ("act", which), act_own.at[which], act_all.at[which])
        for which in range(3)
    ]
    lines[0][0]()

    place = lax.broadcasted_iota(jnp.int32, (rows, 1), 0)
    sorted_kind = sum(
        (place >= table[me, 0, group]).astype(jnp.int32) for group in range(1, groups)
    )
    for which in range(3):
        act = act_own[which]
        span = slice(which * width, (which + 1) * width)
        middle[:, span] = jnp.where(sorted_kind == 1, act, jnp.zeros_like(act))
        for number in range(2):
            at = slice(number * half, (number + 1) * half)
            outer[number, :, span] = jnp.where(
                sorted_kind[at] == 2 * number, act[at], jnp.zeros_like(act[at])
            )

    def multiply(step):
        for load in loads[step]:
            load.wait()
        block = plane_device(*step)
        deep = pl.ds(pl.multiple_of(block * depth, depth), depth)

        def product(acts, group):
            total = None
            for which in range(3):
                act = acts[:, which * width : (which + 1) * width]
                term = dot(act, weights[which, group, deep, :], 1, 1)
                total = term if total is None else total + term
            return total

        both = product(middle, 1)
        for number in range(2):
            at = slice(number * half, (number + 1) * half)
            part = product(outer.at[number], 2 * number) + both[at]
            partial[block, at] = part.astype(jnp.bfloat16)

    def device(turn, da, db):
        return plane_device(da, db) if turn == 0 else plane_device(db, da)

    def second(turn, place):
        offset, number = OFFSETS[place], turn * len(OFFSETS) + place
        return RingSum(
            copies,
            ("b", number),
            lambda db: partial.at[device(turn, offset, db), pl.ds(turn * half, half)],
            lambda way: {"mod": device(turn, 0, way)},
            halves.at[number],
            fulls.at[number],
            sums.at[number],
        )

    def first(turn):
        number = 2 * len(OFFSETS) + turn
        return RingSum(
            copies,
            ("a", turn),
            lambda da: results.at[turn, OFFSETS.index(da)],
            lambda way: {"mod": device(turn, way, 0)},
            halves.at[number],
            fulls.at[number],
            sums.at[number],
        )

    rings = {
        (turn, OFFSETS[place]): second(turn, place) for place in range(4) for turn in range(2)
    }
    tops = [first(turn) for turn in range(2)]
    for number, step in enumerate(order):
        multiply(step)
        for turn in range(2):
            da, db = step if turn == 0 else (step[1], step[0])
            if db == 2:
                rings[turn, da].far()
            elif db != 0:
                rings[turn, da].early(db)
        if number == 4:
            lines[1][0]()
        if number == 6:
            lines[0][1]()
        if number == 8:
            lines[2][0]()
        if number == 10:
            for turn in range(2):
                rings[turn, 2].late()
            lines[1][1]()
        if number == 12:
            for turn in range(2):
                rings[turn, -1].late()
        if number == 14:
            for turn in range(2):
                rings[turn, 1].late()
    for turn in range(2):
        rings[turn, 0].late()
    lines[2][1]()

    for offset in OFFSETS:
        for turn in range(2):
            results[turn, OFFSETS.index(offset)] = rings[turn, offset].result()
            if offset == 2:
                tops[turn].far()
            elif offset != 0:
                tops[turn].early(offset)
        if offset == 2:
            lines[0][2]()
    for top in tops:
        top.late()
    lines[1][2]()
    total = None
    for turn, top in enumerate(tops):
        term = dot(sort[turn * half : (turn + 1) * half], top.result(), 0, 0)
        total = term if total is None else total + term
    out[...] = total.astype(out.dtype)
    lines[2][2]()
    for line in lines:
        line[3]()
    copies.finish()
    for own in own_act:
        own.wait()


def tail(table, act_query, act_key_value, sort, weights, count):
    rows, width = act_query.shape
    groups, tall, _ = weights[0].shape
    kind = act_query.dtype
    half, blocks = rows // 2, SIDE * SIDE
    depth = tall // blocks

    def buffer(*shape):
        return pltpu.VMEM((*shape, depth), kind)

    return pl.pallas_call(
        tail_kernel,
        out_shape=(
            jax.ShapeDtypeStruct((3, count, rows, width), kind),
            jax.ShapeDtypeStruct((rows, depth), kind),
        ),
        in_specs=[SMEM, WHOLE, WHOLE, WHOLE, ANY, ANY, ANY],
        out_specs=(ANY, WHOLE),
        scratch_shapes=[
            pltpu.VMEM((3, groups, tall, width), kind),
            pltpu.VMEM((3, rows, width), kind),
            pltpu.VMEM((rows, 3 * width), kind),
            pltpu.VMEM((2, half, 3 * width), kind),
            buffer(blocks, rows),
            buffer(10, 2, half // 2),
            buffer(10, 2, half),
            buffer(10, 2, half // 2),
            buffer(2, 4, half),
            *semaphores(96),
            pltpu.SemaphoreType.DMA((3,)),
            pltpu.SemaphoreType.DMA((3 * blocks,)),
        ],
        compiler_params=remote_params(3),
    )(table, act_query, act_key_value, sort, *weights)


def per_device(tokens, modality, doc_lengths, w_query, w_key, w_value, d_out):
    groups = w_query.shape[0]
    seq_count = lax.axis_size("seq")
    weights = (w_query, w_key, w_value)
    queries, sort_matrix, table, keys, values, token_columns = front(
        tokens, modality, weights, seq_count
    )
    attn_out, act_query, act_key_value = attention(
        doc_lengths, queries, keys, values, d_out
    )
    act_all, grad_tokens = tail(
        table, act_query, act_key_value, sort_matrix, weights, seq_count
    )
    grads = weight_grads(table, token_columns, act_all, groups)
    return (attn_out, grad_tokens, *grads)


def solution(mesh):
    placed = (
        P("seq", "mod"),
        P("seq", None),
        P(),
        P(None, None, "mod"),
        P(None, None, "mod"),
        P(None, None, "mod"),
        P("seq", "mod"),
    )
    return jax.shard_map(
        per_device,
        mesh=mesh,
        in_specs=placed,
        out_specs=(
            P("seq", "mod"),
            P("seq", "mod"),
            P(None, "seq", "mod"),
            P(None, "seq", "mod"),
            P(None, "seq", "mod"),
        ),
        check_vma=False,
    )
```

```python
import functools
import math

import jax
import jax.numpy as jnp
from jax import lax
from jax.experimental import pallas as pl
from jax.experimental.pallas import tpu as pltpu
from jax.sharding import PartitionSpec as P

HEAD_DIM = 128
WINDOW_PAD = 16
MAX_BACK = 5
VMEM_BYTES = 56 * 1024 * 1024


def dot(left, right, left_dim=1, right_dim=0):
    return lax.dot_general(
        left,
        right,
        (((left_dim,), (right_dim,)), ((), ())),
        preferred_element_type=jnp.float32,
    )


def params():
    return pltpu.CompilerParams(vmem_limit_bytes=VMEM_BYTES)


ANY = pl.BlockSpec(memory_space=pl.ANY)
SMEM = pl.BlockSpec(memory_space=pltpu.SMEM)
WHOLE = pl.BlockSpec(memory_space=pltpu.VMEM)


def weight_kernel(
    table,
    x_ref,
    act_ref,
    attended,
    token_grads,
    attn_out,
    grad_tokens,
    gq_ref,
    gk_ref,
    gv_ref,
    x_in,
    act_in,
    x_rows,
    x_turned,
    grads,
    sem,
    x_sem,
):
    count, rows, wide = x_rows.shape
    groups, _, depth = x_turned.shape
    window = depth // count

    def load_rows(block):
        return pltpu.make_async_copy(x_ref.at[:, block], x_in.at[:, block], x_sem.at[block])

    for block in range(count):
        load_rows(block).start()
    loads = [
        pltpu.make_async_copy(act_ref.at[which], act_in.at[which], sem.at[which])
        for which in range(3)
    ]
    for load in loads:
        load.start()
    stores = [
        pltpu.make_async_copy(attended, attn_out, sem.at[6]),
        pltpu.make_async_copy(token_grads, grad_tokens, sem.at[7]),
    ]
    for store in stores:
        store.start()

    def bounds(block, group):
        low, high = table[block, 0, group], table[block, 0, group + 1]
        start = jnp.minimum((low // WINDOW_PAD) * WINDOW_PAD, rows - window)
        return low, high, pl.multiple_of(start, WINDOW_PAD)

    def chosen(block, group, start, size):
        low, high, _ = bounds(block, group)
        at = pl.ds(start, size)
        place = lax.broadcasted_iota(jnp.int32, (size, 1), 0) + start
        picked = x_rows[block, at, :]
        return jnp.where((place >= low) & (place < high), picked, jnp.zeros_like(picked))

    def turn(block, _):
        load_rows(block).wait()
        for part in range(x_in.shape[2]):
            cols = x_in.shape[4]
            x_rows[block, :, part * cols : (part + 1) * cols] = x_in[:, block, part].reshape(
                rows, cols
            )
        columns = pl.ds(pl.multiple_of(block * window, window), window)
        for group in range(groups):
            picked = chosen(block, group, bounds(block, group)[2], window)
            x_turned[group, :, columns] = picked.T
        return 0

    lax.fori_loop(0, count, turn, 0)
    for which, out in enumerate((gq_ref, gk_ref, gv_ref)):
        loads[which].wait()
        def one(group, _):
            total = None
            for block in range(count):
                at = pl.ds(bounds(block, group)[2], window)
                term = dot(
                    x_turned[group, :, block * window : (block + 1) * window],
                    act_in[which, block, at, :],
                )
                total = term if total is None else total + term
            grads[which, group] = total

            def rest(block, _):
                low, high, start = bounds(block, group)

                @pl.when(high > start + window)
                def _():
                    at = pl.multiple_of(start + window, WINDOW_PAD)
                    picked = chosen(block, group, at, WINDOW_PAD)
                    act = act_in[which, block, pl.ds(at, WINDOW_PAD), :]
                    grads[which, group] += dot(picked, act, 0, 0)

                return 0

            lax.fori_loop(0, count, rest, 0)
            return 0

        lax.fori_loop(0, groups, one, 0)
        stores.append(pltpu.make_async_copy(grads.at[which], out, sem.at[3 + which]))
        stores[-1].start()
    for store in stores:
        store.wait()


def weight_grads(table, x, act, attended, token_grads, groups):
    pieces, count, parts, deep, cols = x.shape
    rows, wide = pieces * deep, parts * cols
    width = act.shape[3]
    out = jax.ShapeDtypeStruct((groups, wide, width), jnp.float32)
    return pl.pallas_call(
        weight_kernel,
        out_shape=(
            jax.ShapeDtypeStruct(attended.shape, attended.dtype),
            jax.ShapeDtypeStruct(token_grads.shape, token_grads.dtype),
            out,
            out,
            out,
        ),
        in_specs=[SMEM] + [ANY] * 4,
        out_specs=(ANY,) * 5,
        scratch_shapes=[
            pltpu.VMEM(x.shape, x.dtype),
            pltpu.VMEM(act.shape, act.dtype),
            pltpu.VMEM((count, rows, wide), x.dtype),
            pltpu.VMEM((groups, wide, count * (rows // 2)), x.dtype),
            pltpu.VMEM((3, groups, wide, width), jnp.float32),
            pltpu.SemaphoreType.DMA((8,)),
            pltpu.SemaphoreType.DMA((count,)),
        ],
        compiler_params=params(),
    )(table, x, act, attended, token_grads)


SIDE = 4
OFFSETS = (2, -1, 1, 0)


def greet(devices):
    barrier = pltpu.get_barrier_semaphore()
    for device in devices:
        pl.semaphore_signal(
            barrier, inc=1, device_id=device, device_id_type=pl.DeviceIdType.MESH
        )


def enter(devices):
    greet(devices)
    pl.semaphore_wait(pltpu.get_barrier_semaphore(), len(devices))


class Copies:
    def __init__(self, send_sem, recv_sem):
        self.send_sem, self.recv_sem = send_sem, recv_sem
        self.names = {}
        self.started = []

    def make(self, name, src, dst, device):
        number = self.names.setdefault(name, len(self.names))
        return pltpu.make_async_remote_copy(
            src_ref=src,
            dst_ref=dst,
            send_sem=self.send_sem.at[number],
            recv_sem=self.recv_sem.at[number],
            device_id=device,
            device_id_type=pl.DeviceIdType.MESH,
        )

    def send(self, name, src, dst, device):
        copy = self.make(name, src, dst, device)
        copy.start()
        self.started.append(copy)

    def receive(self, name, dst, device):
        self.make(name, dst, dst, device).wait_recv()

    def finish(self):
        for copy in self.started:
            copy.wait_send()


def plane_device(dx, dy):
    rank = lax.axis_index("mod")
    x, y = lax.rem(rank, SIDE), rank // SIDE
    return lax.rem(y + dy + SIDE, SIDE) * SIDE + lax.rem(x + dx + SIDE, SIDE)


def line_device(dz, other=False):
    rank = lax.axis_index("seq")
    z, core = rank // 2, lax.rem(rank, 2)
    return lax.rem(z + dz + SIDE, SIDE) * 2 + (1 - core if other else core)


def plane_neighbours():
    return [{"mod": plane_device(*step)} for step in ((1, 0), (-1, 0), (0, 1), (0, -1))]


def line_neighbours():
    return [{"seq": line_device(1)}, {"seq": line_device(-1)}, {"seq": line_device(0, True)}]


def plane_gather(copies, name, src, out):
    half = src.shape[0] // 2

    def part(turn, which):
        if which is None:
            return pl.ds(turn * half, half)
        return pl.ds(turn * half + which * (half // 2), half // 2)

    def device(turn, da, db):
        return plane_device(da, db) if turn == 0 else plane_device(db, da)

    def region(turn, da, db, which):
        return out.at[device(turn, da, db), part(turn, which)]

    def target(turn, axis, way):
        return {"mod": device(turn, way, 0) if axis == "a" else device(turn, 0, way)}

    def send(turn, axis, way, kind, offset):
        which = None if kind == "full" else (0 if way > 0 else 1)
        own = kind == "full" and offset == 0
        da = (0 if kind == "full" else -way) if axis == "a" else offset
        db = 0 if axis == "a" or kind == "full" else -way
        there = region(turn, da, db, which)
        here = src.at[part(turn, which)] if own else there
        copies.send((name, turn, axis, way, kind, offset), here, there, target(turn, axis, way))

    def receive(turn, axis, way, kind, offset):
        which = None if kind == "full" else (0 if way > 0 else 1)
        far = -way if kind == "full" else 2
        da, db = (far, 0) if axis == "a" else (offset, far)
        copies.receive(
            (name, turn, axis, way, kind, offset),
            region(turn, da, db, which),
            target(turn, axis, way),
        )

    ways, turns = (1, -1), (0, 1)

    def begin():
        for turn in turns:
            for way in ways:
                send(turn, "a", way, "full", 0)
        for turn in turns:
            for way in ways:
                send(turn, "b", way, "full", 0)

    def near():
        for way in ways:
            for turn in turns:
                receive(turn, "a", way, "full", 0)
                send(turn, "a", way, "half", 0)
                for second in ways:
                    send(turn, "b", second, "full", -way)

    def far():
        for turn in turns:
            for way in ways:
                receive(turn, "a", way, "half", 0)
            for second in ways:
                send(turn, "b", second, "full", 2)

    def fold(offset):
        for turn in turns:
            for way in ways:
                receive(turn, "b", way, "full", offset)
                send(turn, "b", way, "half", offset)

    def last(offset):
        for turn in turns:
            for way in ways:
                receive(turn, "b", way, "half", offset)

    return begin, near, far, fold, last


def line_gather(copies, name, src, out):
    half = src.shape[0] // 2

    def region(dz, other, which):
        rows = pl.ds(0, 2 * half) if which is None else pl.ds(which * half, half)
        return out.at[line_device(dz, other), rows]

    def along(way):
        return {"seq": line_device(way)}

    sibling = {"seq": line_device(0, True)}

    def pass_on(dz):
        copies.send((name, "sib", dz), region(dz, False, None), region(dz, False, None), sibling)

    def stage_0():
        for turn in range(2):
            for way in (1, -1):
                which = turn if way > 0 else 1 - turn
                here = src.at[pl.ds(which * half, half)]
                copies.send((name, way, "full", turn), here, region(0, False, which), along(way))

    def stage_1():
        for way in (1, -1):
            which = 0 if way > 0 else 1
            there = region(-way, False, which)
            copies.receive((name, way, "full", 0), there, along(way))
            copies.send((name, way, "half"), there, there, along(way))
        copies.send((name, "sib", 0), src, region(0, False, None), sibling)
        for way in (1, -1):
            which = 1 if way > 0 else 0
            copies.receive((name, way, "full", 1), region(-way, False, which), along(way))
            pass_on(-way)

    def stage_2():
        for way in (1, -1):
            which = 0 if way > 0 else 1
            copies.receive((name, way, "half"), region(2, False, which), along(way))
        pass_on(2)

    def last():
        for dz in (0, -1, 1, 2):
            copies.receive((name, "sib", dz), region(dz, True, None), sibling)

    return [stage_0, stage_1, stage_2, last]


def add(*terms):
    total = terms[0].astype(jnp.float32)
    for term in terms[1:]:
        total = total + term.astype(jnp.float32)
    return total.astype(jnp.bfloat16)


class RingSum:
    def __init__(self, copies, name, source, device, halves, fulls, sums, absent=()):
        self.absent = absent
        self.copies, self.name, self.source, self.device = copies, name, source, device
        self.halves, self.fulls, self.sums = halves, fulls, sums
        self.half = halves.shape[1]

    def rows(self, which):
        return pl.ds(which * self.half, self.half)

    def send(self, kind, way, src, dst):
        self.copies.send((self.name, kind, way), src, dst, self.device(way))

    def receive(self, kind, way, dst):
        self.copies.receive((self.name, kind, way), dst, self.device(way))

    def far(self):
        for number, way in enumerate((1, -1)):
            self.send("half", way, self.source(2).at[self.rows(number)], self.halves.at[number])

    def early(self, way):
        number = 0 if way > 0 else 1
        there = self.fulls.at[number, self.rows(1 - number)]
        self.send("early", way, self.source(way).at[self.rows(1 - number)], there)

    def late(self):
        for number, way in enumerate((1, -1)):
            self.receive("half", way, self.halves.at[number])
            there = self.fulls.at[number, self.rows(number)]
            if way in self.absent:
                self.send("late", way, self.halves.at[number], there)
                continue
            term = self.source(way)[self.rows(number)]
            self.sums[number] = add(term, self.halves[number])
            self.send("late", way, self.sums.at[number], there)

    def result(self):
        parts = [[self.source(0)[self.rows(number)]] for number in range(2)]
        for number, way in enumerate((1, -1)):
            if way not in self.absent:
                there = self.rows(1 - number)
                self.receive("early", way, self.fulls.at[number, there])
                parts[1 - number].append(self.fulls[number, there])
            there = self.rows(number)
            self.receive("late", way, self.fulls.at[number, there])
            parts[number].append(self.fulls[number, there])
        return jnp.concatenate([add(*terms) for terms in parts], 0)


def remote_params(number):
    return pltpu.CompilerParams(
        collective_id=number, has_side_effects=True, vmem_limit_bytes=VMEM_BYTES
    )


def semaphores(count):
    return [pltpu.SemaphoreType.DMA((count,)), pltpu.SemaphoreType.DMA((count,))]


def front_kernel(
    tokens,
    modality,
    wq_ref,
    wk_ref,
    wv_ref,
    q_out,
    sort_out,
    table_out,
    k_all,
    v_all,
    columns,
    rows_all,
    weights,
    pieces,
    acc,
    kv_own,
    table,
    send_sem,
    recv_sem,
    own_sem,
):
    copies = Copies(send_sem, recv_sem)
    rows, depth = tokens.shape
    groups, width, half = weights.shape[1], q_out.shape[1], rows // 2
    count = pieces.shape[0]
    me, place = lax.axis_index("seq"), lax.axis_index("mod")
    others = [lax.rem(me + step, count) for step in range(1, count)]
    greeted = [{"seq": other} for other in others] + plane_neighbours()
    greet(greeted)
    loads = [
        pltpu.make_async_copy(weight, weights.at[which], own_sem.at[which])
        for which, weight in enumerate((wq_ref, wk_ref, wv_ref))
    ]
    for load in loads:
        load.start()

    marks = modality[...]
    lanes = marks.shape[1]
    diagonal = lax.broadcasted_iota(jnp.int32, (lanes, lanes), 0) == lax.broadcasted_iota(
        jnp.int32, (lanes, lanes), 1
    )
    kind = jnp.concatenate(
        [
            jnp.sum(jnp.where(diagonal, marks[number : number + 1], 0), 1, keepdims=True)
            for number in range(marks.shape[0])
        ],
        0,
    )
    counts = [jnp.sum((kind == group).astype(jnp.int32)) for group in range(groups)]
    firsts = [jnp.int32(0)]
    for group in range(groups):
        firsts.append(firsts[-1] + counts[group])
    lane = lax.broadcasted_iota(jnp.int32, table.shape, 1)
    table[...] = sum(jnp.where(lane > group, counts[group], 0) for group in range(groups))

    lanes = lax.broadcasted_iota(jnp.int32, (rows, 128), 1)
    one_hot = (lanes == kind).astype(jnp.bfloat16)
    down = lax.broadcasted_iota(jnp.int32, (rows, rows), 0)
    across = lax.broadcasted_iota(jnp.int32, (rows, rows), 1)
    first_lane = lax.broadcasted_iota(jnp.int32, (1, 128), 1)
    base = jnp.zeros((1, 128), jnp.float32)
    for group in range(groups):
        base = jnp.where(first_lane == group, firsts[group].astype(jnp.float32), base)
    before = dot((across < down).astype(jnp.bfloat16), one_hot) + base
    rank = jnp.sum(before * one_hot.astype(jnp.float32), 1, keepdims=True).astype(jnp.int32)
    unsort = (rank == across).astype(jnp.bfloat16)
    sort = unsort.T
    sort_out[...] = sort
    rows_all[place] = dot(sort, tokens[...]).astype(jnp.bfloat16)

    line = lax.broadcasted_iota(jnp.int32, (rows, 1), 0)
    sorted_kind = sum((line >= firsts[group]).astype(jnp.int32) for group in range(1, groups))

    def multiply(blocks, new, wanted=(0, 3)):
        def one(which, _):
            low = middle = high = None
            for step in blocks:
                block = plane_device(*step)
                deep = pl.ds(pl.multiple_of(block * depth, depth), depth)
                x = rows_all[block]
                terms = []
                for group, at in enumerate((slice(0, half), slice(0, rows), slice(half, rows))):
                    own = jnp.where(sorted_kind[at] == group, x[at], jnp.zeros_like(x[at]))
                    terms.append(dot(own, weights[which, group, deep, :]))
                low = terms[0] if low is None else low + terms[0]
                middle = terms[1] if middle is None else middle + terms[1]
                high = terms[2] if high is None else high + terms[2]
            for number, part in enumerate((low, high)):
                at = slice(number * half, (number + 1) * half)
                if new:
                    acc[which, at] = part + middle[at]
                else:
                    acc[which, at] += part + middle[at]
            return 0

        lax.fori_loop(*wanted, one, 0)

    def projected(which):
        return dot(unsort, acc[which].astype(jnp.bfloat16)).astype(jnp.bfloat16)

    pl.semaphore_wait(pltpu.get_barrier_semaphore(), len(greeted))
    for step, other in enumerate(others):
        copies.send(("table", step), table, table_out.at[me], {"seq": other})
    own_table = pltpu.make_async_copy(table, table_out.at[me], own_sem.at[3])
    own_table.start()
    begin, near, far, fold, last = plane_gather(
        copies, "rows", rows_all.at[place], rows_all
    )
    begin()
    near()
    fold(0)
    for load in loads:
        load.wait()
    multiply([(0, 0), (1, 0), (-1, 0), (0, 1), (0, -1)], True)
    far()
    last(0)
    fold(-1)
    multiply([(2, 0), (0, 2)], False)
    fold(1)
    fold(2)
    multiply([(1, 1), (1, -1), (-1, 1), (-1, -1)], False)
    last(-1)
    last(1)
    rest = [(1, 2), (-1, 2), (2, 1), (2, -1)]
    multiply(rest, False, (1, 3))
    last(2)

    deep = pieces.shape[2]

    def piece(target):
        return rows_all.at[
            pl.ds(2 * target, 2), pl.ds(pl.multiple_of(place * deep, deep), deep)
        ]

    own_piece = pltpu.make_async_copy(piece(me), pieces.at[me], own_sem.at[4])
    own_piece.start()
    for step, other in enumerate(others):
        copies.send(("piece", step), piece(other), pieces.at[me], {"seq": other})
    multiply([(2, 2)], False, (1, 3))
    kv_own[0] = projected(1)
    kv_own[1] = projected(2)
    own_keys = pltpu.make_async_copy(kv_own.at[0], k_all.at[me], own_sem.at[5])
    own_values = pltpu.make_async_copy(kv_own.at[1], v_all.at[me], own_sem.at[6])
    own_keys.start()
    own_values.start()
    keys = line_gather(copies, "keys", kv_own.at[0], k_all)
    values = line_gather(copies, "values", kv_own.at[1], v_all)
    keys[0]()
    for step in range(count - 1):
        sender = lax.rem(me + count - 1 - step, count)
        copies.receive(("piece", step), pieces.at[sender], {"seq": others[step]})
    own_piece.wait()
    own_columns = pltpu.make_async_copy(pieces, columns.at[place], own_sem.at[7])
    own_columns.start()
    begin, near, far, fold, last = plane_gather(copies, "columns", pieces, columns)
    begin()
    values[0]()
    multiply([*rest, (2, 2)], False, (0, 1))
    near()
    fold(0)
    keys[1]()
    far()
    last(0)
    q_out[...] = projected(0)
    fold(-1)
    values[1]()
    fold(1)
    keys[2]()
    fold(2)
    values[2]()
    for offset in (-1, 1, 2):
        last(offset)
    keys[3]()
    values[3]()
    for step in range(count - 1):
        sender = lax.rem(me + count - 1 - step, count)
        copies.receive(("table", step), table_out.at[sender], {"seq": others[step]})
    copies.finish()
    for own in (own_table, own_keys, own_values, own_columns):
        own.wait()


def front(tokens, modality, weights, count):
    rows, depth = tokens.shape
    groups, tall, width = weights[0].shape
    blocks = SIDE * SIDE
    kind = tokens.dtype
    piece = (count, 2, rows // blocks, depth)
    half = jax.ShapeDtypeStruct((count, rows, width), kind)
    return pl.pallas_call(
        front_kernel,
        out_shape=(
            jax.ShapeDtypeStruct((rows, width), kind),
            jax.ShapeDtypeStruct((rows, rows), kind),
            jax.ShapeDtypeStruct((count, 8, 128), jnp.int32),
            half,
            half,
            jax.ShapeDtypeStruct((blocks, *piece), kind),
        ),
        in_specs=[WHOLE, WHOLE, ANY, ANY, ANY],
        out_specs=(WHOLE, WHOLE, WHOLE, ANY, ANY, ANY),
        scratch_shapes=[
            pltpu.VMEM((blocks, rows, depth), kind),
            pltpu.VMEM((3, groups, tall, width), kind),
            pltpu.VMEM(piece, kind),
            pltpu.VMEM((3, rows, width), jnp.float32),
            pltpu.VMEM((2, rows, width), kind),
            pltpu.VMEM((8, 128), jnp.int32),
            *semaphores(116),
            pltpu.SemaphoreType.DMA((8,)),
        ],
        compiler_params=remote_params(0),
    )(tokens, modality, *weights)


def attention_kernel(
    lengths,
    q_ref,
    k_ref,
    v_ref,
    do_ref,
    out_ref,
    dq_ref,
    dkv_ref,
    scores,
    dq_sum,
    made,
    theirs,
    ours,
    halves,
    fulls,
    sums,
    send_sem,
    recv_sem,
    pair_send,
    pair_recv,
):
    copies = Copies(send_sem, recv_sem)
    greeted = line_neighbours()
    greet(greeted)
    rows, width = q_ref.shape
    heads = width // HEAD_DIM
    scale = 1.0 / math.sqrt(HEAD_DIM)
    me = lax.axis_index("seq")
    first = jnp.maximum(me - (MAX_BACK - 1), 0)
    ends = [lengths[0]]
    for number in range(1, lengths.shape[0]):
        ends.append(ends[-1] + lengths[number])

    def document(positions):
        return sum((positions >= end).astype(jnp.int32) for end in ends)

    own = lax.broadcasted_iota(jnp.int32, (rows, 1), 0) + me * rows
    own_document = document(own)
    cols = [slice(h * HEAD_DIM, (h + 1) * HEAD_DIM) for h in range(heads)]
    vcols = [slice(width + h * HEAD_DIM, width + (h + 1) * HEAD_DIM) for h in range(heads)]

    def score_step(block, row_max):
        key_pos = lax.broadcasted_iota(jnp.int32, (1, rows), 1) + block * rows
        visible = (key_pos <= own) & (document(key_pos) == own_document)
        new = []
        for h in range(heads):
            part = dot(q_ref[:, cols[h]], k_ref[block, :, cols[h]], 1, 1) * scale
            part = jnp.where(visible, part, -jnp.inf)
            scores[h, block - first] = part
            new.append(jnp.maximum(row_max[h], jnp.max(part, 1, keepdims=True)))
        return tuple(new)

    start = tuple(jnp.full((rows, 1), -jnp.inf, jnp.float32) for _ in range(heads))
    row_max = lax.fori_loop(first, me + 1, score_step, start)

    def value_step(block, carry):
        new = []
        for h in range(heads):
            total, summed = carry[h]
            weights = jnp.exp(scores[h, block - first] - row_max[h])
            scores[h, block - first] = weights
            total = total + jnp.sum(weights, 1, keepdims=True)
            summed = summed + dot(weights.astype(jnp.bfloat16), v_ref[block, :, cols[h]])
            new.append((total, summed))
        return tuple(new)

    start = tuple(
        (jnp.zeros((rows, 1), jnp.float32), jnp.zeros((rows, HEAD_DIM), jnp.float32))
        for _ in range(heads)
    )
    totals = lax.fori_loop(first, me + 1, value_step, start)
    inverse, row_dot = [], []
    for h in range(heads):
        total, summed = totals[h]
        attended = (summed / total).astype(jnp.bfloat16)
        out_ref[:, cols[h]] = attended
        inverse.append(1.0 / total)
        row_dot.append(
            jnp.sum(
                do_ref[:, cols[h]].astype(jnp.float32) * attended.astype(jnp.float32),
                1,
                keepdims=True,
            )
        )
    dq_sum[...] = jnp.zeros_like(dq_sum)
    pl.semaphore_wait(pltpu.get_barrier_semaphore(), len(greeted))

    def grads(block, result):
        seen = (block >= first) & (block <= me)

        @pl.when(seen)
        def _():
            for h in range(heads):
                spread = dot(do_ref[:, cols[h]], v_ref[block, :, cols[h]], 1, 1)
                chances = scores[h, block - first] * inverse[h]
                dscore = (chances * (spread - row_dot[h]) * scale).astype(jnp.bfloat16)
                dq_sum[:, cols[h]] += dot(dscore, k_ref[block, :, cols[h]])
                result[:, cols[h]] = dot(dscore, q_ref[:, cols[h]], 0, 0).astype(jnp.bfloat16)
                result[:, vcols[h]] = dot(
                    chances.astype(jnp.bfloat16), do_ref[:, cols[h]], 0, 0
                ).astype(jnp.bfloat16)

        @pl.when(jnp.logical_not(seen))
        def _():
            result[...] = jnp.zeros(result.shape, jnp.bfloat16)

    order = (2, -1, 0)

    def pair(number):
        return pltpu.make_async_remote_copy(
            src_ref=made.at[0, number],
            dst_ref=theirs.at[number],
            send_sem=pair_send.at[number],
            recv_sem=pair_recv.at[number],
            device_id={"seq": line_device(0, True)},
            device_id_type=pl.DeviceIdType.MESH,
        )

    def compute(number):
        def one(turn, _):
            chip = lax.rem(me // 2 + SIDE + order[number], SIDE)
            block = chip * 2 + lax.rem(lax.rem(me, 2) + 1 + turn, 2)
            grads(block, made.at[turn, number])

            @pl.when(turn == 0)
            def _():
                pair(number).start()

            return 0

        lax.fori_loop(0, 2, one, 0)

    def join(number):
        pair(number).wait_recv()
        ours[number] = add(made[1, number], theirs[number])

    ring = RingSum(
        copies,
        "ring",
        lambda offset: ours.at[order.index(offset)],
        lambda way: {"seq": line_device(way)},
        halves,
        fulls,
        sums,
        (1,),
    )
    compute(0)
    join(0)
    ring.far()
    compute(1)
    join(1)
    ring.early(-1)
    compute(2)
    for h in range(heads):
        dq_ref[:, cols[h]] = dq_sum[:, cols[h]].astype(jnp.bfloat16)
    ring.late()
    join(2)
    dkv_ref[...] = ring.result()
    copies.finish()
    for number in range(3):
        pair(number).wait_send()


def attention(lengths, q, k, v, do):
    rows, width = q.shape
    kind = q.dtype
    shape = jax.ShapeDtypeStruct((rows, width), kind)

    def buffer(count, tall):
        return pltpu.VMEM((count, tall, 2 * width), kind)

    return pl.pallas_call(
        attention_kernel,
        out_shape=(
            shape,
            shape,
            jax.ShapeDtypeStruct((rows, 2 * width), kind),
        ),
        in_specs=[SMEM] + [WHOLE] * 4,
        out_specs=(WHOLE,) * 3,
        scratch_shapes=[
            pltpu.VMEM((width // HEAD_DIM, MAX_BACK, rows, rows), jnp.float32),
            pltpu.VMEM((rows, width), jnp.float32),
            pltpu.VMEM((2, 3, rows, 2 * width), kind),
            buffer(3, rows),
            buffer(3, rows),
            buffer(2, rows // 2),
            buffer(2, rows),
            buffer(2, rows // 2),
            *semaphores(8),
            *semaphores(3),
        ],
        compiler_params=remote_params(1),
    )(lengths, q, k, v, do)


def tail_kernel(
    table,
    act_query,
    act_key_value,
    sort,
    wq_ref,
    wk_ref,
    wv_ref,
    act_all,
    out,
    weights,
    act_own,
    middle,
    outer,
    partial,
    halves,
    fulls,
    sums,
    results,
    send_sem,
    recv_sem,
    own_sem,
    load_sem,
):
    copies = Copies(send_sem, recv_sem)
    greeted = plane_neighbours() + line_neighbours()
    greet(greeted)
    _, groups, _, depth = weights.shape
    rows = sort.shape[0]
    me = lax.axis_index("seq")
    half = rows // 2
    order = [(2, 2), (1, 2), (-1, 2), (2, 1), (2, -1), (0, 2), (2, 0)]
    order += [(1, 1), (1, -1), (-1, 1), (-1, -1)]
    order += [(0, 1), (0, -1), (1, 0), (-1, 0), (0, 0)]
    loads = {}
    for number, step in enumerate(order):
        at = pl.ds(pl.multiple_of(plane_device(*step) * depth, depth), depth)
        loads[step] = [
            pltpu.make_async_copy(
                weight.at[:, at], weights.at[which, :, at], load_sem.at[3 * number + which]
            )
            for which, weight in enumerate((wq_ref, wk_ref, wv_ref))
        ]
        for load in loads[step]:
            load.start()

    width = act_query.shape[1]
    acts = (act_query[...], act_key_value[:, :width], act_key_value[:, width:])
    for which, act in enumerate(acts):
        act_own[which] = dot(sort[...], act).astype(jnp.bfloat16)
    own_act = [
        pltpu.make_async_copy(act_own.at[which], act_all.at[which, me], own_sem.at[which])
        for which in range(3)
    ]
    for own in own_act:
        own.start()
    pl.semaphore_wait(pltpu.get_barrier_semaphore(), len(greeted))
    lines = [
        line_gather(copies, ("act", which), act_own.at[which], act_all.at[which])
        for which in range(3)
    ]
    lines[0][0]()

    place = lax.broadcasted_iota(jnp.int32, (rows, 1), 0)
    sorted_kind = sum(
        (place >= table[me, 0, group]).astype(jnp.int32) for group in range(1, groups)
    )
    for which in range(3):
        act = act_own[which]
        span = slice(which * width, (which + 1) * width)
        middle[:, span] = jnp.where(sorted_kind == 1, act, jnp.zeros_like(act))
        for number in range(2):
            at = slice(number * half, (number + 1) * half)
            outer[number, :, span] = jnp.where(
                sorted_kind[at] == 2 * number, act[at], jnp.zeros_like(act[at])
            )

    def multiply(step):
        for load in loads[step]:
            load.wait()
        block = plane_device(*step)
        deep = pl.ds(pl.multiple_of(block * depth, depth), depth)

        def product(acts, group):
            total = None
            for which in range(3):
                act = acts[:, which * width : (which + 1) * width]
                term = dot(act, weights[which, group, deep, :], 1, 1)
                total = term if total is None else total + term
            return total

        both = product(middle, 1)
        for number in range(2):
            at = slice(number * half, (number + 1) * half)
            part = product(outer.at[number], 2 * number) + both[at]
            partial[block, at] = part.astype(jnp.bfloat16)

    def device(turn, da, db):
        return plane_device(da, db) if turn == 0 else plane_device(db, da)

    def second(turn, place):
        offset, number = OFFSETS[place], turn * len(OFFSETS) + place
        return RingSum(
            copies,
            ("b", number),
            lambda db: partial.at[device(turn, offset, db), pl.ds(turn * half, half)],
            lambda way: {"mod": device(turn, 0, way)},
            halves.at[number],
            fulls.at[number],
            sums.at[number],
        )

    def first(turn):
        number = 2 * len(OFFSETS) + turn
        return RingSum(
            copies,
            ("a", turn),
            lambda da: results.at[turn, OFFSETS.index(da)],
            lambda way: {"mod": device(turn, way, 0)},
            halves.at[number],
            fulls.at[number],
            sums.at[number],
        )

    rings = {
        (turn, OFFSETS[place]): second(turn, place) for place in range(4) for turn in range(2)
    }
    tops = [first(turn) for turn in range(2)]
    for number, step in enumerate(order):
        multiply(step)
        for turn in range(2):
            da, db = step if turn == 0 else (step[1], step[0])
            if db == 2:
                rings[turn, da].far()
            elif db != 0:
                rings[turn, da].early(db)
        if number == 4:
            lines[1][0]()
        if number == 6:
            lines[0][1]()
        if number == 8:
            lines[2][0]()
        if number == 10:
            for turn in range(2):
                rings[turn, 2].late()
            lines[1][1]()
        if number == 12:
            for turn in range(2):
                rings[turn, -1].late()
        if number == 14:
            for turn in range(2):
                rings[turn, 1].late()
    for turn in range(2):
        rings[turn, 0].late()
    lines[2][1]()

    for offset in OFFSETS:
        for turn in range(2):
            results[turn, OFFSETS.index(offset)] = rings[turn, offset].result()
            if offset == 2:
                tops[turn].far()
            elif offset != 0:
                tops[turn].early(offset)
        if offset == 2:
            lines[0][2]()
    for top in tops:
        top.late()
    lines[1][2]()
    total = None
    for turn, top in enumerate(tops):
        term = dot(sort[turn * half : (turn + 1) * half], top.result(), 0, 0)
        total = term if total is None else total + term
    out[...] = total.astype(out.dtype)
    lines[2][2]()
    for line in lines:
        line[3]()
    copies.finish()
    for own in own_act:
        own.wait()


def tail(table, act_query, act_key_value, sort, weights, count):
    rows, width = act_query.shape
    groups, tall, _ = weights[0].shape
    kind = act_query.dtype
    half, blocks = rows // 2, SIDE * SIDE
    depth = tall // blocks

    def buffer(*shape):
        return pltpu.VMEM((*shape, depth), kind)

    return pl.pallas_call(
        tail_kernel,
        out_shape=(
            jax.ShapeDtypeStruct((3, count, rows, width), kind),
            jax.ShapeDtypeStruct((rows, depth), kind),
        ),
        in_specs=[SMEM, WHOLE, WHOLE, WHOLE, ANY, ANY, ANY],
        out_specs=(ANY, WHOLE),
        scratch_shapes=[
            pltpu.VMEM((3, groups, tall, width), kind),
            pltpu.VMEM((3, rows, width), kind),
            pltpu.VMEM((rows, 3 * width), kind),
            pltpu.VMEM((2, half, 3 * width), kind),
            buffer(blocks, rows),
            buffer(10, 2, half // 2),
            buffer(10, 2, half),
            buffer(10, 2, half // 2),
            buffer(2, 4, half),
            *semaphores(96),
            pltpu.SemaphoreType.DMA((3,)),
            pltpu.SemaphoreType.DMA((3 * blocks,)),
        ],
        compiler_params=remote_params(3),
    )(table, act_query, act_key_value, sort, *weights)


def per_device(tokens, modality, doc_lengths, w_query, w_key, w_value, d_out):
    groups = w_query.shape[0]
    seq_count = lax.axis_size("seq")
    weights = (w_query, w_key, w_value)
    queries, sort_matrix, table, keys, values, token_columns = front(
        tokens, modality.reshape(-1, 128), weights, seq_count
    )
    attn_out, act_query, act_key_value = attention(
        doc_lengths, queries, keys, values, d_out
    )
    act_all, grad_tokens = tail(
        table, act_query, act_key_value, sort_matrix, weights, seq_count
    )
    return weight_grads(table, token_columns, act_all, attn_out, grad_tokens, groups)


def solution(mesh):
    placed = (
        P("seq", "mod"),
        P("seq", None),
        P(),
        P(None, None, "mod"),
        P(None, None, "mod"),
        P(None, None, "mod"),
        P("seq", "mod"),
    )
    return jax.shard_map(
        per_device,
        mesh=mesh,
        in_specs=placed,
        out_specs=(
            P("seq", "mod"),
            P("seq", "mod"),
            P(None, "seq", "mod"),
            P(None, "seq", "mod"),
            P(None, "seq", "mod"),
        ),
        check_vma=False,
    )
```

```python
import functools
import math

import jax
import jax.numpy as jnp
from jax import lax
from jax.experimental import pallas as pl
from jax.experimental.pallas import tpu as pltpu
from jax.sharding import PartitionSpec as P

HEAD_DIM = 128
WINDOW_PAD = 16
MAX_BACK = 5
VMEM_BYTES = 56 * 1024 * 1024


def dot(left, right, left_dim=1, right_dim=0):
    return lax.dot_general(
        left,
        right,
        (((left_dim,), (right_dim,)), ((), ())),
        preferred_element_type=jnp.float32,
    )


def params():
    return pltpu.CompilerParams(vmem_limit_bytes=VMEM_BYTES)


ANY = pl.BlockSpec(memory_space=pl.ANY)
SMEM = pl.BlockSpec(memory_space=pltpu.SMEM)
WHOLE = pl.BlockSpec(memory_space=pltpu.VMEM)


def weight_kernel(
    table,
    x_ref,
    act_ref,
    attended,
    token_grads,
    attn_out,
    grad_tokens,
    gq_ref,
    gk_ref,
    gv_ref,
    x_in,
    act_in,
    x_rows,
    x_turned,
    grads,
    passed,
    sem,
    x_sem,
):
    count, rows, wide = x_rows.shape
    groups, _, depth = x_turned.shape
    window = depth // count

    def load_rows(block):
        return pltpu.make_async_copy(x_ref.at[:, block], x_in.at[:, block], x_sem.at[block])

    for block in range(count):
        load_rows(block).start()
    loads = [
        pltpu.make_async_copy(act_ref.at[which], act_in.at[which], sem.at[which])
        for which in range(3)
    ]
    for load in loads:
        load.start()
    passing = [
        pltpu.make_async_copy(attended, passed.at[0], sem.at[6]),
        pltpu.make_async_copy(token_grads, passed.at[1], sem.at[7]),
    ]
    for load in passing:
        load.start()

    def bounds(block, group):
        low, high = table[block, 0, group], table[block, 0, group + 1]
        start = jnp.minimum((low // WINDOW_PAD) * WINDOW_PAD, rows - window)
        return low, high, pl.multiple_of(start, WINDOW_PAD)

    def chosen(block, group, start, size):
        low, high, _ = bounds(block, group)
        at = pl.ds(start, size)
        place = lax.broadcasted_iota(jnp.int32, (size, 1), 0) + start
        picked = x_rows[block, at, :]
        return jnp.where((place >= low) & (place < high), picked, jnp.zeros_like(picked))

    def turn(block, _):
        load_rows(block).wait()
        for part in range(x_in.shape[2]):
            cols = x_in.shape[4]
            x_rows[block, :, part * cols : (part + 1) * cols] = x_in[:, block, part].reshape(
                rows, cols
            )
        columns = pl.ds(pl.multiple_of(block * window, window), window)
        for group in range(groups):
            picked = chosen(block, group, bounds(block, group)[2], window)
            x_turned[group, :, columns] = picked.T
        return 0

    lax.fori_loop(0, count, turn, 0)
    for load in passing:
        load.wait()
    stores = [
        pltpu.make_async_copy(passed.at[0], attn_out, sem.at[6]),
        pltpu.make_async_copy(passed.at[1], grad_tokens, sem.at[7]),
    ]
    for store in stores:
        store.start()
    for which, out in enumerate((gq_ref, gk_ref, gv_ref)):
        loads[which].wait()
        def one(group, _):
            total = None
            for block in range(count):
                at = pl.ds(bounds(block, group)[2], window)
                term = dot(
                    x_turned[group, :, block * window : (block + 1) * window],
                    act_in[which, block, at, :],
                )
                total = term if total is None else total + term
            grads[which, group] = total

            def rest(block, _):
                low, high, start = bounds(block, group)

                @pl.when(high > start + window)
                def _():
                    at = pl.multiple_of(start + window, WINDOW_PAD)
                    picked = chosen(block, group, at, WINDOW_PAD)
                    act = act_in[which, block, pl.ds(at, WINDOW_PAD), :]
                    grads[which, group] += dot(picked, act, 0, 0)

                return 0

            lax.fori_loop(0, count, rest, 0)
            return 0

        lax.fori_loop(0, groups, one, 0)
        stores.append(pltpu.make_async_copy(grads.at[which], out, sem.at[3 + which]))
        stores[-1].start()
    for store in stores:
        store.wait()


def weight_grads(table, x, act, attended, token_grads, groups):
    pieces, count, parts, deep, cols = x.shape
    rows, wide = pieces * deep, parts * cols
    width = act.shape[3]
    out = jax.ShapeDtypeStruct((groups, wide, width), jnp.float32)
    return pl.pallas_call(
        weight_kernel,
        out_shape=(
            jax.ShapeDtypeStruct(attended.shape, attended.dtype),
            jax.ShapeDtypeStruct(token_grads.shape, token_grads.dtype),
            out,
            out,
            out,
        ),
        in_specs=[SMEM] + [ANY] * 4,
        out_specs=(ANY,) * 5,
        scratch_shapes=[
            pltpu.VMEM(x.shape, x.dtype),
            pltpu.VMEM(act.shape, act.dtype),
            pltpu.VMEM((count, rows, wide), x.dtype),
            pltpu.VMEM((groups, wide, count * (rows // 2)), x.dtype),
            pltpu.VMEM((3, groups, wide, width), jnp.float32),
            pltpu.VMEM((2, *attended.shape), attended.dtype),
            pltpu.SemaphoreType.DMA((8,)),
            pltpu.SemaphoreType.DMA((count,)),
        ],
        compiler_params=params(),
    )(table, x, act, attended, token_grads)


SIDE = 4
OFFSETS = (2, -1, 1, 0)


def greet(devices):
    barrier = pltpu.get_barrier_semaphore()
    for device in devices:
        pl.semaphore_signal(
            barrier, inc=1, device_id=device, device_id_type=pl.DeviceIdType.MESH
        )


def enter(devices):
    greet(devices)
    pl.semaphore_wait(pltpu.get_barrier_semaphore(), len(devices))


class Copies:
    def __init__(self, send_sem, recv_sem):
        self.send_sem, self.recv_sem = send_sem, recv_sem
        self.names = {}
        self.started = []

    def make(self, name, src, dst, device):
        number = self.names.setdefault(name, len(self.names))
        return pltpu.make_async_remote_copy(
            src_ref=src,
            dst_ref=dst,
            send_sem=self.send_sem.at[number],
            recv_sem=self.recv_sem.at[number],
            device_id=device,
            device_id_type=pl.DeviceIdType.MESH,
        )

    def send(self, name, src, dst, device):
        copy = self.make(name, src, dst, device)
        copy.start()
        self.started.append(copy)

    def receive(self, name, dst, device):
        self.make(name, dst, dst, device).wait_recv()

    def finish(self):
        for copy in self.started:
            copy.wait_send()


def plane_device(dx, dy):
    rank = lax.axis_index("mod")
    x, y = lax.rem(rank, SIDE), rank // SIDE
    return lax.rem(y + dy + SIDE, SIDE) * SIDE + lax.rem(x + dx + SIDE, SIDE)


def line_device(dz, other=False):
    rank = lax.axis_index("seq")
    z, core = rank // 2, lax.rem(rank, 2)
    return lax.rem(z + dz + SIDE, SIDE) * 2 + (1 - core if other else core)


def plane_neighbours():
    return [{"mod": plane_device(*step)} for step in ((1, 0), (-1, 0), (0, 1), (0, -1))]


def line_neighbours():
    return [{"seq": line_device(1)}, {"seq": line_device(-1)}, {"seq": line_device(0, True)}]


def plane_gather(copies, name, src, out):
    half = src.shape[0] // 2

    def part(turn, which):
        if which is None:
            return pl.ds(turn * half, half)
        return pl.ds(turn * half + which * (half // 2), half // 2)

    def device(turn, da, db):
        return plane_device(da, db) if turn == 0 else plane_device(db, da)

    def region(turn, da, db, which):
        return out.at[device(turn, da, db), part(turn, which)]

    def target(turn, axis, way):
        return {"mod": device(turn, way, 0) if axis == "a" else device(turn, 0, way)}

    def send(turn, axis, way, kind, offset):
        which = None if kind == "full" else (0 if way > 0 else 1)
        own = kind == "full" and offset == 0
        da = (0 if kind == "full" else -way) if axis == "a" else offset
        db = 0 if axis == "a" or kind == "full" else -way
        there = region(turn, da, db, which)
        here = src.at[part(turn, which)] if own else there
        copies.send((name, turn, axis, way, kind, offset), here, there, target(turn, axis, way))

    def receive(turn, axis, way, kind, offset):
        which = None if kind == "full" else (0 if way > 0 else 1)
        far = -way if kind == "full" else 2
        da, db = (far, 0) if axis == "a" else (offset, far)
        copies.receive(
            (name, turn, axis, way, kind, offset),
            region(turn, da, db, which),
            target(turn, axis, way),
        )

    ways, turns = (1, -1), (0, 1)

    def begin():
        for turn in turns:
            for way in ways:
                send(turn, "a", way, "full", 0)
        for turn in turns:
            for way in ways:
                send(turn, "b", way, "full", 0)

    def near():
        for way in ways:
            for turn in turns:
                receive(turn, "a", way, "full", 0)
                send(turn, "a", way, "half", 0)
                for second in ways:
                    send(turn, "b", second, "full", -way)

    def far():
        for turn in turns:
            for way in ways:
                receive(turn, "a", way, "half", 0)
            for second in ways:
                send(turn, "b", second, "full", 2)

    def fold(offset):
        for turn in turns:
            for way in ways:
                receive(turn, "b", way, "full", offset)
                send(turn, "b", way, "half", offset)

    def last(offset):
        for turn in turns:
            for way in ways:
                receive(turn, "b", way, "half", offset)

    return begin, near, far, fold, last


def line_gather(copies, name, src, out):
    half = src.shape[0] // 2

    def region(dz, other, which):
        rows = pl.ds(0, 2 * half) if which is None else pl.ds(which * half, half)
        return out.at[line_device(dz, other), rows]

    def along(way):
        return {"seq": line_device(way)}

    sibling = {"seq": line_device(0, True)}

    def pass_on(dz):
        copies.send((name, "sib", dz), region(dz, False, None), region(dz, False, None), sibling)

    def stage_0():
        for turn in range(2):
            for way in (1, -1):
                which = turn if way > 0 else 1 - turn
                here = src.at[pl.ds(which * half, half)]
                copies.send((name, way, "full", turn), here, region(0, False, which), along(way))

    def stage_1():
        for way in (1, -1):
            which = 0 if way > 0 else 1
            there = region(-way, False, which)
            copies.receive((name, way, "full", 0), there, along(way))
            copies.send((name, way, "half"), there, there, along(way))
        copies.send((name, "sib", 0), src, region(0, False, None), sibling)
        for way in (1, -1):
            which = 1 if way > 0 else 0
            copies.receive((name, way, "full", 1), region(-way, False, which), along(way))
            pass_on(-way)

    def stage_2():
        for way in (1, -1):
            which = 0 if way > 0 else 1
            copies.receive((name, way, "half"), region(2, False, which), along(way))
        pass_on(2)

    def last():
        for dz in (0, -1, 1, 2):
            copies.receive((name, "sib", dz), region(dz, True, None), sibling)

    return [stage_0, stage_1, stage_2, last]


def add(*terms):
    total = terms[0].astype(jnp.float32)
    for term in terms[1:]:
        total = total + term.astype(jnp.float32)
    return total.astype(jnp.bfloat16)


class RingSum:
    def __init__(self, copies, name, source, device, halves, fulls, sums, absent=()):
        self.absent = absent
        self.copies, self.name, self.source, self.device = copies, name, source, device
        self.halves, self.fulls, self.sums = halves, fulls, sums
        self.half = halves.shape[1]

    def rows(self, which):
        return pl.ds(which * self.half, self.half)

    def send(self, kind, way, src, dst):
        self.copies.send((self.name, kind, way), src, dst, self.device(way))

    def receive(self, kind, way, dst):
        self.copies.receive((self.name, kind, way), dst, self.device(way))

    def far(self):
        for number, way in enumerate((1, -1)):
            self.send("half", way, self.source(2).at[self.rows(number)], self.halves.at[number])

    def early(self, way):
        number = 0 if way > 0 else 1
        there = self.fulls.at[number, self.rows(1 - number)]
        self.send("early", way, self.source(way).at[self.rows(1 - number)], there)

    def late(self):
        for number, way in enumerate((1, -1)):
            self.receive("half", way, self.halves.at[number])
            there = self.fulls.at[number, self.rows(number)]
            if way in self.absent:
                self.send("late", way, self.halves.at[number], there)
                continue
            term = self.source(way)[self.rows(number)]
            self.sums[number] = add(term, self.halves[number])
            self.send("late", way, self.sums.at[number], there)

    def result(self):
        parts = [[self.source(0)[self.rows(number)]] for number in range(2)]
        for number, way in enumerate((1, -1)):
            if way not in self.absent:
                there = self.rows(1 - number)
                self.receive("early", way, self.fulls.at[number, there])
                parts[1 - number].append(self.fulls[number, there])
            there = self.rows(number)
            self.receive("late", way, self.fulls.at[number, there])
            parts[number].append(self.fulls[number, there])
        return jnp.concatenate([add(*terms) for terms in parts], 0)


def remote_params(number):
    return pltpu.CompilerParams(
        collective_id=number, has_side_effects=True, vmem_limit_bytes=VMEM_BYTES
    )


def semaphores(count):
    return [pltpu.SemaphoreType.DMA((count,)), pltpu.SemaphoreType.DMA((count,))]


def front_kernel(
    tokens,
    modality,
    wq_ref,
    wk_ref,
    wv_ref,
    q_out,
    sort_out,
    table_out,
    k_all,
    v_all,
    columns,
    rows_all,
    weights,
    pieces,
    acc,
    kv_own,
    table,
    send_sem,
    recv_sem,
    own_sem,
):
    copies = Copies(send_sem, recv_sem)
    rows, depth = tokens.shape
    groups, width, half = weights.shape[1], q_out.shape[1], rows // 2
    count = pieces.shape[0]
    me, place = lax.axis_index("seq"), lax.axis_index("mod")
    others = [lax.rem(me + step, count) for step in range(1, count)]
    greeted = [{"seq": other} for other in others] + plane_neighbours()
    greet(greeted)
    loads = [
        pltpu.make_async_copy(weight, weights.at[which], own_sem.at[which])
        for which, weight in enumerate((wq_ref, wk_ref, wv_ref))
    ]
    for load in loads:
        load.start()

    marks = modality[...]
    lanes = marks.shape[1]
    diagonal = lax.broadcasted_iota(jnp.int32, (lanes, lanes), 0) == lax.broadcasted_iota(
        jnp.int32, (lanes, lanes), 1
    )
    kind = jnp.concatenate(
        [
            jnp.sum(jnp.where(diagonal, marks[number : number + 1], 0), 1, keepdims=True)
            for number in range(marks.shape[0])
        ],
        0,
    )
    counts = [jnp.sum((kind == group).astype(jnp.int32)) for group in range(groups)]
    firsts = [jnp.int32(0)]
    for group in range(groups):
        firsts.append(firsts[-1] + counts[group])
    lane = lax.broadcasted_iota(jnp.int32, table.shape, 1)
    table[...] = sum(jnp.where(lane > group, counts[group], 0) for group in range(groups))

    lanes = lax.broadcasted_iota(jnp.int32, (rows, 128), 1)
    one_hot = (lanes == kind).astype(jnp.bfloat16)
    down = lax.broadcasted_iota(jnp.int32, (rows, rows), 0)
    across = lax.broadcasted_iota(jnp.int32, (rows, rows), 1)
    first_lane = lax.broadcasted_iota(jnp.int32, (1, 128), 1)
    base = jnp.zeros((1, 128), jnp.float32)
    for group in range(groups):
        base = jnp.where(first_lane == group, firsts[group].astype(jnp.float32), base)
    before = dot((across < down).astype(jnp.bfloat16), one_hot) + base
    rank = jnp.sum(before * one_hot.astype(jnp.float32), 1, keepdims=True).astype(jnp.int32)
    unsort = (rank == across).astype(jnp.bfloat16)
    sort = unsort.T
    sort_out[...] = sort
    rows_all[place] = dot(sort, tokens[...]).astype(jnp.bfloat16)

    line = lax.broadcasted_iota(jnp.int32, (rows, 1), 0)
    sorted_kind = sum((line >= firsts[group]).astype(jnp.int32) for group in range(1, groups))

    def multiply(blocks, new, wanted=(0, 3)):
        def one(which, _):
            low = middle = high = None
            for step in blocks:
                block = plane_device(*step)
                deep = pl.ds(pl.multiple_of(block * depth, depth), depth)
                x = rows_all[block]
                terms = []
                for group, at in enumerate((slice(0, half), slice(0, rows), slice(half, rows))):
                    own = jnp.where(sorted_kind[at] == group, x[at], jnp.zeros_like(x[at]))
                    terms.append(dot(own, weights[which, group, deep, :]))
                low = terms[0] if low is None else low + terms[0]
                middle = terms[1] if middle is None else middle + terms[1]
                high = terms[2] if high is None else high + terms[2]
            for number, part in enumerate((low, high)):
                at = slice(number * half, (number + 1) * half)
                if new:
                    acc[which, at] = part + middle[at]
                else:
                    acc[which, at] += part + middle[at]
            return 0

        lax.fori_loop(*wanted, one, 0)

    def projected(which):
        return dot(unsort, acc[which].astype(jnp.bfloat16)).astype(jnp.bfloat16)

    pl.semaphore_wait(pltpu.get_barrier_semaphore(), len(greeted))
    for step, other in enumerate(others):
        copies.send(("table", step), table, table_out.at[me], {"seq": other})
    own_table = pltpu.make_async_copy(table, table_out.at[me], own_sem.at[3])
    own_table.start()
    begin, near, far, fold, last = plane_gather(
        copies, "rows", rows_all.at[place], rows_all
    )
    begin()
    near()
    fold(0)
    for load in loads:
        load.wait()
    multiply([(0, 0), (1, 0), (-1, 0), (0, 1), (0, -1)], True)
    far()
    last(0)
    fold(-1)
    multiply([(2, 0), (0, 2)], False)
    fold(1)
    fold(2)
    multiply([(1, 1), (1, -1), (-1, 1), (-1, -1)], False)
    last(-1)
    last(1)
    rest = [(1, 2), (-1, 2), (2, 1), (2, -1)]
    multiply(rest, False, (1, 3))
    last(2)

    deep = pieces.shape[2]

    def piece(target):
        return rows_all.at[
            pl.ds(2 * target, 2), pl.ds(pl.multiple_of(place * deep, deep), deep)
        ]

    own_piece = pltpu.make_async_copy(piece(me), pieces.at[me], own_sem.at[4])
    own_piece.start()
    for step, other in enumerate(others):
        copies.send(("piece", step), piece(other), pieces.at[me], {"seq": other})
    multiply([(2, 2)], False, (1, 3))
    kv_own[0] = projected(1)
    kv_own[1] = projected(2)
    own_keys = pltpu.make_async_copy(kv_own.at[0], k_all.at[me], own_sem.at[5])
    own_values = pltpu.make_async_copy(kv_own.at[1], v_all.at[me], own_sem.at[6])
    own_keys.start()
    own_values.start()
    keys = line_gather(copies, "keys", kv_own.at[0], k_all)
    values = line_gather(copies, "values", kv_own.at[1], v_all)
    keys[0]()
    for step in range(count - 1):
        sender = lax.rem(me + count - 1 - step, count)
        copies.receive(("piece", step), pieces.at[sender], {"seq": others[step]})
    own_piece.wait()
    own_columns = pltpu.make_async_copy(pieces, columns.at[place], own_sem.at[7])
    own_columns.start()
    begin, near, far, fold, last = plane_gather(copies, "columns", pieces, columns)
    begin()
    values[0]()
    multiply([*rest, (2, 2)], False, (0, 1))
    near()
    fold(0)
    keys[1]()
    far()
    last(0)
    q_out[...] = projected(0)
    fold(-1)
    values[1]()
    fold(1)
    keys[2]()
    fold(2)
    values[2]()
    for offset in (-1, 1, 2):
        last(offset)
    keys[3]()
    values[3]()
    for step in range(count - 1):
        sender = lax.rem(me + count - 1 - step, count)
        copies.receive(("table", step), table_out.at[sender], {"seq": others[step]})
    copies.finish()
    for own in (own_table, own_keys, own_values, own_columns):
        own.wait()


def front(tokens, modality, weights, count):
    rows, depth = tokens.shape
    groups, tall, width = weights[0].shape
    blocks = SIDE * SIDE
    kind = tokens.dtype
    piece = (count, 2, rows // blocks, depth)
    half = jax.ShapeDtypeStruct((count, rows, width), kind)
    return pl.pallas_call(
        front_kernel,
        out_shape=(
            jax.ShapeDtypeStruct((rows, width), kind),
            jax.ShapeDtypeStruct((rows, rows), kind),
            jax.ShapeDtypeStruct((count, 8, 128), jnp.int32),
            half,
            half,
            jax.ShapeDtypeStruct((blocks, *piece), kind),
        ),
        in_specs=[WHOLE, WHOLE, ANY, ANY, ANY],
        out_specs=(WHOLE, WHOLE, WHOLE, ANY, ANY, ANY),
        scratch_shapes=[
            pltpu.VMEM((blocks, rows, depth), kind),
            pltpu.VMEM((3, groups, tall, width), kind),
            pltpu.VMEM(piece, kind),
            pltpu.VMEM((3, rows, width), jnp.float32),
            pltpu.VMEM((2, rows, width), kind),
            pltpu.VMEM((8, 128), jnp.int32),
            *semaphores(116),
            pltpu.SemaphoreType.DMA((8,)),
        ],
        compiler_params=remote_params(0),
    )(tokens, modality, *weights)


def attention_kernel(
    lengths,
    q_ref,
    k_ref,
    v_ref,
    do_ref,
    out_ref,
    dq_ref,
    dkv_ref,
    scores,
    dq_sum,
    made,
    theirs,
    ours,
    halves,
    fulls,
    sums,
    send_sem,
    recv_sem,
    pair_send,
    pair_recv,
):
    copies = Copies(send_sem, recv_sem)
    greeted = line_neighbours()
    greet(greeted)
    rows, width = q_ref.shape
    heads = width // HEAD_DIM
    scale = 1.0 / math.sqrt(HEAD_DIM)
    me = lax.axis_index("seq")
    first = jnp.maximum(me - (MAX_BACK - 1), 0)
    ends = [lengths[0]]
    for number in range(1, lengths.shape[0]):
        ends.append(ends[-1] + lengths[number])

    def document(positions):
        return sum((positions >= end).astype(jnp.int32) for end in ends)

    own = lax.broadcasted_iota(jnp.int32, (rows, 1), 0) + me * rows
    own_document = document(own)
    cols = [slice(h * HEAD_DIM, (h + 1) * HEAD_DIM) for h in range(heads)]
    vcols = [slice(width + h * HEAD_DIM, width + (h + 1) * HEAD_DIM) for h in range(heads)]

    def score_step(block, row_max):
        key_pos = lax.broadcasted_iota(jnp.int32, (1, rows), 1) + block * rows
        visible = (key_pos <= own) & (document(key_pos) == own_document)
        new = []
        for h in range(heads):
            part = dot(q_ref[:, cols[h]], k_ref[block, :, cols[h]], 1, 1) * scale
            part = jnp.where(visible, part, -jnp.inf)
            scores[h, block - first] = part
            new.append(jnp.maximum(row_max[h], jnp.max(part, 1, keepdims=True)))
        return tuple(new)

    start = tuple(jnp.full((rows, 1), -jnp.inf, jnp.float32) for _ in range(heads))
    row_max = lax.fori_loop(first, me + 1, score_step, start)

    def value_step(block, carry):
        new = []
        for h in range(heads):
            total, summed = carry[h]
            weights = jnp.exp(scores[h, block - first] - row_max[h])
            scores[h, block - first] = weights
            total = total + jnp.sum(weights, 1, keepdims=True)
            summed = summed + dot(weights.astype(jnp.bfloat16), v_ref[block, :, cols[h]])
            new.append((total, summed))
        return tuple(new)

    start = tuple(
        (jnp.zeros((rows, 1), jnp.float32), jnp.zeros((rows, HEAD_DIM), jnp.float32))
        for _ in range(heads)
    )
    totals = lax.fori_loop(first, me + 1, value_step, start)
    inverse, row_dot = [], []
    for h in range(heads):
        total, summed = totals[h]
        attended = (summed / total).astype(jnp.bfloat16)
        out_ref[:, cols[h]] = attended
        inverse.append(1.0 / total)
        row_dot.append(
            jnp.sum(
                do_ref[:, cols[h]].astype(jnp.float32) * attended.astype(jnp.float32),
                1,
                keepdims=True,
            )
        )
    dq_sum[...] = jnp.zeros_like(dq_sum)
    pl.semaphore_wait(pltpu.get_barrier_semaphore(), len(greeted))

    def grads(block, result):
        seen = (block >= first) & (block <= me)

        @pl.when(seen)
        def _():
            for h in range(heads):
                spread = dot(do_ref[:, cols[h]], v_ref[block, :, cols[h]], 1, 1)
                chances = scores[h, block - first] * inverse[h]
                dscore = (chances * (spread - row_dot[h]) * scale).astype(jnp.bfloat16)
                dq_sum[:, cols[h]] += dot(dscore, k_ref[block, :, cols[h]])
                result[:, cols[h]] = dot(dscore, q_ref[:, cols[h]], 0, 0).astype(jnp.bfloat16)
                result[:, vcols[h]] = dot(
                    chances.astype(jnp.bfloat16), do_ref[:, cols[h]], 0, 0
                ).astype(jnp.bfloat16)

        @pl.when(jnp.logical_not(seen))
        def _():
            result[...] = jnp.zeros(result.shape, jnp.bfloat16)

    order = (2, -1, 0)

    def pair(number):
        return pltpu.make_async_remote_copy(
            src_ref=made.at[0, number],
            dst_ref=theirs.at[number],
            send_sem=pair_send.at[number],
            recv_sem=pair_recv.at[number],
            device_id={"seq": line_device(0, True)},
            device_id_type=pl.DeviceIdType.MESH,
        )

    def compute(number):
        def one(turn, _):
            chip = lax.rem(me // 2 + SIDE + order[number], SIDE)
            block = chip * 2 + lax.rem(lax.rem(me, 2) + 1 + turn, 2)
            grads(block, made.at[turn, number])

            @pl.when(turn == 0)
            def _():
                pair(number).start()

            return 0

        lax.fori_loop(0, 2, one, 0)

    def join(number):
        pair(number).wait_recv()
        ours[number] = add(made[1, number], theirs[number])

    ring = RingSum(
        copies,
        "ring",
        lambda offset: ours.at[order.index(offset)],
        lambda way: {"seq": line_device(way)},
        halves,
        fulls,
        sums,
        (1,),
    )
    compute(0)
    join(0)
    ring.far()
    compute(1)
    join(1)
    ring.early(-1)
    compute(2)
    for h in range(heads):
        dq_ref[:, cols[h]] = dq_sum[:, cols[h]].astype(jnp.bfloat16)
    ring.late()
    join(2)
    dkv_ref[...] = ring.result()
    copies.finish()
    for number in range(3):
        pair(number).wait_send()


def attention(lengths, q, k, v, do):
    rows, width = q.shape
    kind = q.dtype
    shape = jax.ShapeDtypeStruct((rows, width), kind)

    def buffer(count, tall):
        return pltpu.VMEM((count, tall, 2 * width), kind)

    return pl.pallas_call(
        attention_kernel,
        out_shape=(
            shape,
            shape,
            jax.ShapeDtypeStruct((rows, 2 * width), kind),
        ),
        in_specs=[SMEM] + [WHOLE] * 4,
        out_specs=(WHOLE,) * 3,
        scratch_shapes=[
            pltpu.VMEM((width // HEAD_DIM, MAX_BACK, rows, rows), jnp.float32),
            pltpu.VMEM((rows, width), jnp.float32),
            pltpu.VMEM((2, 3, rows, 2 * width), kind),
            buffer(3, rows),
            buffer(3, rows),
            buffer(2, rows // 2),
            buffer(2, rows),
            buffer(2, rows // 2),
            *semaphores(8),
            *semaphores(3),
        ],
        compiler_params=remote_params(1),
    )(lengths, q, k, v, do)


def tail_kernel(
    table,
    act_query,
    act_key_value,
    sort,
    wq_ref,
    wk_ref,
    wv_ref,
    act_all,
    out,
    weights,
    act_own,
    middle,
    outer,
    partial,
    halves,
    fulls,
    sums,
    results,
    send_sem,
    recv_sem,
    own_sem,
    load_sem,
):
    copies = Copies(send_sem, recv_sem)
    greeted = plane_neighbours() + line_neighbours()
    greet(greeted)
    _, groups, _, depth = weights.shape
    rows = sort.shape[0]
    me = lax.axis_index("seq")
    half = rows // 2
    order = [(2, 2), (1, 2), (-1, 2), (2, 1), (2, -1), (0, 2), (2, 0)]
    order += [(1, 1), (1, -1), (-1, 1), (-1, -1)]
    order += [(0, 1), (0, -1), (1, 0), (-1, 0), (0, 0)]
    loads = {}
    for number, step in enumerate(order):
        at = pl.ds(pl.multiple_of(plane_device(*step) * depth, depth), depth)
        loads[step] = [
            pltpu.make_async_copy(
                weight.at[:, at], weights.at[which, :, at], load_sem.at[3 * number + which]
            )
            for which, weight in enumerate((wq_ref, wk_ref, wv_ref))
        ]
        for load in loads[step]:
            load.start()

    width = act_query.shape[1]
    acts = (act_query[...], act_key_value[:, :width], act_key_value[:, width:])
    for which, act in enumerate(acts):
        act_own[which] = dot(sort[...], act).astype(jnp.bfloat16)
    own_act = [
        pltpu.make_async_copy(act_own.at[which], act_all.at[which, me], own_sem.at[which])
        for which in range(3)
    ]
    for own in own_act:
        own.start()
    pl.semaphore_wait(pltpu.get_barrier_semaphore(), len(greeted))
    lines = [
        line_gather(copies, ("act", which), act_own.at[which], act_all.at[which])
        for which in range(3)
    ]
    lines[0][0]()

    place = lax.broadcasted_iota(jnp.int32, (rows, 1), 0)
    sorted_kind = sum(
        (place >= table[me, 0, group]).astype(jnp.int32) for group in range(1, groups)
    )
    for which in range(3):
        act = act_own[which]
        span = slice(which * width, (which + 1) * width)
        middle[:, span] = jnp.where(sorted_kind == 1, act, jnp.zeros_like(act))
        for number in range(2):
            at = slice(number * half, (number + 1) * half)
            outer[number, :, span] = jnp.where(
                sorted_kind[at] == 2 * number, act[at], jnp.zeros_like(act[at])
            )

    def multiply(step):
        for load in loads[step]:
            load.wait()
        block = plane_device(*step)
        deep = pl.ds(pl.multiple_of(block * depth, depth), depth)

        def product(acts, group):
            total = None
            for which in range(3):
                act = acts[:, which * width : (which + 1) * width]
                term = dot(act, weights[which, group, deep, :], 1, 1)
                total = term if total is None else total + term
            return total

        both = product(middle, 1)
        for number in range(2):
            at = slice(number * half, (number + 1) * half)
            part = product(outer.at[number], 2 * number) + both[at]
            partial[block, at] = part.astype(jnp.bfloat16)

    def device(turn, da, db):
        return plane_device(da, db) if turn == 0 else plane_device(db, da)

    def second(turn, place):
        offset, number = OFFSETS[place], turn * len(OFFSETS) + place
        return RingSum(
            copies,
            ("b", number),
            lambda db: partial.at[device(turn, offset, db), pl.ds(turn * half, half)],
            lambda way: {"mod": device(turn, 0, way)},
            halves.at[number],
            fulls.at[number],
            sums.at[number],
        )

    def first(turn):
        number = 2 * len(OFFSETS) + turn
        return RingSum(
            copies,
            ("a", turn),
            lambda da: results.at[turn, OFFSETS.index(da)],
            lambda way: {"mod": device(turn, way, 0)},
            halves.at[number],
            fulls.at[number],
            sums.at[number],
        )

    rings = {
        (turn, OFFSETS[place]): second(turn, place) for place in range(4) for turn in range(2)
    }
    tops = [first(turn) for turn in range(2)]
    for number, step in enumerate(order):
        multiply(step)
        for turn in range(2):
            da, db = step if turn == 0 else (step[1], step[0])
            if db == 2:
                rings[turn, da].far()
            elif db != 0:
                rings[turn, da].early(db)
        if number == 4:
            lines[1][0]()
        if number == 6:
            lines[0][1]()
        if number == 8:
            lines[2][0]()
        if number == 10:
            for turn in range(2):
                rings[turn, 2].late()
            lines[1][1]()
        if number == 12:
            for turn in range(2):
                rings[turn, -1].late()
        if number == 14:
            for turn in range(2):
                rings[turn, 1].late()
    for turn in range(2):
        rings[turn, 0].late()
    lines[2][1]()

    for offset in OFFSETS:
        for turn in range(2):
            results[turn, OFFSETS.index(offset)] = rings[turn, offset].result()
            if offset == 2:
                tops[turn].far()
            elif offset != 0:
                tops[turn].early(offset)
        if offset == 2:
            lines[0][2]()
    for top in tops:
        top.late()
    lines[1][2]()
    total = None
    for turn, top in enumerate(tops):
        term = dot(sort[turn * half : (turn + 1) * half], top.result(), 0, 0)
        total = term if total is None else total + term
    out[...] = total.astype(out.dtype)
    lines[2][2]()
    for line in lines:
        line[3]()
    copies.finish()
    for own in own_act:
        own.wait()


def tail(table, act_query, act_key_value, sort, weights, count):
    rows, width = act_query.shape
    groups, tall, _ = weights[0].shape
    kind = act_query.dtype
    half, blocks = rows // 2, SIDE * SIDE
    depth = tall // blocks

    def buffer(*shape):
        return pltpu.VMEM((*shape, depth), kind)

    return pl.pallas_call(
        tail_kernel,
        out_shape=(
            jax.ShapeDtypeStruct((3, count, rows, width), kind),
            jax.ShapeDtypeStruct((rows, depth), kind),
        ),
        in_specs=[SMEM, WHOLE, WHOLE, WHOLE, ANY, ANY, ANY],
        out_specs=(ANY, WHOLE),
        scratch_shapes=[
            pltpu.VMEM((3, groups, tall, width), kind),
            pltpu.VMEM((3, rows, width), kind),
            pltpu.VMEM((rows, 3 * width), kind),
            pltpu.VMEM((2, half, 3 * width), kind),
            buffer(blocks, rows),
            buffer(10, 2, half // 2),
            buffer(10, 2, half),
            buffer(10, 2, half // 2),
            buffer(2, 4, half),
            *semaphores(96),
            pltpu.SemaphoreType.DMA((3,)),
            pltpu.SemaphoreType.DMA((3 * blocks,)),
        ],
        compiler_params=remote_params(3),
    )(table, act_query, act_key_value, sort, *weights)


def per_device(tokens, modality, doc_lengths, w_query, w_key, w_value, d_out):
    groups = w_query.shape[0]
    seq_count = lax.axis_size("seq")
    weights = (w_query, w_key, w_value)
    queries, sort_matrix, table, keys, values, token_columns = front(
        tokens, modality.reshape(-1, 128), weights, seq_count
    )
    attn_out, act_query, act_key_value = attention(
        doc_lengths, queries, keys, values, d_out
    )
    act_all, grad_tokens = tail(
        table, act_query, act_key_value, sort_matrix, weights, seq_count
    )
    return weight_grads(table, token_columns, act_all, attn_out, grad_tokens, groups)


def solution(mesh):
    placed = (
        P("seq", "mod"),
        P("seq", None),
        P(),
        P(None, None, "mod"),
        P(None, None, "mod"),
        P(None, None, "mod"),
        P("seq", "mod"),
    )
    return jax.shard_map(
        per_device,
        mesh=mesh,
        in_specs=placed,
        out_specs=(
            P("seq", "mod"),
            P("seq", "mod"),
            P(None, "seq", "mod"),
            P(None, "seq", "mod"),
            P(None, "seq", "mod"),
        ),
        check_vma=False,
    )
```

```python
import functools
import math

import jax
import jax.numpy as jnp
from jax import lax
from jax.experimental import pallas as pl
from jax.experimental.pallas import tpu as pltpu
from jax.sharding import PartitionSpec as P

HEAD_DIM = 128
WINDOW_PAD = 16
MAX_BACK = 5
VMEM_BYTES = 56 * 1024 * 1024


def dot(left, right, left_dim=1, right_dim=0):
    return lax.dot_general(
        left,
        right,
        (((left_dim,), (right_dim,)), ((), ())),
        preferred_element_type=jnp.float32,
    )


def params():
    return pltpu.CompilerParams(vmem_limit_bytes=VMEM_BYTES)


ANY = pl.BlockSpec(memory_space=pl.ANY)
SMEM = pl.BlockSpec(memory_space=pltpu.SMEM)
WHOLE = pl.BlockSpec(memory_space=pltpu.VMEM)


def weight_kernel(
    table, x_ref, act_ref, gq_ref, gk_ref, gv_ref, x_in, act_in, x_rows, x_turned, grads, sem
):
    count, rows, wide = x_rows.shape
    groups, _, depth = x_turned.shape
    window = depth // count
    loads = [pltpu.make_async_copy(x_ref, x_in, sem.at[0])]
    for which in range(3):
        loads.append(
            pltpu.make_async_copy(act_ref.at[which], act_in.at[which], sem.at[1 + which])
        )
    for load in loads:
        load.start()

    def bounds(block, group):
        low, high = table[block, 0, group], table[block, 0, group + 1]
        start = jnp.minimum((low // WINDOW_PAD) * WINDOW_PAD, rows - window)
        return low, high, pl.multiple_of(start, WINDOW_PAD)

    def chosen(block, group, start, size):
        low, high, _ = bounds(block, group)
        at = pl.ds(start, size)
        place = lax.broadcasted_iota(jnp.int32, (size, 1), 0) + start
        picked = x_rows[block, at, :]
        return jnp.where((place >= low) & (place < high), picked, jnp.zeros_like(picked))

    loads[0].wait()
    def turn(block, _):
        for part in range(x_in.shape[2]):
            cols = x_in.shape[4]
            x_rows[block, :, part * cols : (part + 1) * cols] = x_in[:, block, part].reshape(
                rows, cols
            )
        columns = pl.ds(pl.multiple_of(block * window, window), window)
        for group in range(groups):
            picked = chosen(block, group, bounds(block, group)[2], window)
            x_turned[group, :, columns] = picked.T
        return 0

    lax.fori_loop(0, count, turn, 0)
    stores = []
    for which, out in enumerate((gq_ref, gk_ref, gv_ref)):
        loads[1 + which].wait()
        def one(group, _):
            total = None
            for block in range(count):
                at = pl.ds(bounds(block, group)[2], window)
                term = dot(
                    x_turned[group, :, block * window : (block + 1) * window],
                    act_in[which, block, at, :],
                )
                total = term if total is None else total + term
            grads[which, group] = total

            def rest(block, _):
                low, high, start = bounds(block, group)

                @pl.when(high > start + window)
                def _():
                    at = pl.multiple_of(start + window, WINDOW_PAD)
                    picked = chosen(block, group, at, WINDOW_PAD)
                    act = act_in[which, block, pl.ds(at, WINDOW_PAD), :]
                    grads[which, group] += dot(picked, act, 0, 0)

                return 0

            lax.fori_loop(0, count, rest, 0)
            return 0

        lax.fori_loop(0, groups, one, 0)
        stores.append(pltpu.make_async_copy(grads.at[which], out, sem.at[4 + which]))
        stores[-1].start()
    for store in stores:
        store.wait()


def weight_grads(table, x, act, groups):
    pieces, count, parts, deep, cols = x.shape
    rows, wide = pieces * deep, parts * cols
    width = act.shape[3]
    out = jax.ShapeDtypeStruct((groups, wide, width), jnp.float32)
    return pl.pallas_call(
        weight_kernel,
        out_shape=(out, out, out),
        in_specs=[SMEM, ANY, ANY],
        out_specs=(ANY, ANY, ANY),
        scratch_shapes=[
            pltpu.VMEM(x.shape, x.dtype),
            pltpu.VMEM(act.shape, act.dtype),
            pltpu.VMEM((count, rows, wide), x.dtype),
            pltpu.VMEM((groups, wide, count * (rows // 2)), x.dtype),
            pltpu.VMEM((3, groups, wide, width), jnp.float32),
            pltpu.SemaphoreType.DMA((7,)),
        ],
        compiler_params=params(),
    )(table, x, act)


SIDE = 4
OFFSETS = (2, -1, 1, 0)


def greet(devices):
    barrier = pltpu.get_barrier_semaphore()
    for device in devices:
        pl.semaphore_signal(
            barrier, inc=1, device_id=device, device_id_type=pl.DeviceIdType.MESH
        )


def enter(devices):
    greet(devices)
    pl.semaphore_wait(pltpu.get_barrier_semaphore(), len(devices))


class Copies:
    def __init__(self, send_sem, recv_sem):
        self.send_sem, self.recv_sem = send_sem, recv_sem
        self.names = {}
        self.started = []

    def make(self, name, src, dst, device):
        number = self.names.setdefault(name, len(self.names))
        return pltpu.make_async_remote_copy(
            src_ref=src,
            dst_ref=dst,
            send_sem=self.send_sem.at[number],
            recv_sem=self.recv_sem.at[number],
            device_id=device,
            device_id_type=pl.DeviceIdType.MESH,
        )

    def send(self, name, src, dst, device):
        copy = self.make(name, src, dst, device)
        copy.start()
        self.started.append(copy)

    def receive(self, name, dst, device):
        self.make(name, dst, dst, device).wait_recv()

    def finish(self):
        for copy in self.started:
            copy.wait_send()


def plane_device(dx, dy):
    rank = lax.axis_index("mod")
    x, y = lax.rem(rank, SIDE), rank // SIDE
    return lax.rem(y + dy + SIDE, SIDE) * SIDE + lax.rem(x + dx + SIDE, SIDE)


def line_device(dz, other=False):
    rank = lax.axis_index("seq")
    z, core = rank // 2, lax.rem(rank, 2)
    return lax.rem(z + dz + SIDE, SIDE) * 2 + (1 - core if other else core)


def plane_neighbours():
    return [{"mod": plane_device(*step)} for step in ((1, 0), (-1, 0), (0, 1), (0, -1))]


def line_neighbours():
    return [{"seq": line_device(1)}, {"seq": line_device(-1)}, {"seq": line_device(0, True)}]


def plane_gather(copies, name, src, out):
    half = src.shape[0] // 2

    def part(turn, which):
        if which is None:
            return pl.ds(turn * half, half)
        return pl.ds(turn * half + which * (half // 2), half // 2)

    def device(turn, da, db):
        return plane_device(da, db) if turn == 0 else plane_device(db, da)

    def region(turn, da, db, which):
        return out.at[device(turn, da, db), part(turn, which)]

    def target(turn, axis, way):
        return {"mod": device(turn, way, 0) if axis == "a" else device(turn, 0, way)}

    def send(turn, axis, way, kind, offset):
        which = None if kind == "full" else (0 if way > 0 else 1)
        own = kind == "full" and offset == 0
        da = (0 if kind == "full" else -way) if axis == "a" else offset
        db = 0 if axis == "a" or kind == "full" else -way
        there = region(turn, da, db, which)
        here = src.at[part(turn, which)] if own else there
        copies.send((name, turn, axis, way, kind, offset), here, there, target(turn, axis, way))

    def receive(turn, axis, way, kind, offset):
        which = None if kind == "full" else (0 if way > 0 else 1)
        far = -way if kind == "full" else 2
        da, db = (far, 0) if axis == "a" else (offset, far)
        copies.receive(
            (name, turn, axis, way, kind, offset),
            region(turn, da, db, which),
            target(turn, axis, way),
        )

    ways, turns = (1, -1), (0, 1)

    def begin():
        for turn in turns:
            for way in ways:
                send(turn, "a", way, "full", 0)
        for turn in turns:
            for way in ways:
                send(turn, "b", way, "full", 0)

    def near():
        for way in ways:
            for turn in turns:
                receive(turn, "a", way, "full", 0)
                send(turn, "a", way, "half", 0)
                for second in ways:
                    send(turn, "b", second, "full", -way)

    def far():
        for turn in turns:
            for way in ways:
                receive(turn, "a", way, "half", 0)
            for second in ways:
                send(turn, "b", second, "full", 2)

    def fold(offset):
        for turn in turns:
            for way in ways:
                receive(turn, "b", way, "full", offset)
                send(turn, "b", way, "half", offset)

    def last(offset):
        for turn in turns:
            for way in ways:
                receive(turn, "b", way, "half", offset)

    return begin, near, far, fold, last


def line_gather(copies, name, src, out):
    half = src.shape[0] // 2

    def region(dz, other, which):
        rows = pl.ds(0, 2 * half) if which is None else pl.ds(which * half, half)
        return out.at[line_device(dz, other), rows]

    def along(way):
        return {"seq": line_device(way)}

    sibling = {"seq": line_device(0, True)}

    def pass_on(dz):
        copies.send((name, "sib", dz), region(dz, False, None), region(dz, False, None), sibling)

    def stage_0():
        for turn in range(2):
            for way in (1, -1):
                which = turn if way > 0 else 1 - turn
                here = src.at[pl.ds(which * half, half)]
                copies.send((name, way, "full", turn), here, region(0, False, which), along(way))

    def stage_1():
        for way in (1, -1):
            which = 0 if way > 0 else 1
            there = region(-way, False, which)
            copies.receive((name, way, "full", 0), there, along(way))
            copies.send((name, way, "half"), there, there, along(way))
        copies.send((name, "sib", 0), src, region(0, False, None), sibling)
        for way in (1, -1):
            which = 1 if way > 0 else 0
            copies.receive((name, way, "full", 1), region(-way, False, which), along(way))
            pass_on(-way)

    def stage_2():
        for way in (1, -1):
            which = 0 if way > 0 else 1
            copies.receive((name, way, "half"), region(2, False, which), along(way))
        pass_on(2)

    def last():
        for dz in (0, -1, 1, 2):
            copies.receive((name, "sib", dz), region(dz, True, None), sibling)

    return [stage_0, stage_1, stage_2, last]


def add(*terms):
    total = terms[0].astype(jnp.float32)
    for term in terms[1:]:
        total = total + term.astype(jnp.float32)
    return total.astype(jnp.bfloat16)


class RingSum:
    def __init__(self, copies, name, source, device, halves, fulls, sums, absent=()):
        self.absent = absent
        self.copies, self.name, self.source, self.device = copies, name, source, device
        self.halves, self.fulls, self.sums = halves, fulls, sums
        self.half = halves.shape[1]

    def rows(self, which):
        return pl.ds(which * self.half, self.half)

    def send(self, kind, way, src, dst):
        self.copies.send((self.name, kind, way), src, dst, self.device(way))

    def receive(self, kind, way, dst):
        self.copies.receive((self.name, kind, way), dst, self.device(way))

    def far(self):
        for number, way in enumerate((1, -1)):
            self.send("half", way, self.source(2).at[self.rows(number)], self.halves.at[number])

    def early(self, way):
        number = 0 if way > 0 else 1
        there = self.fulls.at[number, self.rows(1 - number)]
        self.send("early", way, self.source(way).at[self.rows(1 - number)], there)

    def late(self):
        for number, way in enumerate((1, -1)):
            self.receive("half", way, self.halves.at[number])
            there = self.fulls.at[number, self.rows(number)]
            if way in self.absent:
                self.send("late", way, self.halves.at[number], there)
                continue
            term = self.source(way)[self.rows(number)]
            self.sums[number] = add(term, self.halves[number])
            self.send("late", way, self.sums.at[number], there)

    def result(self):
        parts = [[self.source(0)[self.rows(number)]] for number in range(2)]
        for number, way in enumerate((1, -1)):
            if way not in self.absent:
                there = self.rows(1 - number)
                self.receive("early", way, self.fulls.at[number, there])
                parts[1 - number].append(self.fulls[number, there])
            there = self.rows(number)
            self.receive("late", way, self.fulls.at[number, there])
            parts[number].append(self.fulls[number, there])
        return jnp.concatenate([add(*terms) for terms in parts], 0)


def remote_params(number):
    return pltpu.CompilerParams(
        collective_id=number, has_side_effects=True, vmem_limit_bytes=VMEM_BYTES
    )


def semaphores(count):
    return [pltpu.SemaphoreType.DMA((count,)), pltpu.SemaphoreType.DMA((count,))]


def front_kernel(
    tokens,
    modality,
    wq_ref,
    wk_ref,
    wv_ref,
    q_out,
    sort_out,
    table_out,
    k_all,
    v_all,
    columns,
    rows_all,
    weights,
    pieces,
    acc,
    kv_own,
    table,
    send_sem,
    recv_sem,
    own_sem,
):
    copies = Copies(send_sem, recv_sem)
    rows, depth = tokens.shape
    groups, width, half = weights.shape[1], q_out.shape[1], rows // 2
    count = pieces.shape[0]
    me, place = lax.axis_index("seq"), lax.axis_index("mod")
    others = [lax.rem(me + step, count) for step in range(1, count)]
    greeted = [{"seq": other} for other in others] + plane_neighbours()
    greet(greeted)
    loads = [
        pltpu.make_async_copy(weight, weights.at[which], own_sem.at[which])
        for which, weight in enumerate((wq_ref, wk_ref, wv_ref))
    ]
    for load in loads:
        load.start()

    marks = modality[...]
    lanes = marks.shape[1]
    diagonal = lax.broadcasted_iota(jnp.int32, (lanes, lanes), 0) == lax.broadcasted_iota(
        jnp.int32, (lanes, lanes), 1
    )
    kind = jnp.concatenate(
        [
            jnp.sum(jnp.where(diagonal, marks[number : number + 1], 0), 1, keepdims=True)
            for number in range(marks.shape[0])
        ],
        0,
    )
    counts = [jnp.sum((kind == group).astype(jnp.int32)) for group in range(groups)]
    firsts = [jnp.int32(0)]
    for group in range(groups):
        firsts.append(firsts[-1] + counts[group])
    lane = lax.broadcasted_iota(jnp.int32, table.shape, 1)
    table[...] = sum(jnp.where(lane > group, counts[group], 0) for group in range(groups))

    lanes = lax.broadcasted_iota(jnp.int32, (rows, 128), 1)
    one_hot = (lanes == kind).astype(jnp.bfloat16)
    down = lax.broadcasted_iota(jnp.int32, (rows, rows), 0)
    across = lax.broadcasted_iota(jnp.int32, (rows, rows), 1)
    first_lane = lax.broadcasted_iota(jnp.int32, (1, 128), 1)
    base = jnp.zeros((1, 128), jnp.float32)
    for group in range(groups):
        base = jnp.where(first_lane == group, firsts[group].astype(jnp.float32), base)
    before = dot((across < down).astype(jnp.bfloat16), one_hot) + base
    rank = jnp.sum(before * one_hot.astype(jnp.float32), 1, keepdims=True).astype(jnp.int32)
    unsort = (rank == across).astype(jnp.bfloat16)
    sort = unsort.T
    sort_out[...] = sort
    rows_all[place] = dot(sort, tokens[...]).astype(jnp.bfloat16)

    line = lax.broadcasted_iota(jnp.int32, (rows, 1), 0)
    sorted_kind = sum((line >= firsts[group]).astype(jnp.int32) for group in range(1, groups))

    def multiply(blocks, new, wanted=(0, 3)):
        def one(which, _):
            low = middle = high = None
            for step in blocks:
                block = plane_device(*step)
                deep = pl.ds(pl.multiple_of(block * depth, depth), depth)
                x = rows_all[block]
                terms = []
                for group, at in enumerate((slice(0, half), slice(0, rows), slice(half, rows))):
                    own = jnp.where(sorted_kind[at] == group, x[at], jnp.zeros_like(x[at]))
                    terms.append(dot(own, weights[which, group, deep, :]))
                low = terms[0] if low is None else low + terms[0]
                middle = terms[1] if middle is None else middle + terms[1]
                high = terms[2] if high is None else high + terms[2]
            for number, part in enumerate((low, high)):
                at = slice(number * half, (number + 1) * half)
                if new:
                    acc[which, at] = part + middle[at]
                else:
                    acc[which, at] += part + middle[at]
            return 0

        lax.fori_loop(*wanted, one, 0)

    def projected(which):
        return dot(unsort, acc[which].astype(jnp.bfloat16)).astype(jnp.bfloat16)

    pl.semaphore_wait(pltpu.get_barrier_semaphore(), len(greeted))
    for step, other in enumerate(others):
        copies.send(("table", step), table, table_out.at[me], {"seq": other})
    own_table = pltpu.make_async_copy(table, table_out.at[me], own_sem.at[3])
    own_table.start()
    begin, near, far, fold, last = plane_gather(
        copies, "rows", rows_all.at[place], rows_all
    )
    begin()
    near()
    fold(0)
    for load in loads:
        load.wait()
    multiply([(0, 0), (1, 0), (-1, 0), (0, 1), (0, -1)], True)
    far()
    last(0)
    fold(-1)
    multiply([(2, 0), (0, 2)], False)
    fold(1)
    fold(2)
    multiply([(1, 1), (1, -1), (-1, 1), (-1, -1)], False)
    last(-1)
    last(1)
    rest = [(1, 2), (-1, 2), (2, 1), (2, -1)]
    multiply(rest, False, (1, 3))
    last(2)

    deep = pieces.shape[2]

    def piece(target):
        return rows_all.at[
            pl.ds(2 * target, 2), pl.ds(pl.multiple_of(place * deep, deep), deep)
        ]

    own_piece = pltpu.make_async_copy(piece(me), pieces.at[me], own_sem.at[4])
    own_piece.start()
    for step, other in enumerate(others):
        copies.send(("piece", step), piece(other), pieces.at[me], {"seq": other})
    multiply([(2, 2)], False, (1, 3))
    kv_own[0] = projected(1)
    kv_own[1] = projected(2)
    own_keys = pltpu.make_async_copy(kv_own.at[0], k_all.at[me], own_sem.at[5])
    own_values = pltpu.make_async_copy(kv_own.at[1], v_all.at[me], own_sem.at[6])
    own_keys.start()
    own_values.start()
    keys = line_gather(copies, "keys", kv_own.at[0], k_all)
    values = line_gather(copies, "values", kv_own.at[1], v_all)
    keys[0]()
    for step in range(count - 1):
        sender = lax.rem(me + count - 1 - step, count)
        copies.receive(("piece", step), pieces.at[sender], {"seq": others[step]})
    own_piece.wait()
    own_columns = pltpu.make_async_copy(pieces, columns.at[place], own_sem.at[7])
    own_columns.start()
    begin, near, far, fold, last = plane_gather(copies, "columns", pieces, columns)
    begin()
    values[0]()
    multiply([*rest, (2, 2)], False, (0, 1))
    near()
    fold(0)
    keys[1]()
    far()
    last(0)
    q_out[...] = projected(0)
    fold(-1)
    values[1]()
    fold(1)
    keys[2]()
    fold(2)
    values[2]()
    for offset in (-1, 1, 2):
        last(offset)
    keys[3]()
    values[3]()
    for step in range(count - 1):
        sender = lax.rem(me + count - 1 - step, count)
        copies.receive(("table", step), table_out.at[sender], {"seq": others[step]})
    copies.finish()
    for own in (own_table, own_keys, own_values, own_columns):
        own.wait()


def front(tokens, modality, weights, count):
    rows, depth = tokens.shape
    groups, tall, width = weights[0].shape
    blocks = SIDE * SIDE
    kind = tokens.dtype
    piece = (count, 2, rows // blocks, depth)
    half = jax.ShapeDtypeStruct((count, rows, width), kind)
    return pl.pallas_call(
        front_kernel,
        out_shape=(
            jax.ShapeDtypeStruct((rows, width), kind),
            jax.ShapeDtypeStruct((rows, rows), kind),
            jax.ShapeDtypeStruct((count, 8, 128), jnp.int32),
            half,
            half,
            jax.ShapeDtypeStruct((blocks, *piece), kind),
        ),
        in_specs=[WHOLE, WHOLE, ANY, ANY, ANY],
        out_specs=(WHOLE, WHOLE, WHOLE, ANY, ANY, ANY),
        scratch_shapes=[
            pltpu.VMEM((blocks, rows, depth), kind),
            pltpu.VMEM((3, groups, tall, width), kind),
            pltpu.VMEM(piece, kind),
            pltpu.VMEM((3, rows, width), jnp.float32),
            pltpu.VMEM((2, rows, width), kind),
            pltpu.VMEM((8, 128), jnp.int32),
            *semaphores(116),
            pltpu.SemaphoreType.DMA((8,)),
        ],
        compiler_params=remote_params(0),
    )(tokens, modality, *weights)


def attention_kernel(
    lengths,
    q_ref,
    k_ref,
    v_ref,
    do_ref,
    out_ref,
    dq_ref,
    dkv_ref,
    scores,
    dq_sum,
    made,
    theirs,
    ours,
    halves,
    fulls,
    sums,
    send_sem,
    recv_sem,
    pair_send,
    pair_recv,
):
    copies = Copies(send_sem, recv_sem)
    greeted = line_neighbours()
    greet(greeted)
    rows, width = q_ref.shape
    heads = width // HEAD_DIM
    scale = 1.0 / math.sqrt(HEAD_DIM)
    me = lax.axis_index("seq")
    first = jnp.maximum(me - (MAX_BACK - 1), 0)
    ends = [lengths[0]]
    for number in range(1, lengths.shape[0]):
        ends.append(ends[-1] + lengths[number])

    def document(positions):
        return sum((positions >= end).astype(jnp.int32) for end in ends)

    own = lax.broadcasted_iota(jnp.int32, (rows, 1), 0) + me * rows
    own_document = document(own)
    cols = [slice(h * HEAD_DIM, (h + 1) * HEAD_DIM) for h in range(heads)]
    vcols = [slice(width + h * HEAD_DIM, width + (h + 1) * HEAD_DIM) for h in range(heads)]

    def score_step(block, row_max):
        key_pos = lax.broadcasted_iota(jnp.int32, (1, rows), 1) + block * rows
        visible = (key_pos <= own) & (document(key_pos) == own_document)
        new = []
        for h in range(heads):
            part = dot(q_ref[:, cols[h]], k_ref[block, :, cols[h]], 1, 1) * scale
            part = jnp.where(visible, part, -jnp.inf)
            scores[h, block - first] = part
            new.append(jnp.maximum(row_max[h], jnp.max(part, 1, keepdims=True)))
        return tuple(new)

    start = tuple(jnp.full((rows, 1), -jnp.inf, jnp.float32) for _ in range(heads))
    row_max = lax.fori_loop(first, me + 1, score_step, start)

    def value_step(block, carry):
        new = []
        for h in range(heads):
            total, summed = carry[h]
            weights = jnp.exp(scores[h, block - first] - row_max[h])
            scores[h, block - first] = weights
            total = total + jnp.sum(weights, 1, keepdims=True)
            summed = summed + dot(weights.astype(jnp.bfloat16), v_ref[block, :, cols[h]])
            new.append((total, summed))
        return tuple(new)

    start = tuple(
        (jnp.zeros((rows, 1), jnp.float32), jnp.zeros((rows, HEAD_DIM), jnp.float32))
        for _ in range(heads)
    )
    totals = lax.fori_loop(first, me + 1, value_step, start)
    inverse, row_dot = [], []
    for h in range(heads):
        total, summed = totals[h]
        attended = (summed / total).astype(jnp.bfloat16)
        out_ref[:, cols[h]] = attended
        inverse.append(1.0 / total)
        row_dot.append(
            jnp.sum(
                do_ref[:, cols[h]].astype(jnp.float32) * attended.astype(jnp.float32),
                1,
                keepdims=True,
            )
        )
    dq_sum[...] = jnp.zeros_like(dq_sum)
    pl.semaphore_wait(pltpu.get_barrier_semaphore(), len(greeted))

    def grads(block, result):
        seen = (block >= first) & (block <= me)

        @pl.when(seen)
        def _():
            for h in range(heads):
                spread = dot(do_ref[:, cols[h]], v_ref[block, :, cols[h]], 1, 1)
                chances = scores[h, block - first] * inverse[h]
                dscore = (chances * (spread - row_dot[h]) * scale).astype(jnp.bfloat16)
                dq_sum[:, cols[h]] += dot(dscore, k_ref[block, :, cols[h]])
                result[:, cols[h]] = dot(dscore, q_ref[:, cols[h]], 0, 0).astype(jnp.bfloat16)
                result[:, vcols[h]] = dot(
                    chances.astype(jnp.bfloat16), do_ref[:, cols[h]], 0, 0
                ).astype(jnp.bfloat16)

        @pl.when(jnp.logical_not(seen))
        def _():
            result[...] = jnp.zeros(result.shape, jnp.bfloat16)

    order = (2, -1, 0)

    def pair(number):
        return pltpu.make_async_remote_copy(
            src_ref=made.at[0, number],
            dst_ref=theirs.at[number],
            send_sem=pair_send.at[number],
            recv_sem=pair_recv.at[number],
            device_id={"seq": line_device(0, True)},
            device_id_type=pl.DeviceIdType.MESH,
        )

    def compute(number):
        def one(turn, _):
            chip = lax.rem(me // 2 + SIDE + order[number], SIDE)
            block = chip * 2 + lax.rem(lax.rem(me, 2) + 1 + turn, 2)
            grads(block, made.at[turn, number])

            @pl.when(turn == 0)
            def _():
                pair(number).start()

            return 0

        lax.fori_loop(0, 2, one, 0)

    def join(number):
        pair(number).wait_recv()
        ours[number] = add(made[1, number], theirs[number])

    ring = RingSum(
        copies,
        "ring",
        lambda offset: ours.at[order.index(offset)],
        lambda way: {"seq": line_device(way)},
        halves,
        fulls,
        sums,
        (1,),
    )
    compute(0)
    join(0)
    ring.far()
    compute(1)
    join(1)
    ring.early(-1)
    compute(2)
    for h in range(heads):
        dq_ref[:, cols[h]] = dq_sum[:, cols[h]].astype(jnp.bfloat16)
    ring.late()
    join(2)
    dkv_ref[...] = ring.result()
    copies.finish()
    for number in range(3):
        pair(number).wait_send()


def attention(lengths, q, k, v, do):
    rows, width = q.shape
    kind = q.dtype
    shape = jax.ShapeDtypeStruct((rows, width), kind)

    def buffer(count, tall):
        return pltpu.VMEM((count, tall, 2 * width), kind)

    return pl.pallas_call(
        attention_kernel,
        out_shape=(
            shape,
            shape,
            jax.ShapeDtypeStruct((rows, 2 * width), kind),
        ),
        in_specs=[SMEM] + [WHOLE] * 4,
        out_specs=(WHOLE,) * 3,
        scratch_shapes=[
            pltpu.VMEM((width // HEAD_DIM, MAX_BACK, rows, rows), jnp.float32),
            pltpu.VMEM((rows, width), jnp.float32),
            pltpu.VMEM((2, 3, rows, 2 * width), kind),
            buffer(3, rows),
            buffer(3, rows),
            buffer(2, rows // 2),
            buffer(2, rows),
            buffer(2, rows // 2),
            *semaphores(8),
            *semaphores(3),
        ],
        compiler_params=remote_params(1),
    )(lengths, q, k, v, do)


def tail_kernel(
    table,
    act_query,
    act_key_value,
    sort,
    wq_ref,
    wk_ref,
    wv_ref,
    act_all,
    out,
    weights,
    act_own,
    middle,
    outer,
    partial,
    halves,
    fulls,
    sums,
    results,
    send_sem,
    recv_sem,
    own_sem,
    load_sem,
):
    copies = Copies(send_sem, recv_sem)
    greeted = plane_neighbours() + line_neighbours()
    greet(greeted)
    _, groups, _, depth = weights.shape
    rows = sort.shape[0]
    me = lax.axis_index("seq")
    half = rows // 2
    order = [(2, 2), (1, 2), (-1, 2), (2, 1), (2, -1), (0, 2), (2, 0)]
    order += [(1, 1), (1, -1), (-1, 1), (-1, -1)]
    order += [(0, 1), (0, -1), (1, 0), (-1, 0), (0, 0)]
    loads = {}
    for number, step in enumerate(order):
        at = pl.ds(pl.multiple_of(plane_device(*step) * depth, depth), depth)
        loads[step] = [
            pltpu.make_async_copy(
                weight.at[:, at], weights.at[which, :, at], load_sem.at[3 * number + which]
            )
            for which, weight in enumerate((wq_ref, wk_ref, wv_ref))
        ]
        for load in loads[step]:
            load.start()

    width = act_query.shape[1]
    acts = (act_query[...], act_key_value[:, :width], act_key_value[:, width:])
    for which, act in enumerate(acts):
        act_own[which] = dot(sort[...], act).astype(jnp.bfloat16)
    own_act = [
        pltpu.make_async_copy(act_own.at[which], act_all.at[which, me], own_sem.at[which])
        for which in range(3)
    ]
    for own in own_act:
        own.start()
    pl.semaphore_wait(pltpu.get_barrier_semaphore(), len(greeted))
    lines = [
        line_gather(copies, ("act", which), act_own.at[which], act_all.at[which])
        for which in range(3)
    ]
    lines[0][0]()

    place = lax.broadcasted_iota(jnp.int32, (rows, 1), 0)
    sorted_kind = sum(
        (place >= table[me, 0, group]).astype(jnp.int32) for group in range(1, groups)
    )
    for which in range(3):
        act = act_own[which]
        span = slice(which * width, (which + 1) * width)
        middle[:, span] = jnp.where(sorted_kind == 1, act, jnp.zeros_like(act))
        for number in range(2):
            at = slice(number * half, (number + 1) * half)
            outer[number, :, span] = jnp.where(
                sorted_kind[at] == 2 * number, act[at], jnp.zeros_like(act[at])
            )

    def multiply(step):
        for load in loads[step]:
            load.wait()
        block = plane_device(*step)
        deep = pl.ds(pl.multiple_of(block * depth, depth), depth)

        def product(acts, group):
            total = None
            for which in range(3):
                act = acts[:, which * width : (which + 1) * width]
                term = dot(act, weights[which, group, deep, :], 1, 1)
                total = term if total is None else total + term
            return total

        both = product(middle, 1)
        for number in range(2):
            at = slice(number * half, (number + 1) * half)
            part = product(outer.at[number], 2 * number) + both[at]
            partial[block, at] = part.astype(jnp.bfloat16)

    def device(turn, da, db):
        return plane_device(da, db) if turn == 0 else plane_device(db, da)

    def second(turn, place):
        offset, number = OFFSETS[place], turn * len(OFFSETS) + place
        return RingSum(
            copies,
            ("b", number),
            lambda db: partial.at[device(turn, offset, db), pl.ds(turn * half, half)],
            lambda way: {"mod": device(turn, 0, way)},
            halves.at[number],
            fulls.at[number],
            sums.at[number],
        )

    def first(turn):
        number = 2 * len(OFFSETS) + turn
        return RingSum(
            copies,
            ("a", turn),
            lambda da: results.at[turn, OFFSETS.index(da)],
            lambda way: {"mod": device(turn, way, 0)},
            halves.at[number],
            fulls.at[number],
            sums.at[number],
        )

    rings = {
        (turn, OFFSETS[place]): second(turn, place) for place in range(4) for turn in range(2)
    }
    tops = [first(turn) for turn in range(2)]
    for number, step in enumerate(order):
        multiply(step)
        for turn in range(2):
            da, db = step if turn == 0 else (step[1], step[0])
            if db == 2:
                rings[turn, da].far()
            elif db != 0:
                rings[turn, da].early(db)
        if number == 4:
            lines[1][0]()
        if number == 6:
            lines[0][1]()
        if number == 8:
            lines[2][0]()
        if number == 10:
            for turn in range(2):
                rings[turn, 2].late()
            lines[1][1]()
        if number == 12:
            for turn in range(2):
                rings[turn, -1].late()
        if number == 14:
            for turn in range(2):
                rings[turn, 1].late()
    for turn in range(2):
        rings[turn, 0].late()
    lines[2][1]()

    for offset in OFFSETS:
        for turn in range(2):
            results[turn, OFFSETS.index(offset)] = rings[turn, offset].result()
            if offset == 2:
                tops[turn].far()
            elif offset != 0:
                tops[turn].early(offset)
        if offset == 2:
            lines[0][2]()
    for top in tops:
        top.late()
    lines[1][2]()
    total = None
    for turn, top in enumerate(tops):
        term = dot(sort[turn * half : (turn + 1) * half], top.result(), 0, 0)
        total = term if total is None else total + term
    out[...] = total.astype(out.dtype)
    lines[2][2]()
    for line in lines:
        line[3]()
    copies.finish()
    for own in own_act:
        own.wait()


def tail(table, act_query, act_key_value, sort, weights, count):
    rows, width = act_query.shape
    groups, tall, _ = weights[0].shape
    kind = act_query.dtype
    half, blocks = rows // 2, SIDE * SIDE
    depth = tall // blocks

    def buffer(*shape):
        return pltpu.VMEM((*shape, depth), kind)

    return pl.pallas_call(
        tail_kernel,
        out_shape=(
            jax.ShapeDtypeStruct((3, count, rows, width), kind),
            jax.ShapeDtypeStruct((rows, depth), kind),
        ),
        in_specs=[SMEM, WHOLE, WHOLE, WHOLE, ANY, ANY, ANY],
        out_specs=(ANY, WHOLE),
        scratch_shapes=[
            pltpu.VMEM((3, groups, tall, width), kind),
            pltpu.VMEM((3, rows, width), kind),
            pltpu.VMEM((rows, 3 * width), kind),
            pltpu.VMEM((2, half, 3 * width), kind),
            buffer(blocks, rows),
            buffer(10, 2, half // 2),
            buffer(10, 2, half),
            buffer(10, 2, half // 2),
            buffer(2, 4, half),
            *semaphores(96),
            pltpu.SemaphoreType.DMA((3,)),
            pltpu.SemaphoreType.DMA((3 * blocks,)),
        ],
        compiler_params=remote_params(3),
    )(table, act_query, act_key_value, sort, *weights)


def per_device(tokens, modality, doc_lengths, w_query, w_key, w_value, d_out):
    groups = w_query.shape[0]
    seq_count = lax.axis_size("seq")
    weights = (w_query, w_key, w_value)
    queries, sort_matrix, table, keys, values, token_columns = front(
        tokens, modality.reshape(-1, 128), weights, seq_count
    )
    attn_out, act_query, act_key_value = attention(
        doc_lengths, queries, keys, values, d_out
    )
    act_all, grad_tokens = tail(
        table, act_query, act_key_value, sort_matrix, weights, seq_count
    )
    grads = weight_grads(table, token_columns, act_all, groups)
    return (attn_out, grad_tokens, *grads)


def solution(mesh):
    placed = (
        P("seq", "mod"),
        P("seq", None),
        P(),
        P(None, None, "mod"),
        P(None, None, "mod"),
        P(None, None, "mod"),
        P("seq", "mod"),
    )
    return jax.shard_map(
        per_device,
        mesh=mesh,
        in_specs=placed,
        out_specs=(
            P("seq", "mod"),
            P("seq", "mod"),
            P(None, "seq", "mod"),
            P(None, "seq", "mod"),
            P(None, "seq", "mod"),
        ),
        check_vma=False,
    )
```

```python
import functools
import math

import jax
import jax.numpy as jnp
from jax import lax
from jax.experimental import pallas as pl
from jax.experimental.pallas import tpu as pltpu
from jax.sharding import PartitionSpec as P

HEAD_DIM = 128
WINDOW_PAD = 16
MAX_BACK = 5
VMEM_BYTES = 56 * 1024 * 1024


def dot(left, right, left_dim=1, right_dim=0):
    return lax.dot_general(
        left,
        right,
        (((left_dim,), (right_dim,)), ((), ())),
        preferred_element_type=jnp.float32,
    )


def params():
    return pltpu.CompilerParams(vmem_limit_bytes=VMEM_BYTES)


ANY = pl.BlockSpec(memory_space=pl.ANY)
SMEM = pl.BlockSpec(memory_space=pltpu.SMEM)
WHOLE = pl.BlockSpec(memory_space=pltpu.VMEM)


def weight_kernel(
    table, x_ref, act_ref, gq_ref, gk_ref, gv_ref, x_in, act_in, x_rows, x_turned, grads, sem
):
    count, rows, wide = x_rows.shape
    groups, _, depth = x_turned.shape
    window = depth // count
    loads = [pltpu.make_async_copy(x_ref, x_in, sem.at[0])]
    for which in range(3):
        loads.append(
            pltpu.make_async_copy(act_ref.at[which], act_in.at[which], sem.at[1 + which])
        )
    for load in loads:
        load.start()

    def bounds(block, group):
        low, high = table[block, 0, group], table[block, 0, group + 1]
        start = jnp.minimum((low // WINDOW_PAD) * WINDOW_PAD, rows - window)
        return low, high, pl.multiple_of(start, WINDOW_PAD)

    def chosen(block, group, start, size):
        low, high, _ = bounds(block, group)
        at = pl.ds(start, size)
        place = lax.broadcasted_iota(jnp.int32, (size, 1), 0) + start
        picked = x_rows[block, at, :]
        return jnp.where((place >= low) & (place < high), picked, jnp.zeros_like(picked))

    loads[0].wait()
    def turn(block, _):
        for part in range(x_in.shape[2]):
            cols = x_in.shape[4]
            x_rows[block, :, part * cols : (part + 1) * cols] = x_in[:, block, part].reshape(
                rows, cols
            )
        columns = pl.ds(pl.multiple_of(block * window, window), window)
        for group in range(groups):
            picked = chosen(block, group, bounds(block, group)[2], window)
            x_turned[group, :, columns] = picked.T
        return 0

    lax.fori_loop(0, count, turn, 0)
    stores = []
    for which, out in enumerate((gq_ref, gk_ref, gv_ref)):
        loads[1 + which].wait()
        def one(group, _):
            total = None
            for block in range(count):
                at = pl.ds(bounds(block, group)[2], window)
                term = dot(
                    x_turned[group, :, block * window : (block + 1) * window],
                    act_in[which, block, at, :],
                )
                total = term if total is None else total + term
            grads[which, group] = total

            def rest(block, _):
                low, high, start = bounds(block, group)

                @pl.when(high > start + window)
                def _():
                    at = pl.multiple_of(start + window, WINDOW_PAD)
                    picked = chosen(block, group, at, WINDOW_PAD)
                    act = act_in[which, block, pl.ds(at, WINDOW_PAD), :]
                    grads[which, group] += dot(picked, act, 0, 0)

                return 0

            lax.fori_loop(0, count, rest, 0)
            return 0

        lax.fori_loop(0, groups, one, 0)
        stores.append(pltpu.make_async_copy(grads.at[which], out, sem.at[4 + which]))
        stores[-1].start()
    for store in stores:
        store.wait()


def weight_grads(table, x, act, groups):
    pieces, count, parts, deep, cols = x.shape
    rows, wide = pieces * deep, parts * cols
    width = act.shape[3]
    out = jax.ShapeDtypeStruct((groups, wide, width), jnp.float32)
    return pl.pallas_call(
        weight_kernel,
        out_shape=(out, out, out),
        in_specs=[SMEM, ANY, ANY],
        out_specs=(ANY, ANY, ANY),
        scratch_shapes=[
            pltpu.VMEM(x.shape, x.dtype),
            pltpu.VMEM(act.shape, act.dtype),
            pltpu.VMEM((count, rows, wide), x.dtype),
            pltpu.VMEM((groups, wide, count * (rows // 2)), x.dtype),
            pltpu.VMEM((3, groups, wide, width), jnp.float32),
            pltpu.SemaphoreType.DMA((7,)),
        ],
        compiler_params=params(),
    )(table, x, act)


SIDE = 4
OFFSETS = (2, -1, 1, 0)


def greet(devices):
    barrier = pltpu.get_barrier_semaphore()
    for device in devices:
        pl.semaphore_signal(
            barrier, inc=1, device_id=device, device_id_type=pl.DeviceIdType.MESH
        )


def enter(devices):
    greet(devices)
    pl.semaphore_wait(pltpu.get_barrier_semaphore(), len(devices))


class Copies:
    def __init__(self, send_sem, recv_sem):
        self.send_sem, self.recv_sem = send_sem, recv_sem
        self.names = {}
        self.started = []

    def make(self, name, src, dst, device):
        number = self.names.setdefault(name, len(self.names))
        return pltpu.make_async_remote_copy(
            src_ref=src,
            dst_ref=dst,
            send_sem=self.send_sem.at[number],
            recv_sem=self.recv_sem.at[number],
            device_id=device,
            device_id_type=pl.DeviceIdType.MESH,
        )

    def send(self, name, src, dst, device):
        copy = self.make(name, src, dst, device)
        copy.start()
        self.started.append(copy)

    def receive(self, name, dst, device):
        self.make(name, dst, dst, device).wait_recv()

    def finish(self):
        for copy in self.started:
            copy.wait_send()


def plane_device(dx, dy):
    rank = lax.axis_index("mod")
    x, y = lax.rem(rank, SIDE), rank // SIDE
    return lax.rem(y + dy + SIDE, SIDE) * SIDE + lax.rem(x + dx + SIDE, SIDE)


def line_device(dz, other=False):
    rank = lax.axis_index("seq")
    z, core = rank // 2, lax.rem(rank, 2)
    return lax.rem(z + dz + SIDE, SIDE) * 2 + (1 - core if other else core)


def plane_neighbours():
    return [{"mod": plane_device(*step)} for step in ((1, 0), (-1, 0), (0, 1), (0, -1))]


def line_neighbours():
    return [{"seq": line_device(1)}, {"seq": line_device(-1)}, {"seq": line_device(0, True)}]


def plane_gather(copies, name, src, out):
    half = src.shape[0] // 2

    def part(turn, which):
        if which is None:
            return pl.ds(turn * half, half)
        return pl.ds(turn * half + which * (half // 2), half // 2)

    def device(turn, da, db):
        return plane_device(da, db) if turn == 0 else plane_device(db, da)

    def region(turn, da, db, which):
        return out.at[device(turn, da, db), part(turn, which)]

    def target(turn, axis, way):
        return {"mod": device(turn, way, 0) if axis == "a" else device(turn, 0, way)}

    def send(turn, axis, way, kind, offset):
        which = None if kind == "full" else (0 if way > 0 else 1)
        own = kind == "full" and offset == 0
        da = (0 if kind == "full" else -way) if axis == "a" else offset
        db = 0 if axis == "a" or kind == "full" else -way
        there = region(turn, da, db, which)
        here = src.at[part(turn, which)] if own else there
        copies.send((name, turn, axis, way, kind, offset), here, there, target(turn, axis, way))

    def receive(turn, axis, way, kind, offset):
        which = None if kind == "full" else (0 if way > 0 else 1)
        far = -way if kind == "full" else 2
        da, db = (far, 0) if axis == "a" else (offset, far)
        copies.receive(
            (name, turn, axis, way, kind, offset),
            region(turn, da, db, which),
            target(turn, axis, way),
        )

    ways, turns = (1, -1), (0, 1)

    def begin():
        for turn in turns:
            for way in ways:
                send(turn, "a", way, "full", 0)
        for turn in turns:
            for way in ways:
                send(turn, "b", way, "full", 0)

    def near():
        for way in ways:
            for turn in turns:
                receive(turn, "a", way, "full", 0)
                send(turn, "a", way, "half", 0)
                for second in ways:
                    send(turn, "b", second, "full", -way)

    def far():
        for turn in turns:
            for way in ways:
                receive(turn, "a", way, "half", 0)
            for second in ways:
                send(turn, "b", second, "full", 2)

    def fold(offset):
        for turn in turns:
            for way in ways:
                receive(turn, "b", way, "full", offset)
                send(turn, "b", way, "half", offset)

    def last(offset):
        for turn in turns:
            for way in ways:
                receive(turn, "b", way, "half", offset)

    return begin, near, far, fold, last


def line_gather(copies, name, src, out):
    half = src.shape[0] // 2

    def region(dz, other, which):
        rows = pl.ds(0, 2 * half) if which is None else pl.ds(which * half, half)
        return out.at[line_device(dz, other), rows]

    def along(way):
        return {"seq": line_device(way)}

    sibling = {"seq": line_device(0, True)}

    def pass_on(dz):
        copies.send((name, "sib", dz), region(dz, False, None), region(dz, False, None), sibling)

    def stage_0():
        for turn in range(2):
            for way in (1, -1):
                which = turn if way > 0 else 1 - turn
                here = src.at[pl.ds(which * half, half)]
                copies.send((name, way, "full", turn), here, region(0, False, which), along(way))

    def stage_1():
        for way in (1, -1):
            which = 0 if way > 0 else 1
            there = region(-way, False, which)
            copies.receive((name, way, "full", 0), there, along(way))
            copies.send((name, way, "half"), there, there, along(way))
        copies.send((name, "sib", 0), src, region(0, False, None), sibling)
        for way in (1, -1):
            which = 1 if way > 0 else 0
            copies.receive((name, way, "full", 1), region(-way, False, which), along(way))
            pass_on(-way)

    def stage_2():
        for way in (1, -1):
            which = 0 if way > 0 else 1
            copies.receive((name, way, "half"), region(2, False, which), along(way))
        pass_on(2)

    def last():
        for dz in (0, -1, 1, 2):
            copies.receive((name, "sib", dz), region(dz, True, None), sibling)

    return [stage_0, stage_1, stage_2, last]


def add(*terms):
    total = terms[0].astype(jnp.float32)
    for term in terms[1:]:
        total = total + term.astype(jnp.float32)
    return total.astype(jnp.bfloat16)


class RingSum:
    def __init__(self, copies, name, source, device, halves, fulls, sums, absent=()):
        self.absent = absent
        self.copies, self.name, self.source, self.device = copies, name, source, device
        self.halves, self.fulls, self.sums = halves, fulls, sums
        self.half = halves.shape[1]

    def rows(self, which):
        return pl.ds(which * self.half, self.half)

    def send(self, kind, way, src, dst):
        self.copies.send((self.name, kind, way), src, dst, self.device(way))

    def receive(self, kind, way, dst):
        self.copies.receive((self.name, kind, way), dst, self.device(way))

    def far(self):
        for number, way in enumerate((1, -1)):
            self.send("half", way, self.source(2).at[self.rows(number)], self.halves.at[number])

    def early(self, way):
        number = 0 if way > 0 else 1
        there = self.fulls.at[number, self.rows(1 - number)]
        self.send("early", way, self.source(way).at[self.rows(1 - number)], there)

    def late(self):
        for number, way in enumerate((1, -1)):
            self.receive("half", way, self.halves.at[number])
            there = self.fulls.at[number, self.rows(number)]
            if way in self.absent:
                self.send("late", way, self.halves.at[number], there)
                continue
            term = self.source(way)[self.rows(number)]
            self.sums[number] = add(term, self.halves[number])
            self.send("late", way, self.sums.at[number], there)

    def result(self):
        parts = [[self.source(0)[self.rows(number)]] for number in range(2)]
        for number, way in enumerate((1, -1)):
            if way not in self.absent:
                there = self.rows(1 - number)
                self.receive("early", way, self.fulls.at[number, there])
                parts[1 - number].append(self.fulls[number, there])
            there = self.rows(number)
            self.receive("late", way, self.fulls.at[number, there])
            parts[number].append(self.fulls[number, there])
        return jnp.concatenate([add(*terms) for terms in parts], 0)


def remote_params(number):
    return pltpu.CompilerParams(
        collective_id=number, has_side_effects=True, vmem_limit_bytes=VMEM_BYTES
    )


def semaphores(count):
    return [pltpu.SemaphoreType.DMA((count,)), pltpu.SemaphoreType.DMA((count,))]


def front_kernel(
    tokens,
    modality,
    wq_ref,
    wk_ref,
    wv_ref,
    q_out,
    sort_out,
    table_out,
    k_all,
    v_all,
    columns,
    rows_all,
    weights,
    pieces,
    acc,
    kv_own,
    table,
    send_sem,
    recv_sem,
    own_sem,
):
    copies = Copies(send_sem, recv_sem)
    rows, depth = tokens.shape
    groups, width, half = weights.shape[1], q_out.shape[1], rows // 2
    count = pieces.shape[0]
    me, place = lax.axis_index("seq"), lax.axis_index("mod")
    others = [lax.rem(me + step, count) for step in range(1, count)]
    greeted = [{"seq": other} for other in others] + plane_neighbours()
    greet(greeted)
    loads = [
        pltpu.make_async_copy(weight, weights.at[which], own_sem.at[which])
        for which, weight in enumerate((wq_ref, wk_ref, wv_ref))
    ]
    for load in loads:
        load.start()

    marks = modality[...]
    lanes = marks.shape[1]
    diagonal = lax.broadcasted_iota(jnp.int32, (lanes, lanes), 0) == lax.broadcasted_iota(
        jnp.int32, (lanes, lanes), 1
    )
    kind = jnp.concatenate(
        [
            jnp.sum(jnp.where(diagonal, marks[number : number + 1], 0), 1, keepdims=True)
            for number in range(marks.shape[0])
        ],
        0,
    )
    counts = [jnp.sum((kind == group).astype(jnp.int32)) for group in range(groups)]
    firsts = [jnp.int32(0)]
    for group in range(groups):
        firsts.append(firsts[-1] + counts[group])
    lane = lax.broadcasted_iota(jnp.int32, table.shape, 1)
    table[...] = sum(jnp.where(lane > group, counts[group], 0) for group in range(groups))

    lanes = lax.broadcasted_iota(jnp.int32, (rows, 128), 1)
    one_hot = (lanes == kind).astype(jnp.bfloat16)
    down = lax.broadcasted_iota(jnp.int32, (rows, rows), 0)
    across = lax.broadcasted_iota(jnp.int32, (rows, rows), 1)
    first_lane = lax.broadcasted_iota(jnp.int32, (1, 128), 1)
    base = jnp.zeros((1, 128), jnp.float32)
    for group in range(groups):
        base = jnp.where(first_lane == group, firsts[group].astype(jnp.float32), base)
    before = dot((across < down).astype(jnp.bfloat16), one_hot) + base
    rank = jnp.sum(before * one_hot.astype(jnp.float32), 1, keepdims=True).astype(jnp.int32)
    unsort = (rank == across).astype(jnp.bfloat16)
    sort = unsort.T
    sort_out[...] = sort
    rows_all[place] = dot(sort, tokens[...]).astype(jnp.bfloat16)

    line = lax.broadcasted_iota(jnp.int32, (rows, 1), 0)
    sorted_kind = sum((line >= firsts[group]).astype(jnp.int32) for group in range(1, groups))

    def multiply(blocks, new, wanted=(0, 3)):
        def one(which, _):
            low = middle = high = None
            for step in blocks:
                block = plane_device(*step)
                deep = pl.ds(pl.multiple_of(block * depth, depth), depth)
                x = rows_all[block]
                terms = []
                for group, at in enumerate((slice(0, half), slice(0, rows), slice(half, rows))):
                    own = jnp.where(sorted_kind[at] == group, x[at], jnp.zeros_like(x[at]))
                    terms.append(dot(own, weights[which, group, deep, :]))
                low = terms[0] if low is None else low + terms[0]
                middle = terms[1] if middle is None else middle + terms[1]
                high = terms[2] if high is None else high + terms[2]
            for number, part in enumerate((low, high)):
                at = slice(number * half, (number + 1) * half)
                if new:
                    acc[which, at] = part + middle[at]
                else:
                    acc[which, at] += part + middle[at]
            return 0

        lax.fori_loop(*wanted, one, 0)

    def projected(which):
        return dot(unsort, acc[which].astype(jnp.bfloat16)).astype(jnp.bfloat16)

    pl.semaphore_wait(pltpu.get_barrier_semaphore(), len(greeted))
    for step, other in enumerate(others):
        copies.send(("table", step), table, table_out.at[me], {"seq": other})
    own_table = pltpu.make_async_copy(table, table_out.at[me], own_sem.at[3])
    own_table.start()
    begin, near, far, fold, last = plane_gather(
        copies, "rows", rows_all.at[place], rows_all
    )
    begin()
    near()
    fold(0)
    for load in loads:
        load.wait()
    multiply([(0, 0), (1, 0), (-1, 0), (0, 1), (0, -1)], True)
    far()
    last(0)
    fold(-1)
    multiply([(2, 0), (0, 2)], False)
    fold(1)
    fold(2)
    multiply([(1, 1), (1, -1), (-1, 1), (-1, -1)], False)
    last(-1)
    last(1)
    rest = [(1, 2), (-1, 2), (2, 1), (2, -1)]
    multiply(rest, False, (1, 3))
    last(2)

    deep = pieces.shape[2]

    def piece(target):
        return rows_all.at[
            pl.ds(2 * target, 2), pl.ds(pl.multiple_of(place * deep, deep), deep)
        ]

    own_piece = pltpu.make_async_copy(piece(me), pieces.at[me], own_sem.at[4])
    own_piece.start()
    for step, other in enumerate(others):
        copies.send(("piece", step), piece(other), pieces.at[me], {"seq": other})
    multiply([(2, 2)], False, (1, 3))
    kv_own[0] = projected(1)
    kv_own[1] = projected(2)
    own_keys = pltpu.make_async_copy(kv_own.at[0], k_all.at[me], own_sem.at[5])
    own_values = pltpu.make_async_copy(kv_own.at[1], v_all.at[me], own_sem.at[6])
    own_keys.start()
    own_values.start()
    keys = line_gather(copies, "keys", kv_own.at[0], k_all)
    values = line_gather(copies, "values", kv_own.at[1], v_all)
    keys[0]()
    for step in range(count - 1):
        sender = lax.rem(me + count - 1 - step, count)
        copies.receive(("piece", step), pieces.at[sender], {"seq": others[step]})
    own_piece.wait()
    own_columns = pltpu.make_async_copy(pieces, columns.at[place], own_sem.at[7])
    own_columns.start()
    begin, near, far, fold, last = plane_gather(copies, "columns", pieces, columns)
    begin()
    values[0]()
    multiply([*rest, (2, 2)], False, (0, 1))
    near()
    fold(0)
    keys[1]()
    far()
    last(0)
    q_out[...] = projected(0)
    fold(-1)
    values[1]()
    fold(1)
    keys[2]()
    fold(2)
    values[2]()
    for offset in (-1, 1, 2):
        last(offset)
    keys[3]()
    values[3]()
    for step in range(count - 1):
        sender = lax.rem(me + count - 1 - step, count)
        copies.receive(("table", step), table_out.at[sender], {"seq": others[step]})
    copies.finish()
    for own in (own_table, own_keys, own_values, own_columns):
        own.wait()


def front(tokens, modality, weights, count):
    rows, depth = tokens.shape
    groups, tall, width = weights[0].shape
    blocks = SIDE * SIDE
    kind = tokens.dtype
    piece = (count, 2, rows // blocks, depth)
    half = jax.ShapeDtypeStruct((count, rows, width), kind)
    return pl.pallas_call(
        front_kernel,
        out_shape=(
            jax.ShapeDtypeStruct((rows, width), kind),
            jax.ShapeDtypeStruct((rows, rows), kind),
            jax.ShapeDtypeStruct((count, 8, 128), jnp.int32),
            half,
            half,
            jax.ShapeDtypeStruct((blocks, *piece), kind),
        ),
        in_specs=[WHOLE, WHOLE, ANY, ANY, ANY],
        out_specs=(WHOLE, WHOLE, WHOLE, ANY, ANY, ANY),
        scratch_shapes=[
            pltpu.VMEM((blocks, rows, depth), kind),
            pltpu.VMEM((3, groups, tall, width), kind),
            pltpu.VMEM(piece, kind),
            pltpu.VMEM((3, rows, width), jnp.float32),
            pltpu.VMEM((2, rows, width), kind),
            pltpu.VMEM((8, 128), jnp.int32),
            *semaphores(116),
            pltpu.SemaphoreType.DMA((8,)),
        ],
        compiler_params=remote_params(0),
    )(tokens, modality, *weights)


def attention_kernel(
    lengths,
    q_ref,
    k_ref,
    v_ref,
    do_ref,
    out_ref,
    dq_ref,
    dkv_ref,
    scores,
    dq_sum,
    made,
    theirs,
    ours,
    halves,
    fulls,
    sums,
    send_sem,
    recv_sem,
    pair_send,
    pair_recv,
):
    copies = Copies(send_sem, recv_sem)
    greeted = line_neighbours()
    greet(greeted)
    rows, width = q_ref.shape
    heads = width // HEAD_DIM
    scale = 1.0 / math.sqrt(HEAD_DIM)
    me = lax.axis_index("seq")
    first = jnp.maximum(me - (MAX_BACK - 1), 0)
    ends = [lengths[0]]
    for number in range(1, lengths.shape[0]):
        ends.append(ends[-1] + lengths[number])

    def document(positions):
        return sum((positions >= end).astype(jnp.int32) for end in ends)

    own = lax.broadcasted_iota(jnp.int32, (rows, 1), 0) + me * rows
    own_document = document(own)
    cols = [slice(h * HEAD_DIM, (h + 1) * HEAD_DIM) for h in range(heads)]
    vcols = [slice(width + h * HEAD_DIM, width + (h + 1) * HEAD_DIM) for h in range(heads)]

    def score_step(block, row_max):
        key_pos = lax.broadcasted_iota(jnp.int32, (1, rows), 1) + block * rows
        visible = (key_pos <= own) & (document(key_pos) == own_document)
        new = []
        for h in range(heads):
            part = dot(q_ref[:, cols[h]], k_ref[block, :, cols[h]], 1, 1) * scale
            part = jnp.where(visible, part, -jnp.inf)
            scores[h, block - first] = part
            new.append(jnp.maximum(row_max[h], jnp.max(part, 1, keepdims=True)))
        return tuple(new)

    start = tuple(jnp.full((rows, 1), -jnp.inf, jnp.float32) for _ in range(heads))
    row_max = lax.fori_loop(first, me + 1, score_step, start)

    def value_step(block, carry):
        new = []
        for h in range(heads):
            total, summed = carry[h]
            weights = jnp.exp(scores[h, block - first] - row_max[h])
            scores[h, block - first] = weights
            total = total + jnp.sum(weights, 1, keepdims=True)
            summed = summed + dot(weights.astype(jnp.bfloat16), v_ref[block, :, cols[h]])
            new.append((total, summed))
        return tuple(new)

    start = tuple(
        (jnp.zeros((rows, 1), jnp.float32), jnp.zeros((rows, HEAD_DIM), jnp.float32))
        for _ in range(heads)
    )
    totals = lax.fori_loop(first, me + 1, value_step, start)
    inverse, row_dot = [], []
    for h in range(heads):
        total, summed = totals[h]
        attended = (summed / total).astype(jnp.bfloat16)
        out_ref[:, cols[h]] = attended
        inverse.append(1.0 / total)
        row_dot.append(
            jnp.sum(
                do_ref[:, cols[h]].astype(jnp.float32) * attended.astype(jnp.float32),
                1,
                keepdims=True,
            )
        )
    dq_sum[...] = jnp.zeros_like(dq_sum)
    pl.semaphore_wait(pltpu.get_barrier_semaphore(), len(greeted))

    def grads(block, result):
        seen = (block >= first) & (block <= me)

        @pl.when(seen)
        def _():
            for h in range(heads):
                spread = dot(do_ref[:, cols[h]], v_ref[block, :, cols[h]], 1, 1)
                chances = scores[h, block - first] * inverse[h]
                dscore = (chances * (spread - row_dot[h]) * scale).astype(jnp.bfloat16)
                dq_sum[:, cols[h]] += dot(dscore, k_ref[block, :, cols[h]])
                result[:, cols[h]] = dot(dscore, q_ref[:, cols[h]], 0, 0).astype(jnp.bfloat16)
                result[:, vcols[h]] = dot(
                    chances.astype(jnp.bfloat16), do_ref[:, cols[h]], 0, 0
                ).astype(jnp.bfloat16)

        @pl.when(jnp.logical_not(seen))
        def _():
            result[...] = jnp.zeros(result.shape, jnp.bfloat16)

    order = (2, -1, 0)

    def pair(number):
        return pltpu.make_async_remote_copy(
            src_ref=made.at[0, number],
            dst_ref=theirs.at[number],
            send_sem=pair_send.at[number],
            recv_sem=pair_recv.at[number],
            device_id={"seq": line_device(0, True)},
            device_id_type=pl.DeviceIdType.MESH,
        )

    def compute(number):
        def one(turn, _):
            chip = lax.rem(me // 2 + SIDE + order[number], SIDE)
            block = chip * 2 + lax.rem(lax.rem(me, 2) + 1 + turn, 2)
            grads(block, made.at[turn, number])

            @pl.when(turn == 0)
            def _():
                pair(number).start()

            return 0

        lax.fori_loop(0, 2, one, 0)

    def join(number):
        pair(number).wait_recv()
        ours[number] = add(made[1, number], theirs[number])

    ring = RingSum(
        copies,
        "ring",
        lambda offset: ours.at[order.index(offset)],
        lambda way: {"seq": line_device(way)},
        halves,
        fulls,
        sums,
        (1,),
    )
    compute(0)
    join(0)
    ring.far()
    compute(1)
    join(1)
    ring.early(-1)
    compute(2)
    for h in range(heads):
        dq_ref[:, cols[h]] = dq_sum[:, cols[h]].astype(jnp.bfloat16)
    ring.late()
    join(2)
    dkv_ref[...] = ring.result()
    copies.finish()
    for number in range(3):
        pair(number).wait_send()


def attention(lengths, q, k, v, do):
    rows, width = q.shape
    kind = q.dtype
    shape = jax.ShapeDtypeStruct((rows, width), kind)

    def buffer(count, tall):
        return pltpu.VMEM((count, tall, 2 * width), kind)

    return pl.pallas_call(
        attention_kernel,
        out_shape=(
            shape,
            shape,
            jax.ShapeDtypeStruct((rows, 2 * width), kind),
        ),
        in_specs=[SMEM] + [WHOLE] * 4,
        out_specs=(WHOLE,) * 3,
        scratch_shapes=[
            pltpu.VMEM((width // HEAD_DIM, MAX_BACK, rows, rows), jnp.float32),
            pltpu.VMEM((rows, width), jnp.float32),
            pltpu.VMEM((2, 3, rows, 2 * width), kind),
            buffer(3, rows),
            buffer(3, rows),
            buffer(2, rows // 2),
            buffer(2, rows),
            buffer(2, rows // 2),
            *semaphores(8),
            *semaphores(3),
        ],
        compiler_params=remote_params(1),
    )(lengths, q, k, v, do)


def tail_kernel(
    table,
    act_query,
    act_key_value,
    sort,
    wq_ref,
    wk_ref,
    wv_ref,
    act_all,
    out,
    weights,
    act_own,
    middle,
    outer,
    partial,
    halves,
    fulls,
    sums,
    results,
    send_sem,
    recv_sem,
    own_sem,
    load_sem,
):
    copies = Copies(send_sem, recv_sem)
    greeted = plane_neighbours() + line_neighbours()
    greet(greeted)
    _, groups, _, depth = weights.shape
    rows = sort.shape[0]
    me = lax.axis_index("seq")
    half = rows // 2
    order = [(2, 2), (1, 2), (-1, 2), (2, 1), (2, -1), (0, 2), (2, 0)]
    order += [(1, 1), (1, -1), (-1, 1), (-1, -1)]
    order += [(0, 1), (0, -1), (1, 0), (-1, 0), (0, 0)]
    loads = {}
    for number, step in enumerate(order):
        at = pl.ds(pl.multiple_of(plane_device(*step) * depth, depth), depth)
        loads[step] = [
            pltpu.make_async_copy(
                weight.at[:, at], weights.at[which, :, at], load_sem.at[3 * number + which]
            )
            for which, weight in enumerate((wq_ref, wk_ref, wv_ref))
        ]
        for load in loads[step]:
            load.start()

    width = act_query.shape[1]
    acts = (act_query[...], act_key_value[:, :width], act_key_value[:, width:])
    for which, act in enumerate(acts):
        act_own[which] = dot(sort[...], act).astype(jnp.bfloat16)
    own_act = [
        pltpu.make_async_copy(act_own.at[which], act_all.at[which, me], own_sem.at[which])
        for which in range(3)
    ]
    for own in own_act:
        own.start()
    pl.semaphore_wait(pltpu.get_barrier_semaphore(), len(greeted))
    lines = [
        line_gather(copies, ("act", which), act_own.at[which], act_all.at[which])
        for which in range(3)
    ]
    for line in lines:
        line[0]()

    place = lax.broadcasted_iota(jnp.int32, (rows, 1), 0)
    sorted_kind = sum(
        (place >= table[me, 0, group]).astype(jnp.int32) for group in range(1, groups)
    )
    for which in range(3):
        act = act_own[which]
        span = slice(which * width, (which + 1) * width)
        middle[:, span] = jnp.where(sorted_kind == 1, act, jnp.zeros_like(act))
        for number in range(2):
            at = slice(number * half, (number + 1) * half)
            outer[number, :, span] = jnp.where(
                sorted_kind[at] == 2 * number, act[at], jnp.zeros_like(act[at])
            )

    def multiply(step):
        for load in loads[step]:
            load.wait()
        block = plane_device(*step)
        deep = pl.ds(pl.multiple_of(block * depth, depth), depth)

        def product(acts, group):
            total = None
            for which in range(3):
                act = acts[:, which * width : (which + 1) * width]
                term = dot(act, weights[which, group, deep, :], 1, 1)
                total = term if total is None else total + term
            return total

        both = product(middle, 1)
        for number in range(2):
            at = slice(number * half, (number + 1) * half)
            part = product(outer.at[number], 2 * number) + both[at]
            partial[block, at] = part.astype(jnp.bfloat16)

    def device(turn, da, db):
        return plane_device(da, db) if turn == 0 else plane_device(db, da)

    def second(turn, place):
        offset, number = OFFSETS[place], turn * len(OFFSETS) + place
        return RingSum(
            copies,
            ("b", number),
            lambda db: partial.at[device(turn, offset, db), pl.ds(turn * half, half)],
            lambda way: {"mod": device(turn, 0, way)},
            halves.at[number],
            fulls.at[number],
            sums.at[number],
        )

    def first(turn):
        number = 2 * len(OFFSETS) + turn
        return RingSum(
            copies,
            ("a", turn),
            lambda da: results.at[turn, OFFSETS.index(da)],
            lambda way: {"mod": device(turn, way, 0)},
            halves.at[number],
            fulls.at[number],
            sums.at[number],
        )

    rings = {
        (turn, OFFSETS[place]): second(turn, place) for place in range(4) for turn in range(2)
    }
    tops = [first(turn) for turn in range(2)]
    for number, step in enumerate(order):
        multiply(step)
        for turn in range(2):
            da, db = step if turn == 0 else (step[1], step[0])
            if db == 2:
                rings[turn, da].far()
            elif db != 0:
                rings[turn, da].early(db)
        if number == 6:
            lines[0][1]()
        if number == 10:
            for turn in range(2):
                rings[turn, 2].late()
            lines[1][1]()
        if number == 12:
            for turn in range(2):
                rings[turn, -1].late()
        if number == 14:
            for turn in range(2):
                rings[turn, 1].late()
    for turn in range(2):
        rings[turn, 0].late()
    lines[2][1]()

    for offset in OFFSETS:
        for turn in range(2):
            results[turn, OFFSETS.index(offset)] = rings[turn, offset].result()
            if offset == 2:
                tops[turn].far()
            elif offset != 0:
                tops[turn].early(offset)
        if offset == 2:
            lines[0][2]()
    for top in tops:
        top.late()
    lines[1][2]()
    total = None
    for turn, top in enumerate(tops):
        term = dot(sort[turn * half : (turn + 1) * half], top.result(), 0, 0)
        total = term if total is None else total + term
    out[...] = total.astype(out.dtype)
    lines[2][2]()
    for line in lines:
        line[3]()
    copies.finish()
    for own in own_act:
        own.wait()


def tail(table, act_query, act_key_value, sort, weights, count):
    rows, width = act_query.shape
    groups, tall, _ = weights[0].shape
    kind = act_query.dtype
    half, blocks = rows // 2, SIDE * SIDE
    depth = tall // blocks

    def buffer(*shape):
        return pltpu.VMEM((*shape, depth), kind)

    return pl.pallas_call(
        tail_kernel,
        out_shape=(
            jax.ShapeDtypeStruct((3, count, rows, width), kind),
            jax.ShapeDtypeStruct((rows, depth), kind),
        ),
        in_specs=[SMEM, WHOLE, WHOLE, WHOLE, ANY, ANY, ANY],
        out_specs=(ANY, WHOLE),
        scratch_shapes=[
            pltpu.VMEM((3, groups, tall, width), kind),
            pltpu.VMEM((3, rows, width), kind),
            pltpu.VMEM((rows, 3 * width), kind),
            pltpu.VMEM((2, half, 3 * width), kind),
            buffer(blocks, rows),
            buffer(10, 2, half // 2),
            buffer(10, 2, half),
            buffer(10, 2, half // 2),
            buffer(2, 4, half),
            *semaphores(96),
            pltpu.SemaphoreType.DMA((3,)),
            pltpu.SemaphoreType.DMA((3 * blocks,)),
        ],
        compiler_params=remote_params(3),
    )(table, act_query, act_key_value, sort, *weights)


def per_device(tokens, modality, doc_lengths, w_query, w_key, w_value, d_out):
    groups = w_query.shape[0]
    seq_count = lax.axis_size("seq")
    weights = (w_query, w_key, w_value)
    queries, sort_matrix, table, keys, values, token_columns = front(
        tokens, modality.reshape(-1, 128), weights, seq_count
    )
    attn_out, act_query, act_key_value = attention(
        doc_lengths, queries, keys, values, d_out
    )
    act_all, grad_tokens = tail(
        table, act_query, act_key_value, sort_matrix, weights, seq_count
    )
    grads = weight_grads(table, token_columns, act_all, groups)
    return (attn_out, grad_tokens, *grads)


def solution(mesh):
    placed = (
        P("seq", "mod"),
        P("seq", None),
        P(),
        P(None, None, "mod"),
        P(None, None, "mod"),
        P(None, None, "mod"),
        P("seq", "mod"),
    )
    return jax.shard_map(
        per_device,
        mesh=mesh,
        in_specs=placed,
        out_specs=(
            P("seq", "mod"),
            P("seq", "mod"),
            P(None, "seq", "mod"),
            P(None, "seq", "mod"),
            P(None, "seq", "mod"),
        ),
        check_vma=False,
    )
```
